128 devices in a mesh: slab: 32 (over x, z, core), blk: 4 (over y).
Axes of the slice: x: 4, y: 4, z: 4, core: 2. Of those that a mesh axis runs over, the one named last changes fastest.
Arguments:
- thermal_level: float32 [512, 64, 256], P('slab', 'blk'), may hold values from -6 to 6
- deformation_vector: float32 [3, 512, 64, 256], P(None, 'slab', 'blk'), may hold values from -6 to 6
- thermal_elastic_modulus: float32 [512, 64, 256], P('slab', 'blk'), may hold values from 0.25 to 1
- yield_strain: float32 [512, 64, 256], P('slab', 'blk'), may hold values from 0.05 to 2
- refinement_flag: int32 [32, 4, 16], P('slab', 'blk'), may hold values 0 or 1
- destination_holder: int32 [32, 4, 16], P('slab', 'blk'), may hold values from 0 to 31, as said below
- destination_position: int32 [32, 4, 16], P('slab', 'blk'), may hold values from 0 to 15, as said below
Outputs:
- relaxed_thermal_entries: float32 [32, 4, 16, 4096], P('slab', 'blk')
- relaxed_deformation_entries: float32 [32, 4, 16, 3, 4096], P('slab', 'blk')
- redistributed_yield_strain: float32 [32, 4, 16, 4096], P('slab', 'blk')
The draws below stay inside these ranges and needn't reach their ends.
Inputs may be any that keep to these rules, and one draw needn't show every extreme that they name: For each blk index b there is an ordering r of the slab indices and a step t_p for each slot p such that destination_holder[s,b,p] = r[(position of s in r + t_p) mod the number of slab indices]; no step is taken by more than 2 slots and one step by exactly 2, so one device hands at most 2 patches to one device and reaches 2. For each blk index, (destination_holder, destination_position) maps the patches one to one onto slab indices times slots: every device receives exactly 16 patches.
All inputs are finite; a program needn't handle non-finite values. No bound on the sum of `refinement_flag` on one device may be relied on, other than what follows from the above.
Results may differ from the reference program's by a relative error of at most 0.0003.
Values may be sent and summed in bfloat16 or wider, within the bound.
A program may use at most 192 MiB of HBM per device.

```python
import math
import jax
import jax.numpy as jnp
from jax import lax

EDGE = 16
P_DEV = 16
SWEEPS = 4
SMOOTH = 2
CAP = 2
MESH_SPAN_FIRST = 512
MESH_SPAN_SECOND = 64
MESH_SPAN_THIRD = 256
N_SLAB = 32
N_BLK = 4


def repartition(key):
    base_key = jax.random.fold_in(key, 7)

    def column(column_key):
        keys = jax.random.split(column_key, 5)
        cycle_order = jax.random.permutation(keys[0], N_SLAB).astype(jnp.int32)
        cycle_place = jnp.argsort(cycle_order).astype(jnp.int32)
        common_step = jax.random.randint(keys[1], (), 0, N_SLAB).astype(jnp.int32)
        other_steps = (jax.random.permutation(keys[2], (N_SLAB - 1) * CAP) // CAP).astype(jnp.int32)
        other_steps = other_steps + (other_steps >= common_step).astype(jnp.int32)
        lane_steps = jnp.concatenate([jnp.full((CAP,), common_step, jnp.int32), other_steps[:P_DEV - CAP]])
        lane_steps = jax.random.permutation(keys[3], lane_steps)
        owners = cycle_order[(cycle_place[:, None] + lane_steps[None, :]) % N_SLAB]
        slot_keys = jax.random.split(keys[4], N_SLAB)
        slot_orders = jax.vmap(lambda one_key: jax.random.permutation(one_key, P_DEV).astype(jnp.int32))(slot_keys)
        slots = slot_orders[owners, jnp.arange(P_DEV, dtype=jnp.int32)[None, :]]
        return (owners, slots)
    owners, slots = jax.vmap(column)(jax.random.split(base_key, N_BLK))
    return (owners.transpose(1, 0, 2).astype(jnp.int32), slots.transpose(1, 0, 2).astype(jnp.int32))


def draw_destination_holder(key, part):
    return repartition(key)[0]


def draw_destination_position(key, part):
    return repartition(key)[1]


def set_ends(values, rng, least, largest):
    extent = values.shape
    index_at = [jax.random.randint(jax.random.fold_in(rng, axis), (), 0, extent[axis]) for axis in range(len(extent))]
    values = values.at[tuple(index_at)].set(least)
    longest = extent.index(max(extent))
    index_at[longest] = (index_at[longest] + 1) % extent[longest]
    return values.at[tuple(index_at)].set(largest)


def steps_of(stream_key, shape, shards, smallest, high):
    def one(dim, blocks):
        heights = jax.random.uniform(jax.random.fold_in(jax.random.fold_in(stream_key, 6), dim), (blocks,), jnp.float32, smallest / len(shards), high / len(shards))
        return jnp.repeat(jnp.exp(heights), shape[dim] // blocks).reshape((-1,) + (1,) * (len(shape) - dim - 1))

    gain = one(*shards[0])
    for cut in shards[1:]:
        gain = gain * one(*cut)
    return gain


def noise(stream_key, extent, scale, most, cuts=(), kind=jnp.bfloat16):
    values = jax.random.normal(stream_key, extent, jnp.float32) * scale
    if len(cuts) > 0:
        values = steps_of(stream_key, extent, cuts, -0.22, 0.18) * values
    return jnp.clip(values, min=-most, max=most).astype(kind)


def setup_inputs(seed: int = 0) -> dict:
    streams_of = jax.random.split(jax.random.key(seed), 8)
    return {
        "thermal_level": noise(streams_of[0], (MESH_SPAN_FIRST, MESH_SPAN_SECOND, MESH_SPAN_THIRD), 1.0, 6.0, ((0, 32), (1, 4)), jnp.float32),
        "deformation_vector": noise(streams_of[1], (3, MESH_SPAN_FIRST, MESH_SPAN_SECOND, MESH_SPAN_THIRD), 1.0, 6.0, ((1, 32), (2, 4)), jnp.float32),
        "thermal_elastic_modulus": jnp.clip(jnp.exp(math.log(1.0) - 1.3862944 * jax.random.uniform(streams_of[2], (MESH_SPAN_FIRST, MESH_SPAN_SECOND, MESH_SPAN_THIRD), jnp.float32) ** steps_of(streams_of[2], (MESH_SPAN_FIRST, MESH_SPAN_SECOND, MESH_SPAN_THIRD), ((0, 32), (1, 4)), -0.2, 0.2)), 0.25, 1.0),
        "yield_strain": jnp.clip(jnp.exp(math.log(2.0) - 3.6888794 * jax.random.uniform(streams_of[3], (MESH_SPAN_FIRST, MESH_SPAN_SECOND, MESH_SPAN_THIRD), jnp.float32) ** steps_of(streams_of[3], (MESH_SPAN_FIRST, MESH_SPAN_SECOND, MESH_SPAN_THIRD), ((0, 32), (1, 4)), -0.2, 0.2)), 0.05, 2.0),
        "refinement_flag": set_ends((jax.random.randint(streams_of[4], (N_SLAB, N_BLK, P_DEV), 0, 4) < 1).astype(jnp.int32), jax.random.fold_in(streams_of[4], 1), 0, 1),
        "destination_holder": draw_destination_holder(jax.random.fold_in(streams_of[7], 71), 0),
        "destination_position": draw_destination_position(jax.random.fold_in(streams_of[7], 71), 0),
    }


time_step = 0.12
coupling = 1.0


def face_list():
    return [(1, 0, 0), (-1, 0, 0), (0, 1, 0), (0, -1, 0), (0, 0, 1), (0, 0, -1)]


def tile_directions():
    result = []
    for shift_x in (-1, 0, 1):
        for shift_y in (-1, 0, 1):
            for shift_z in (-1, 0, 1):
                reach = abs(shift_x) + abs(shift_y) + abs(shift_z)
                if reach > 0:
                    result.append((shift_x, shift_y, shift_z, [0.0, 0.10, 0.04, 0.02][reach]))
    return result


def window(padded, shift_x, shift_y, shift_z):
    size_x, size_y, size_z = padded.shape[-3:]
    return padded[..., 1 + shift_x:size_x - 1 + shift_x, 1 + shift_y:size_y - 1 + shift_y, 1 + shift_z:size_z - 1 + shift_z]


def sweep_core(heat_pad, moved_pad, conduct_pad):
    centre_heat = window(heat_pad, 0, 0, 0)
    centre_moved = window(moved_pad, 0, 0, 0)
    centre_conduct = window(conduct_pad, 0, 0, 0)
    flux = jnp.zeros_like(centre_heat)
    laplace = jnp.zeros_like(centre_moved)
    for shift_x, shift_y, shift_z in face_list():
        flux = flux + 0.5 * (centre_conduct + window(conduct_pad, shift_x, shift_y, shift_z)) * (window(heat_pad, shift_x, shift_y, shift_z) - centre_heat)
        laplace = laplace + window(moved_pad, shift_x, shift_y, shift_z) - centre_moved
    gradient = jnp.stack([window(heat_pad, 1, 0, 0) - window(heat_pad, -1, 0, 0),
                          window(heat_pad, 0, 1, 0) - window(heat_pad, 0, -1, 0),
                          window(heat_pad, 0, 0, 1) - window(heat_pad, 0, 0, -1)], 0) * 0.5
    return centre_heat + time_step * flux, centre_moved + time_step * laplace - time_step * coupling * gradient


def shift_flat(values, offset):
    length = values.shape[-1]
    if offset == 0:
        return values
    padding = jnp.zeros(values.shape[:-1] + (abs(offset),), values.dtype)
    if offset > 0:
        return jnp.concatenate([values[..., offset:], padding], -1)
    return jnp.concatenate([padding, values[..., :length + offset]], -1)


def inside_mask(shift_x, shift_y, shift_z):
    position = jnp.arange(EDGE ** 3, dtype=jnp.int32)
    coord_x = position // (EDGE * EDGE) + shift_x
    coord_y = (position // EDGE) % EDGE + shift_y
    coord_z = position % EDGE + shift_z
    inside = (coord_x >= 0) & (coord_x < EDGE) & (coord_y >= 0) & (coord_y < EDGE) & (coord_z >= 0) & (coord_z < EDGE)
    return inside.astype(jnp.float32)


def build_tile(heat_rows, conduct_rows, plastic_rows, refined_rows):
    squared = heat_rows * heat_rows
    factor = 1.0 + 3.0 * refined_rows.astype(jnp.float32)
    stiffness = conduct_rows * (1.0 + 0.5 * squared / (1.0 + squared)) / (1.0 + plastic_rows) * factor[:, None]
    entries = []
    for shift_x, shift_y, shift_z, weight in tile_directions():
        offset = shift_x * EDGE * EDGE + shift_y * EDGE + shift_z
        entries.append(weight * 0.5 * (stiffness + shift_flat(stiffness, offset)) * inside_mask(shift_x, shift_y, shift_z))
    return jnp.stack(entries, 1).astype(jnp.bfloat16)


def patch_solve(stencil_tile, fields):
    coeffs = stencil_tile.astype(jnp.float32)
    diagonal = 1.0 + jnp.sum(coeffs, axis=1)
    current = fields
    for smooth_step in range(SMOOTH):
        total = fields
        for number, (shift_x, shift_y, shift_z, weight) in enumerate(tile_directions()):
            offset = shift_x * EDGE * EDGE + shift_y * EDGE + shift_z
            total = total + coeffs[:, number, None, :] * shift_flat(current, offset)
        current = total / diagonal[:, None, :]
    return current


def pad_cells(values):
    return jnp.pad(values, [(0, 0)] * (values.ndim - 3) + [(1, 1)] * 3)


def grid_rows(grid_field):
    blocks = grid_field.reshape(N_SLAB, EDGE, N_BLK, EDGE, P_DEV, EDGE)
    return blocks.transpose(0, 2, 4, 1, 3, 5).reshape(N_SLAB, N_BLK, P_DEV, EDGE ** 3)


def vector_rows(grid_field):
    blocks = grid_field.reshape(3, N_SLAB, EDGE, N_BLK, EDGE, P_DEV, EDGE)
    return blocks.transpose(1, 3, 5, 0, 2, 4, 6).reshape(N_SLAB, N_BLK, P_DEV, 3, EDGE ** 3)


def reference(thermal_level, deformation_vector, thermal_elastic_modulus, yield_strain, refinement_flag, destination_holder, destination_position):
    conduct_pad = pad_cells(thermal_elastic_modulus)
    thermal_state, deformed_state = thermal_level, deformation_vector
    for sweep_index in range(SWEEPS):
        thermal_state, deformed_state = sweep_core(pad_cells(thermal_state), pad_cells(deformed_state), conduct_pad)
    heat_rows = grid_rows(thermal_state)
    moved_rows = vector_rows(deformed_state)
    conduct_rows = grid_rows(thermal_elastic_modulus)
    plastic_rows = grid_rows(yield_strain)
    block_tally = N_BLK * P_DEV

    def per_slab(inputs):
        heat_part, moved_part, conduct_part, plastic_part, refined_part = inputs
        stencil_tile = build_tile(heat_part.reshape(block_tally, -1), conduct_part.reshape(block_tally, -1),
                                  plastic_part.reshape(block_tally, -1), refined_part.reshape(block_tally))
        fields = jnp.concatenate([heat_part.reshape(block_tally, 1, -1), moved_part.reshape(block_tally, 3, -1)], 1)
        return patch_solve(stencil_tile, fields).reshape(N_BLK, P_DEV, 4, -1)

    solved = lax.map(per_slab, (heat_rows, moved_rows, conduct_rows, plastic_rows, refinement_flag))
    column = jnp.broadcast_to(jnp.arange(N_BLK, dtype=jnp.int32)[None, :, None], destination_holder.shape)
    placed = jnp.zeros_like(solved).at[destination_holder, column, destination_position].set(solved)
    moved_plastic = jnp.zeros_like(plastic_rows).at[destination_holder, column, destination_position].set(plastic_rows)
    return placed[:, :, :, 0, :], placed[:, :, :, 1:, :], moved_plastic
```

```python
import jax
import jax.numpy as jnp
from jax import lax
from jax.experimental import pallas as pl
from jax.experimental.pallas import tpu as pltpu
from jax.sharding import PartitionSpec as P

EDGE = 16
DEPTH = 256
SWEEPS = 4
N_SLAB = 32
N_BLK = 4
P_DEV = 16
ROWS = N_SLAB * P_DEV
MESH = pl.DeviceIdType.MESH
F32 = jnp.float32
I32 = jnp.int32
BF16 = jnp.bfloat16

PLASTIC_LOW = 0.2235
PLASTIC_STEPS = 65535.0 / (1.4145 - PLASTIC_LOW)

OFFSETS = [
    (dx, dy, dz)
    for dx in (-1, 0, 1)
    for dy in (-1, 0, 1)
    for dz in (-1, 0, 1)
    if (dx, dy, dz) != (0, 0, 0)
]
WEIGHTS = [0.0, 0.1, 0.04, 0.02]


def plane_number(dy, dz):
    return (dy + 1) * 3 + dz + 1


def lane_of(shape):
    return lax.broadcasted_iota(I32, shape, 1)


def row_of(shape):
    return lax.broadcasted_iota(I32, shape, 0)


def shifted_planes(plane, row, inner):
    below = jnp.where(inner == 0, 0.0, pltpu.roll(plane, 1, 1))
    above = jnp.where(inner == EDGE - 1, 0.0, pltpu.roll(plane, DEPTH - 1, 1))
    three = (below, plane, above)
    low = [jnp.where(row == 0, 0.0, pltpu.roll(part, 1, 0)) for part in three]
    high = [jnp.where(row == EDGE - 1, 0.0, pltpu.roll(part, EDGE - 1, 0)) for part in three]
    return low + list(three) + high


def swap_rows_and_groups(tile, row, group):
    for bit in (4, 2, 1):
        row_bit = (row & bit) != 0
        group_bit = (group & bit) != 0
        down = pltpu.roll(pltpu.roll(tile, bit, 0), 128 - 16 * bit, 1)
        up = down if bit == 4 else pltpu.roll(pltpu.roll(tile, 8 - bit, 0), 16 * bit, 1)
        tile = jnp.where(row_bit == group_bit, tile, jnp.where(row_bit, down, up))
    return tile


def byte_of(words, number):
    part = words if number == 0 else lax.shift_right_logical(words, 8 * number)
    return (part & 255).astype(F32).astype(BF16)


def joined(low, high):
    return (low + 256.0 * high).astype(I32)


def move_kernel(
    thermal, deform, modulus, plastic, flag, holder, position,
    out_words, out_plastic, out_exponents,
    state, halo_y, stage_y, cond, cond_y, cond_stage,
    face_x, face_ym, face_yp, face_zm, face_zp, centre,
    stiff, weights, tile, inverse, values,
    send_one, recv_one, send_two, plastic_one, plastic_got, plastic_two,
    one_hot, table, plastic_table,
    load_sem, x_send, x_recv, y_send, y_recv,
    one_send, one_recv, two_send, two_recv, pl_one_send, pl_one_recv, pl_two_send, pl_two_recv, own_sem,
):
    s = lax.axis_index("slab")
    b = lax.axis_index("blk")
    up, down = lax.rem(s + 1, N_SLAB), lax.rem(s + N_SLAB - 1, N_SLAB)
    right, left = lax.rem(b + 1, N_BLK), lax.rem(b + N_BLK - 1, N_BLK)
    has_up, has_down = s < N_SLAB - 1, s > 0
    has_right, has_left = b < N_BLK - 1, b > 0

    loads = [
        pltpu.make_async_copy(thermal, state.at[0, 0, pl.ds(1, EDGE)], load_sem.at[0]),
        pltpu.make_async_copy(deform, state.at[0, pl.ds(1, 3), pl.ds(1, EDGE)], load_sem.at[1]),
        pltpu.make_async_copy(modulus, cond.at[pl.ds(1, EDGE)], load_sem.at[2]),
    ]
    for load in loads:
        load.start()

    barrier = pltpu.get_barrier_semaphore()

    def greet(step, carry):
        peer = lax.rem(s + step, N_SLAB)
        pl.semaphore_signal(barrier, inc=1, device_id=(peer, b), device_id_type=MESH)
        return carry

    lax.fori_loop(1, N_SLAB, greet, 0)

    @pl.when(has_right)
    def _():
        pl.semaphore_signal(barrier, inc=1, device_id=(s, right), device_id_type=MESH)

    @pl.when(has_left)
    def _():
        pl.semaphore_signal(barrier, inc=1, device_id=(s, left), device_id_type=MESH)

    zero_plane = jnp.zeros((EDGE, DEPTH), F32)

    for has, place, side in ((has_down, 0, 0), (has_up, EDGE + 1, 1)):

        @pl.when(jnp.logical_not(has))
        def _():
            cond[place] = zero_plane
            for t in range(SWEEPS):
                for f in range(4):
                    state[t, f, place] = zero_plane

    for has, side in ((has_left, 0), (has_right, 1)):

        @pl.when(jnp.logical_not(has))
        def _():
            cond_y[side] = zero_plane
            for t in range(SWEEPS):
                for f in range(4):
                    halo_y[t, side, f] = zero_plane

    neighbours = 31 + has_right.astype(I32) + has_left.astype(I32)
    pl.semaphore_wait(barrier, neighbours)

    def x_copies(kind):
        out = []
        for direction, peer in ((0, down), (1, up)):
            mine = 0 if direction == 0 else EDGE - 1
            there = EDGE + 1 if direction == 0 else 0
            if kind == 0:
                source, target = thermal.at[mine], state.at[0, 0, there]
            elif kind == 4:
                source, target = deform.at[:, mine], state.at[0, pl.ds(1, 3), there]
            elif kind == 5:
                source, target = modulus.at[mine], cond.at[there]
            else:
                source, target = state.at[kind, :, mine + 1], state.at[kind, :, there]
            out.append(
                pltpu.make_async_remote_copy(
                    source, target, x_send.at[kind, direction], x_recv.at[kind, direction],
                    device_id=(peer, b), device_id_type=MESH,
                )
            )
        return out

    def y_copies(kind):
        out = []
        for direction, peer in ((0, left), (1, right)):
            if kind == 4:
                source, target = cond_stage.at[direction], cond_y.at[1 - direction]
            else:
                source, target = stage_y.at[kind, direction], halo_y.at[kind, 1 - direction]
            out.append(
                pltpu.make_async_remote_copy(
                    source, target, y_send.at[kind, direction], y_recv.at[kind, direction],
                    device_id=(s, peer), device_id_type=MESH,
                )
            )
        return out

    def start(copies, to_low, to_high):
        @pl.when(to_low)
        def _():
            copies[0].start()

        @pl.when(to_high)
        def _():
            copies[1].start()

    def wait_recv(copies, from_high, from_low):
        @pl.when(from_high)
        def _():
            copies[0].wait_recv()

        @pl.when(from_low)
        def _():
            copies[1].wait_recv()

    def wait_send(copies, to_low, to_high):
        @pl.when(to_low)
        def _():
            copies[0].wait_send()

        @pl.when(to_high)
        def _():
            copies[1].wait_send()

    for kind in (5, 0, 4):
        start(x_copies(kind), has_down, has_up)
    for load in loads:
        load.wait()

    def stage_first(x, carry):
        for side, y in ((0, 0), (1, EDGE - 1)):
            cond_stage[side, pl.ds(x, 1), :] = cond[x + 1, y : y + 1, :]
            for f in range(4):
                stage_y[0, side, f, pl.ds(x, 1), :] = state[0, f, x + 1, y : y + 1, :]
        return carry

    lax.fori_loop(0, EDGE, stage_first, 0)
    start(y_copies(4), has_left, has_right)
    start(y_copies(0), has_left, has_right)

    row8 = row_of((8, 128))
    group8 = lane_of((8, 128)) // EDGE
    row = row_of((EDGE, DEPTH))
    lane = lane_of((EDGE, DEPTH))
    inner = lane & (EDGE - 1)

    slot_lane = lane_of((1, 128))
    slot_row = jnp.zeros((1, 128), I32)
    for p in range(P_DEV):
        code = holder[0, 0, p] * P_DEV + position[0, 0, p]
        slot_row = jnp.where(slot_lane == lax.rem(s, 8) * P_DEV + p, code, slot_row)

    def plastic_out(step, carry):
        x = lax.rem(step + s // 2, EDGE)
        root = plastic[x]
        root = root * lax.rsqrt(root)
        codes = jnp.clip((root - PLASTIC_LOW) * PLASTIC_STEPS + 0.5, 0.0, 65535.0).astype(I32)
        words = (codes[:, 0:128] << 16) | codes[:, 128:256]
        for half in range(2):
            m = 2 * x + half
            plastic_one[m, 0:8, :] = swap_rows_and_groups(words[8 * half : 8 * half + 8], row8, group8)
            plastic_one[m, 8:9, :] = slot_row

            @pl.when(m != s)
            def _():
                pltpu.make_async_remote_copy(
                    plastic_one.at[m, pl.ds(0, 9)], plastic_got.at[s, pl.ds(0, 9)], pl_one_send, pl_one_recv,
                    device_id=(m, b), device_id_type=MESH,
                ).start()

            @pl.when(m == s)
            def _():
                plastic_got[s, 0:9, :] = plastic_one[m, 0:9, :]

        return carry

    lax.fori_loop(0, EDGE, plastic_out, 0)

    for dy in (-1, 0, 1):
        for dz in (-1, 0, 1):
            inside = (row + dy >= 0) & (row + dy < EDGE) & (inner + dz >= 0) & (inner + dz < EDGE)
            reach = abs(dy) + abs(dz)
            weights[0, plane_number(dy, dz)] = jnp.where(inside, 0.5 * WEIGHTS[reach], 0.0)
            weights[1, plane_number(dy, dz)] = jnp.where(inside, 0.5 * WEIGHTS[reach + 1], 0.0)
    for n in range(9):
        for place in (0, EDGE + 1):
            stiff[n, place] = zero_plane
            for k in range(2):
                for f in range(4):
                    values[k, f, n, place] = zero_plane

    factor = jnp.ones((1, DEPTH), F32)
    lane_row = lane_of((1, DEPTH)) // EDGE
    for p in range(P_DEV):
        factor = jnp.where(lane_row == p, 1.0 + 3.0 * flag[0, 0, p].astype(F32), factor)

    wait_recv(x_copies(5), has_up, has_down)
    wait_recv(y_copies(4), has_right, has_left)

    def face(x, carry):
        here = cond[x + 1]
        ym = jnp.where(row == 0, cond_y[0, pl.ds(x, 1), :], pltpu.roll(here, 1, 0))
        yp = jnp.where(row == EDGE - 1, cond_y[1, pl.ds(x, 1), :], pltpu.roll(here, EDGE - 1, 0))
        zm = jnp.where(lane == 0, 0.0, pltpu.roll(here, 1, 1))
        zp = jnp.where(lane == DEPTH - 1, 0.0, pltpu.roll(here, DEPTH - 1, 1))
        low = 0.06 * (cond[x] + here)
        high = 0.06 * (here + cond[x + 2])
        face_x[x] = low
        face_x[x + 1] = high
        ym, yp, zm, zp = (0.06 * (here + beside) for beside in (ym, yp, zm, zp))
        face_ym[x] = ym
        face_yp[x] = yp
        face_zm[x] = zm
        face_zp[x] = zp
        centre[x] = 1.0 - (low + high + ym + yp + zm + zp)
        return carry

    lax.fori_loop(0, EDGE, face, 0)

    def sweep_plane(t, x):
        around = []
        for f in range(4):
            here = state[t, f, x + 1]
            around.append(
                (
                    here,
                    state[t, f, x],
                    state[t, f, x + 2],
                    jnp.where(row == 0, halo_y[t, 0, f, pl.ds(x, 1), :], pltpu.roll(here, 1, 0)),
                    jnp.where(row == EDGE - 1, halo_y[t, 1, f, pl.ds(x, 1), :], pltpu.roll(here, EDGE - 1, 0)),
                    jnp.where(lane == 0, 0.0, pltpu.roll(here, 1, 1)),
                    jnp.where(lane == DEPTH - 1, 0.0, pltpu.roll(here, DEPTH - 1, 1)),
                )
            )
        h, xm, xp, ym, yp, zm, zp = around[0]
        fresh = [
            centre[x] * h
            + face_x[x] * xm
            + face_x[x + 1] * xp
            + face_ym[x] * ym
            + face_yp[x] * yp
            + face_zm[x] * zm
            + face_zp[x] * zp
        ]
        slopes = (xp - xm, yp - ym, zp - zm)
        for c in range(3):
            u, *six = around[c + 1]
            total = (six[0] + six[1]) + (six[2] + six[3]) + (six[4] + six[5])
            fresh.append(0.28 * u + 0.12 * total - 0.06 * slopes[c])
        for f in range(4):
            state[t + 1, f, x + 1] = fresh[f]
            if t + 1 < SWEEPS:
                stage_y[t + 1, 0, f, pl.ds(x, 1), :] = fresh[f][0:1]
                stage_y[t + 1, 1, f, pl.ds(x, 1), :] = fresh[f][EDGE - 1 : EDGE]

    def sweep(t):
        def middle(x, carry):
            sweep_plane(t, x)
            return carry

        if t + 1 < SWEEPS:
            sweep_plane(t, 0)
            sweep_plane(t, EDGE - 1)
            start(x_copies(t + 1), has_down, has_up)
            lax.fori_loop(1, EDGE - 1, middle, 0)
            start(y_copies(t + 1), has_left, has_right)
        else:
            lax.fori_loop(0, EDGE, middle, 0)

    wait_recv(x_copies(0), has_up, has_down)
    wait_recv(x_copies(4), has_up, has_down)
    wait_recv(y_copies(0), has_right, has_left)
    sweep(0)

    def wait_all(ref, semaphore):
        pltpu.make_async_copy(ref, ref, semaphore).wait()

    wait_all(plastic_got.at[pl.ds(0, N_SLAB - 1), pl.ds(0, 9)], pl_one_recv)
    slot_id = row_of((ROWS, 128))
    for g in range(4):
        codes = plastic_got[8 * g, 8:9, :]
        for k in range(1, 8):
            codes = codes + plastic_got[8 * g + k, 8:9, :]
        one_hot[:, 128 * g : 128 * g + 128] = jnp.where(slot_id == codes, 1.0, 0.0).astype(BF16)

    def plastic_unpack(g, carry):
        words = plastic_got[pl.ds(4 * g, 4), 0:8, :]
        both = jnp.concatenate([lax.shift_right_logical(words, 16), words & 65535], axis=1).reshape(64, 128)
        place = pl.ds(pl.multiple_of(64 * g, 64), 64)
        plastic_table[place, 0:128] = byte_of(both, 0)
        plastic_table[place, 128:256] = byte_of(both, 1)
        return carry

    lax.fori_loop(0, 8, plastic_unpack, 0)

    def plastic_on(step, carry):
        g = lax.rem(step + s // 8, 4)
        place = pl.ds(pl.multiple_of(128 * g, 128), 128)
        rows = jnp.dot(one_hot[place, :], plastic_table[...], preferred_element_type=F32)
        codes = joined(rows[:, 0:128], rows[:, 128:256]).reshape(8, P_DEV, 128)
        plastic_two[pl.ds(8 * g, 8)] = (codes[:, 0:8] << 16) | codes[:, 8:16]
        for k in range(8):
            d = 8 * g + lax.rem(s + k, 8)

            @pl.when(d != s)
            def _():
                pltpu.make_async_remote_copy(
                    plastic_two.at[d], out_plastic.at[s], pl_two_send, pl_two_recv,
                    device_id=(d, b), device_id_type=MESH,
                ).start()

            @pl.when(d == s)
            def _():
                pltpu.make_async_copy(plastic_two.at[d], out_plastic.at[s], own_sem.at[0]).start()

        return carry

    lax.fori_loop(0, 4, plastic_on, 0)

    for t in range(1, SWEEPS):
        wait_recv(x_copies(t), has_up, has_down)
        wait_recv(y_copies(t), has_right, has_left)
        sweep(t)

    def prepare(x, most):
        fields = [state[SWEEPS, f, x + 1] for f in range(4)]
        squared = fields[0] * fields[0]
        stiffness = cond[x + 1] * (1.0 + 0.5 * squared / (1.0 + squared)) / (1.0 + plastic[x]) * factor
        for n, plane in enumerate(shifted_planes(stiffness, row, inner)):
            stiff[n, x + 1] = plane
        for f in range(4):
            for n, plane in enumerate(shifted_planes(fields[f], row, inner)):
                values[0, f, n, x + 1] = plane
        return tuple(jnp.maximum(most[f], jnp.abs(fields[f])) for f in range(4))

    most = lax.fori_loop(0, EDGE, prepare, (zero_plane,) * 4)
    exponents = []
    exponent_row = jnp.zeros((1, 128), I32)
    scales = []
    for f in range(4):
        largest = jnp.max(jnp.max(most[f], axis=0, keepdims=True), axis=1, keepdims=True)
        exponent = jnp.ceil(jnp.log2(jnp.maximum(largest, 1e-30)) + 0.001)
        scales.append(jnp.exp2(-exponent))
        exponent_row = jnp.where(slot_lane == f, exponent.astype(I32), exponent_row)

    def build(x, carry):
        own = stiff[4, x + 1]
        total = jnp.ones((EDGE, DEPTH), F32)
        for number, (dx, dy, dz) in enumerate(OFFSETS):
            n = plane_number(dy, dz)
            weight = weights[abs(dx), n]
            entry = weight * (own + stiff[n, x + 1 + dx])
            if dx < 0:
                entry = entry * (x > 0).astype(F32)
            if dx > 0:
                entry = entry * (x < EDGE - 1).astype(F32)
            entry = entry.astype(BF16).astype(F32)
            tile[number, x] = entry
            total = total + entry
        inverse[x] = 1.0 / total
        return carry

    lax.fori_loop(0, EDGE, build, 0)

    def smoothed(k, x):
        totals = [state[SWEEPS, f, x + 1] for f in range(4)]
        for number, (dx, dy, dz) in enumerate(OFFSETS):
            entry = tile[number, x]
            for f in range(4):
                totals[f] = totals[f] + entry * values[k, f, plane_number(dy, dz), x + 1 + dx]
        scale = inverse[x]
        return [total * scale for total in totals]

    def first(x, carry):
        fields = smoothed(0, x)
        for f in range(4):
            for n, plane in enumerate(shifted_planes(fields[f], row, inner)):
                values[1, f, n, x + 1] = plane
        return carry

    lax.fori_loop(0, EDGE, first, 0)

    def second(step, carry):
        x = lax.rem(step + s // 2, EDGE)
        codes = []
        for f, field in enumerate(smoothed(1, x)):
            part = jnp.abs(field) * scales[f]
            part = jnp.minimum(part * lax.rsqrt(part + 1e-37), 1.0) * 32767.0
            codes.append((jnp.where(field < 0.0, -part, part) + 32768.5).astype(I32))
        words = [(codes[0] << 16) | codes[1], (codes[2] << 16) | codes[3]]
        for half in range(2):
            m = 2 * x + half
            for w in range(2):
                for side in range(2):
                    part = words[w][8 * half : 8 * half + 8, 128 * side : 128 * side + 128]
                    place = 16 * w + 8 * side
                    send_one[m, place : place + 8, :] = swap_rows_and_groups(part, row8, group8)
            send_one[m, 32:33, :] = exponent_row

            @pl.when(m != s)
            def _():
                pltpu.make_async_remote_copy(
                    send_one.at[m, pl.ds(0, 33)], recv_one.at[s, pl.ds(0, 33)], one_send, one_recv,
                    device_id=(m, b), device_id_type=MESH,
                ).start()

            @pl.when(m == s)
            def _():
                recv_one[s, 0:33, :] = send_one[m, 0:33, :]

        return carry

    lax.fori_loop(0, EDGE, second, 0)
    wait_all(recv_one.at[pl.ds(0, N_SLAB - 1), pl.ds(0, 33)], one_recv)

    def unpack(g, carry):
        place = pl.ds(pl.multiple_of(64 * g, 64), 64)
        for w in range(2):
            words = recv_one[pl.ds(4 * g, 4), 16 * w : 16 * w + 16, :].reshape(64, 128)
            for number in range(4):
                at = 128 * (4 * w + number)
                table[place, at : at + 128] = byte_of(words, number)
        return carry

    lax.fori_loop(0, 8, unpack, 0)

    def onward(step, carry):
        g = lax.rem(step + s // 8, 4)
        place = pl.ds(pl.multiple_of(128 * g, 128), 128)
        rows = jnp.dot(one_hot[place, :], table[...], preferred_element_type=F32)
        for w in range(2):
            parts = [rows[:, 128 * (4 * w + n) : 128 * (4 * w + n) + 128] for n in range(4)]
            words = joined(parts[0], parts[1]) | (joined(parts[2], parts[3]) << 16)
            send_two[pl.ds(8 * g, 8), 16 * w : 16 * w + 16, :] = words.reshape(8, P_DEV, 128)
        for k in range(8):
            d = 8 * g + lax.rem(s + k, 8)

            @pl.when(d != s)
            def _():
                pltpu.make_async_remote_copy(
                    send_two.at[d], out_words.at[s], two_send, two_recv,
                    device_id=(d, b), device_id_type=MESH,
                ).start()

            @pl.when(d == s)
            def _():
                pltpu.make_async_copy(send_two.at[d], out_words.at[s], own_sem.at[1]).start()

        return carry

    lax.fori_loop(0, 4, onward, 0)

    sources = jnp.concatenate(
        [jnp.broadcast_to(recv_one[k, 32:33, :].astype(F32), (P_DEV, 128)) for k in range(N_SLAB)], axis=0
    ).astype(BF16)
    mine = one_hot[pl.ds(pl.multiple_of(s * P_DEV, P_DEV), P_DEV), :]
    out_exponents[...] = jnp.dot(mine, sources, preferred_element_type=F32)

    for kind in (0, 1, 2, 3, 4, 5):
        wait_send(x_copies(kind), has_down, has_up)
    for kind in (0, 1, 2, 3, 4):
        wait_send(y_copies(kind), has_left, has_right)
    wait_all(plastic_one.at[pl.ds(0, N_SLAB - 1), pl.ds(0, 9)], pl_one_send)
    wait_all(send_one.at[pl.ds(0, N_SLAB - 1), pl.ds(0, 33)], one_send)
    wait_all(plastic_two.at[pl.ds(0, N_SLAB - 1)], pl_two_send)
    wait_all(send_two.at[pl.ds(0, N_SLAB - 1)], two_send)
    pltpu.make_async_copy(plastic_two.at[s], out_plastic.at[s], own_sem.at[0]).wait()
    pltpu.make_async_copy(send_two.at[s], out_words.at[s], own_sem.at[1]).wait()
    wait_all(out_plastic.at[pl.ds(0, N_SLAB - 1)], pl_two_recv)
    wait_all(out_words.at[pl.ds(0, N_SLAB - 1)], two_recv)


def move(thermal, deform, modulus, plastic, flag, holder, position):
    anywhere = pl.BlockSpec(memory_space=pl.ANY)
    vmem = pl.BlockSpec(memory_space=pltpu.VMEM)
    smem = pl.BlockSpec(memory_space=pltpu.SMEM)
    plane = (EDGE, DEPTH)
    dma = pltpu.SemaphoreType.DMA
    return pl.pallas_call(
        move_kernel,
        name="sweep_solve_move",
        out_shape=(
            jax.ShapeDtypeStruct((N_SLAB, 32, 128), I32),
            jax.ShapeDtypeStruct((N_SLAB, 8, 128), I32),
            jax.ShapeDtypeStruct((P_DEV, 128), F32),
        ),
        in_specs=[anywhere, anywhere, anywhere, vmem, smem, smem, smem],
        out_specs=(anywhere, anywhere, vmem),
        scratch_shapes=[
            pltpu.VMEM((SWEEPS + 1, 4, EDGE + 2) + plane, F32),
            pltpu.VMEM((SWEEPS, 2, 4) + plane, F32),
            pltpu.VMEM((SWEEPS, 2, 4) + plane, F32),
            pltpu.VMEM((EDGE + 2,) + plane, F32),
            pltpu.VMEM((2,) + plane, F32),
            pltpu.VMEM((2,) + plane, F32),
            pltpu.VMEM((EDGE + 1,) + plane, F32),
            pltpu.VMEM((EDGE,) + plane, F32),
            pltpu.VMEM((EDGE,) + plane, F32),
            pltpu.VMEM((EDGE,) + plane, F32),
            pltpu.VMEM((EDGE,) + plane, F32),
            pltpu.VMEM((EDGE,) + plane, F32),
            pltpu.VMEM((9, EDGE + 2) + plane, F32),
            pltpu.VMEM((2, 9) + plane, F32),
            pltpu.VMEM((26, EDGE) + plane, F32),
            pltpu.VMEM((EDGE,) + plane, F32),
            pltpu.VMEM((2, 4, 9, EDGE + 2) + plane, F32),
            pltpu.VMEM((N_SLAB, 40, 128), I32),
            pltpu.VMEM((N_SLAB, 40, 128), I32),
            pltpu.VMEM((N_SLAB, 32, 128), I32),
            pltpu.VMEM((N_SLAB, 16, 128), I32),
            pltpu.VMEM((N_SLAB, 16, 128), I32),
            pltpu.VMEM((N_SLAB, 8, 128), I32),
            pltpu.VMEM((ROWS, ROWS), BF16),
            pltpu.VMEM((ROWS, 1024), BF16),
            pltpu.VMEM((ROWS, 256), BF16),
            dma((3,)),
            dma((6, 2)),
            dma((6, 2)),
            dma((5, 2)),
            dma((5, 2)),
            dma(()),
            dma(()),
            dma(()),
            dma(()),
            dma(()),
            dma(()),
            dma(()),
            dma(()),
            dma((2,)),
        ],
        compiler_params=pltpu.CompilerParams(
            collective_id=0, has_side_effects=True, vmem_limit_bytes=56 * 1024 * 1024
        ),
    )(thermal, deform, modulus, plastic, flag, holder, position)


def decode_kernel(words, plastic, exponents, heat_out, moved_out, plastic_out):
    scales = [jnp.exp2(exponents[:, f : f + 1]) * (1.0 / (32767.0 * 32767.0)) for f in range(4)]

    def piece(m, carry):
        at = pl.ds(pl.multiple_of(128 * m, 128), 128)
        for w in range(2):
            word = words[m, 16 * w : 16 * w + 16, :]
            for part in range(2):
                code = lax.shift_right_logical(word, 16) if part == 0 else word & 65535
                root = (code - 32768).astype(F32)
                field = root * jnp.abs(root) * scales[2 * w + part]
                if w == 0 and part == 0:
                    heat_out[0, 0, :, at] = field
                else:
                    moved_out[0, 0, :, 2 * w + part - 1, at] = field
        word = plastic[m]
        for part in range(2):
            code = lax.shift_right_logical(word, 16) if part == 0 else word & 65535
            root = code.astype(F32) * (1.0 / PLASTIC_STEPS) + PLASTIC_LOW
            plastic_out[0, 0, 8 * part : 8 * part + 8, at] = root * root
        return carry

    lax.fori_loop(0, N_SLAB, piece, 0)


def decode(words, plastic, exponents):
    vmem = pl.BlockSpec(memory_space=pltpu.VMEM)
    length = EDGE**3
    return pl.pallas_call(
        decode_kernel,
        name="decode",
        out_shape=(
            jax.ShapeDtypeStruct((1, 1, P_DEV, length), F32),
            jax.ShapeDtypeStruct((1, 1, P_DEV, 3, length), F32),
            jax.ShapeDtypeStruct((1, 1, P_DEV, length), F32),
        ),
        in_specs=[vmem] * 3,
        out_specs=(vmem,) * 3,
        compiler_params=pltpu.CompilerParams(vmem_limit_bytes=24 * 1024 * 1024),
    )(words, plastic, exponents)


def on_device(thermal, deform, modulus, plastic, flag, holder, position):
    return decode(*move(thermal, deform, modulus, plastic, flag, holder, position))


def solution(mesh):
    placed = (
        P("slab", "blk", None),
        P(None, "slab", "blk", None),
        P("slab", "blk", None),
        P("slab", "blk", None),
        P("slab", "blk", None),
        P("slab", "blk", None),
        P("slab", "blk", None),
    )
    return jax.shard_map(
        on_device,
        mesh=mesh,
        in_specs=placed,
        out_specs=(
            P("slab", "blk", None, None),
            P("slab", "blk", None, None, None),
            P("slab", "blk", None, None),
        ),
        check_vma=False,
    )
```

```python
import jax
import jax.numpy as jnp
from jax import lax
from jax.experimental import pallas as pl
from jax.experimental.pallas import tpu as pltpu
from jax.sharding import PartitionSpec as P

EDGE = 16
DEPTH = 256
SWEEPS = 4
N_SLAB = 32
N_BLK = 4
P_DEV = 16
ROWS = N_SLAB * P_DEV
MESH = pl.DeviceIdType.MESH
F32 = jnp.float32
I32 = jnp.int32
BF16 = jnp.bfloat16

PLASTIC_LOW = 0.2235
PLASTIC_STEPS = 65535.0 / (1.4145 - PLASTIC_LOW)

OFFSETS = [
    (dx, dy, dz)
    for dx in (-1, 0, 1)
    for dy in (-1, 0, 1)
    for dz in (-1, 0, 1)
    if (dx, dy, dz) != (0, 0, 0)
]
WEIGHTS = [0.0, 0.1, 0.04, 0.02]


def plane_number(dy, dz):
    return (dy + 1) * 3 + dz + 1


def lane_of(shape):
    return lax.broadcasted_iota(I32, shape, 1)


def row_of(shape):
    return lax.broadcasted_iota(I32, shape, 0)


def shifted_pairs(pair, row8):
    low, high = pair
    out = [None] * 9
    for dz in (-1, 0, 1):
        a, b = (low, high) if dz == 0 else [pltpu.roll(part, 1 if dz < 0 else 127, 1) for part in pair]
        a_down, b_down = pltpu.roll(a, 1, 0), pltpu.roll(b, 1, 0)
        a_up, b_up = pltpu.roll(a, 7, 0), pltpu.roll(b, 7, 0)
        out[plane_number(-1, dz)] = (a_down, jnp.where(row8 == 0, a_down, b_down))
        out[plane_number(0, dz)] = (a, b)
        out[plane_number(1, dz)] = (jnp.where(row8 == 7, b_up, a_up), b_up)
    return out


def swap_rows_and_groups(tiles, group, first, second):
    for k in range(8):
        first[8 * k : 8 * k + 8, :] = tiles[k]
    parts = [first[pl.ds(k, 8, stride=8), :] for k in range(8)]
    for bit in (4, 2, 1):
        low_group = (group & bit) == 0
        for k in range(8):
            if k & bit == 0:
                low, high = parts[k], parts[k | bit]
                parts[k] = jnp.where(low_group, low, pltpu.roll(high, 16 * bit, 1))
                parts[k | bit] = jnp.where(low_group, pltpu.roll(low, 128 - 16 * bit, 1), high)
    for k in range(8):
        second[8 * k : 8 * k + 8, :] = parts[k]
    return [second[pl.ds(k, 8, stride=8), :] for k in range(8)]


def byte_of(words, number):
    part = words if number == 0 else lax.shift_right_logical(words, 8 * number)
    return (part & 255).astype(F32).astype(BF16)


def joined(low, high):
    return (low + 256.0 * high).astype(I32)


def move_kernel(
    thermal, deform, modulus, plastic, flag, holder, position,
    out_words, out_plastic, out_exponents,
    state, halo_y, stage_y, cond, cond_y, cond_stage,
    face_x, face_ym, face_yp, face_zm, face_zp, centre,
    stiff, weights, tile, inverse, values,
    send_one, recv_one, send_two, plastic_one, plastic_got, plastic_two,
    one_hot, table, plastic_table, swap_a, swap_b,
    load_sem, x_send, x_recv, y_send, y_recv,
    one_send, one_recv, two_send, two_recv, pl_one_send, pl_one_recv, pl_two_send, pl_two_recv, own_sem,
):
    s = lax.axis_index("slab")
    b = lax.axis_index("blk")
    chip = s // 2
    up, down = lax.rem(s + 1, N_SLAB), lax.rem(s + N_SLAB - 1, N_SLAB)
    right, left = lax.rem(b + 1, N_BLK), lax.rem(b + N_BLK - 1, N_BLK)
    has_up, has_down = s < N_SLAB - 1, s > 0
    has_right, has_left = b < N_BLK - 1, b > 0

    loads = [
        pltpu.make_async_copy(thermal, state.at[0, 0, pl.ds(1, EDGE)], load_sem.at[0]),
        pltpu.make_async_copy(deform, state.at[0, pl.ds(1, 3), pl.ds(1, EDGE)], load_sem.at[1]),
        pltpu.make_async_copy(modulus, cond.at[pl.ds(1, EDGE)], load_sem.at[2]),
    ]
    for load in loads:
        load.start()

    barrier = pltpu.get_barrier_semaphore()

    def greet(step, carry):
        peer = lax.rem(s + step, N_SLAB)
        pl.semaphore_signal(barrier, inc=1, device_id=(peer, b), device_id_type=MESH)
        return carry

    lax.fori_loop(1, N_SLAB, greet, 0)

    @pl.when(has_right)
    def _():
        pl.semaphore_signal(barrier, inc=1, device_id=(s, right), device_id_type=MESH)

    @pl.when(has_left)
    def _():
        pl.semaphore_signal(barrier, inc=1, device_id=(s, left), device_id_type=MESH)

    zero_plane = jnp.zeros((EDGE, DEPTH), F32)

    for has, place, side in ((has_down, 0, 0), (has_up, EDGE + 1, 1)):

        @pl.when(jnp.logical_not(has))
        def _():
            cond[place] = zero_plane
            for t in range(SWEEPS):
                for f in range(4):
                    state[t, f, place] = zero_plane

    for has, side in ((has_left, 0), (has_right, 1)):

        @pl.when(jnp.logical_not(has))
        def _():
            cond_y[side] = zero_plane
            for t in range(SWEEPS):
                for f in range(4):
                    halo_y[t, side, f] = zero_plane

    neighbours = 31 + has_right.astype(I32) + has_left.astype(I32)
    pl.semaphore_wait(barrier, neighbours)

    def x_copies(kind):
        out = []
        for direction, peer in ((0, down), (1, up)):
            mine = 0 if direction == 0 else EDGE - 1
            there = EDGE + 1 if direction == 0 else 0
            if kind == 0:
                source, target = thermal.at[mine], state.at[0, 0, there]
            elif kind == 4:
                source, target = deform.at[:, mine], state.at[0, pl.ds(1, 3), there]
            elif kind == 5:
                source, target = modulus.at[mine], cond.at[there]
            else:
                source, target = state.at[kind, :, mine + 1], state.at[kind, :, there]
            out.append(
                pltpu.make_async_remote_copy(
                    source, target, x_send.at[kind, direction], x_recv.at[kind, direction],
                    device_id=(peer, b), device_id_type=MESH,
                )
            )
        return out

    def y_copies(kind):
        out = []
        for direction, peer in ((0, left), (1, right)):
            if kind == 4:
                source, target = cond_stage.at[direction], cond_y.at[1 - direction]
            else:
                source, target = stage_y.at[kind, direction], halo_y.at[kind, 1 - direction]
            out.append(
                pltpu.make_async_remote_copy(
                    source, target, y_send.at[kind, direction], y_recv.at[kind, direction],
                    device_id=(s, peer), device_id_type=MESH,
                )
            )
        return out

    def start(copies, to_low, to_high):
        @pl.when(to_low)
        def _():
            copies[0].start()

        @pl.when(to_high)
        def _():
            copies[1].start()

    def wait_recv(copies, from_high, from_low):
        @pl.when(from_high)
        def _():
            copies[0].wait_recv()

        @pl.when(from_low)
        def _():
            copies[1].wait_recv()

    def wait_send(copies, to_low, to_high):
        @pl.when(to_low)
        def _():
            copies[0].wait_send()

        @pl.when(to_high)
        def _():
            copies[1].wait_send()

    for kind in (5, 0, 4):
        start(x_copies(kind), has_down, has_up)
    for load in loads:
        load.wait()

    def stage_first(x, carry):
        for side, y in ((0, 0), (1, EDGE - 1)):
            cond_stage[side, pl.ds(x, 1), :] = cond[x + 1, y : y + 1, :]
            for f in range(4):
                stage_y[0, side, f, pl.ds(x, 1), :] = state[0, f, x + 1, y : y + 1, :]
        return carry

    lax.fori_loop(0, EDGE, stage_first, 0)
    start(y_copies(4), has_left, has_right)
    start(y_copies(0), has_left, has_right)

    row8 = row_of((8, 128))
    group8 = lane_of((8, 128)) // EDGE
    row = row_of((EDGE, DEPTH))
    lane = lane_of((EDGE, DEPTH))
    inner = lane & (EDGE - 1)

    slot_lane = lane_of((1, 128))
    slot_row = jnp.zeros((1, 128), I32)
    for p in range(P_DEV):
        code = holder[0, 0, p] * P_DEV + position[0, 0, p]
        slot_row = jnp.where(slot_lane == lax.rem(s, 8) * P_DEV + p, code, slot_row)

    sibling = lax.bitwise_xor(s, 1)

    def send_plastic(m):
        pltpu.make_async_remote_copy(
            plastic_one.at[m, pl.ds(0, 9)], plastic_got.at[s, pl.ds(0, 9)], pl_one_send, pl_one_recv,
            device_id=(m, b), device_id_type=MESH,
        ).start()

    def plastic_planes(planes):
        tiles = []
        for x in planes:
            root = plastic[x]
            root = root * lax.rsqrt(root)
            codes = jnp.clip((root - PLASTIC_LOW) * PLASTIC_STEPS + 0.5, 0.0, 65535.0).astype(I32)
            words = (codes[:, 0:128] << 16) | codes[:, 128:256]
            tiles += [words[0:8], words[8:16]]
        tiles = swap_rows_and_groups(tiles, group8, swap_a, swap_b)
        for k in range(8):
            m = 2 * planes[k // 2] + k % 2
            plastic_one[m, 0:8, :] = tiles[k]
            plastic_one[m, 8:9, :] = slot_row

    def plastic_out(step, carry):
        planes = [lax.rem(chip + 4 * step + j, EDGE) for j in range(4)]
        plastic_planes(planes)
        for x in planes:
            send_plastic(2 * x)
            send_plastic(2 * x + 1)
        return carry

    planes = [lax.rem(chip + j, EDGE) for j in range(4)]
    plastic_planes(planes)
    send_plastic(sibling)
    plastic_got[s, 0:9, :] = plastic_one[s, 0:9, :]
    for x in planes[1:]:
        send_plastic(2 * x)
        send_plastic(2 * x + 1)
    lax.fori_loop(1, 4, plastic_out, 0)

    for dy in (-1, 0, 1):
        for dz in (-1, 0, 1):
            inside = (row + dy >= 0) & (row + dy < EDGE) & (inner + dz >= 0) & (inner + dz < EDGE)
            reach = abs(dy) + abs(dz)
            weights[0, plane_number(dy, dz)] = jnp.where(inside, 0.5 * WEIGHTS[reach], 0.0)
            weights[1, plane_number(dy, dz)] = jnp.where(inside, 0.5 * WEIGHTS[reach + 1], 0.0)
    for n in range(9):
        for f in range(4):
            values[f, n, 0] = zero_plane
            values[f, n, EDGE + 1] = zero_plane
    for number, (dx, dy, dz) in enumerate(OFFSETS):
        if dx != 0:
            tile[number, 1 if dx < 0 else EDGE] = zero_plane

    factor = jnp.ones((1, DEPTH), F32)
    lane_row = lane_of((1, DEPTH)) // EDGE
    for p in range(P_DEV):
        factor = jnp.where(lane_row == p, 1.0 + 3.0 * flag[0, 0, p].astype(F32), factor)

    wait_recv(x_copies(5), has_up, has_down)
    wait_recv(y_copies(4), has_right, has_left)

    def face(x, carry):
        here = cond[x + 1]
        ym = jnp.where(row == 0, cond_y[0, pl.ds(x, 1), :], pltpu.roll(here, 1, 0))
        yp = jnp.where(row == EDGE - 1, cond_y[1, pl.ds(x, 1), :], pltpu.roll(here, EDGE - 1, 0))
        zm = jnp.where(lane == 0, 0.0, pltpu.roll(here, 1, 1))
        zp = jnp.where(lane == DEPTH - 1, 0.0, pltpu.roll(here, DEPTH - 1, 1))
        low = 0.06 * (cond[x] + here)
        high = 0.06 * (here + cond[x + 2])
        face_x[x] = low
        face_x[x + 1] = high
        ym, yp, zm, zp = (0.06 * (here + beside) for beside in (ym, yp, zm, zp))
        face_ym[x] = ym
        face_yp[x] = yp
        face_zm[x] = zm
        face_zp[x] = zp
        centre[x] = 1.0 - (low + high + ym + yp + zm + zp)
        return carry

    lax.fori_loop(0, EDGE, face, 0)

    def sweep_plane(t, x):
        around = []
        for f in range(4):
            here = state[t, f, x + 1]
            around.append(
                (
                    here,
                    state[t, f, x],
                    state[t, f, x + 2],
                    jnp.where(row == 0, halo_y[t, 0, f, pl.ds(x, 1), :], pltpu.roll(here, 1, 0)),
                    jnp.where(row == EDGE - 1, halo_y[t, 1, f, pl.ds(x, 1), :], pltpu.roll(here, EDGE - 1, 0)),
                    jnp.where(lane == 0, 0.0, pltpu.roll(here, 1, 1)),
                    jnp.where(lane == DEPTH - 1, 0.0, pltpu.roll(here, DEPTH - 1, 1)),
                )
            )
        h, xm, xp, ym, yp, zm, zp = around[0]
        fresh = [
            centre[x] * h
            + face_x[x] * xm
            + face_x[x + 1] * xp
            + face_ym[x] * ym
            + face_yp[x] * yp
            + face_zm[x] * zm
            + face_zp[x] * zp
        ]
        slopes = (xp - xm, yp - ym, zp - zm)
        for c in range(3):
            u, *six = around[c + 1]
            total = (six[0] + six[1]) + (six[2] + six[3]) + (six[4] + six[5])
            fresh.append(0.28 * u + 0.12 * total - 0.06 * slopes[c])
        for f in range(4):
            state[t + 1, f, x + 1] = fresh[f]
            if t + 1 < SWEEPS:
                stage_y[t + 1, 0, f, pl.ds(x, 1), :] = fresh[f][0:1]
                stage_y[t + 1, 1, f, pl.ds(x, 1), :] = fresh[f][EDGE - 1 : EDGE]

    def sweep(t):
        def middle(x, carry):
            sweep_plane(t, x)
            return carry

        if t + 1 < SWEEPS:
            sweep_plane(t, 0)
            sweep_plane(t, EDGE - 1)
            start(x_copies(t + 1), has_down, has_up)
            lax.fori_loop(1, EDGE - 1, middle, 0)
            start(y_copies(t + 1), has_left, has_right)
        else:
            lax.fori_loop(0, EDGE, middle, 0)

    wait_recv(x_copies(0), has_up, has_down)
    wait_recv(x_copies(4), has_up, has_down)
    wait_recv(y_copies(0), has_right, has_left)
    sweep(0)

    def wait_all(ref, semaphore):
        pltpu.make_async_copy(ref, ref, semaphore).wait()

    wait_all(plastic_got.at[pl.ds(0, N_SLAB - 1), pl.ds(0, 9)], pl_one_recv)
    slot_id = row_of((ROWS, 128))
    for g in range(4):
        codes = plastic_got[8 * g, 8:9, :]
        for k in range(1, 8):
            codes = codes + plastic_got[8 * g + k, 8:9, :]
        one_hot[:, 128 * g : 128 * g + 128] = jnp.where(slot_id == codes, 1.0, 0.0).astype(BF16)

    def plastic_unpack(g, carry):
        words = plastic_got[pl.ds(4 * g, 4), 0:8, :]
        both = jnp.concatenate([lax.shift_right_logical(words, 16), words & 65535], axis=1).reshape(64, 128)
        place = pl.ds(pl.multiple_of(64 * g, 64), 64)
        plastic_table[place, 0:128] = byte_of(both, 0)
        plastic_table[place, 128:256] = byte_of(both, 1)
        return carry

    lax.fori_loop(0, 8, plastic_unpack, 0)

    def plastic_group(g):
        place = pl.ds(pl.multiple_of(128 * g, 128), 128)
        rows = jnp.dot(one_hot[place, :], plastic_table[...], preferred_element_type=F32)
        codes = joined(rows[:, 0:128], rows[:, 128:256]).reshape(8, P_DEV, 128)
        plastic_two[pl.ds(8 * g, 8)] = (codes[:, 0:8] << 16) | codes[:, 8:16]

    def pass_plastic(d):
        pltpu.make_async_remote_copy(
            plastic_two.at[d], out_plastic.at[s], pl_two_send, pl_two_recv,
            device_id=(d, b), device_id_type=MESH,
        ).start()

    def plastic_on(step, carry):
        g = lax.rem(step + s // 8, 4)
        plastic_group(g)
        for k in range(8):
            pass_plastic(8 * g + lax.rem(s + k, 8))
        return carry

    plastic_group(s // 8)
    pltpu.make_async_copy(plastic_two.at[s], out_plastic.at[s], own_sem.at[0]).start()
    for k in range(1, 8):
        pass_plastic(8 * (s // 8) + lax.rem(s + k, 8))
    lax.fori_loop(1, 4, plastic_on, 0)

    for t in range(1, SWEEPS):
        wait_recv(x_copies(t), has_up, has_down)
        wait_recv(y_copies(t), has_right, has_left)
        sweep(t)

    def prepare(x, most):
        fields = [state[SWEEPS, f, x + 1] for f in range(4)]
        squared = fields[0] * fields[0]
        stiff[x + 1] = cond[x + 1] * (1.0 + 0.5 * squared / (1.0 + squared)) / (1.0 + plastic[x]) * factor
        return tuple(jnp.maximum(most[f], jnp.abs(fields[f])) for f in range(4))

    most = lax.fori_loop(0, EDGE, prepare, (zero_plane,) * 4)
    exponents = []
    exponent_row = jnp.zeros((1, 128), I32)
    scales = []
    for f in range(4):
        largest = jnp.max(jnp.max(most[f], axis=0, keepdims=True), axis=1, keepdims=True)
        exponent = jnp.ceil(jnp.log2(jnp.maximum(largest, 1e-30)) + 0.001)
        scales.append(jnp.exp2(-exponent))
        exponent_row = jnp.where(slot_lane == f, exponent.astype(I32), exponent_row)

    numbers = {offset: number for number, offset in enumerate(OFFSETS)}
    halves = (slice(0, 8), slice(8, 16))
    ones = (jnp.ones((8, 128), F32),) * 2

    def built(x, done, active, side):
        lanes = slice(128 * side, 128 * side + 128)
        begun = [ones] + [tuple(state[SWEEPS, f, x + 2, rows, lanes] for rows in halves) for f in range(4)]
        totals = {1: list(done), 0: list(active), -1: begun}
        own = {dx: [stiff[x + 1 - dx, rows, lanes] for rows in halves] for dx in (-1, 0, 1)}
        near = shifted_pairs(own[0], row8)
        fields = [
            shifted_pairs([state[SWEEPS, f, x + 1, rows, lanes] for rows in halves], row8) for f in range(4)
        ]
        for dz in (-1, 0, 1):
            for dy in (-1, 0, 1):
                n = plane_number(dy, dz)
                for dx in (-1, 0, 1):
                    if (dx, dy, dz) == (0, 0, 0):
                        continue
                    number = numbers[dx, dy, dz]
                    entries = []
                    for j, rows in enumerate(halves):
                        entry = weights[abs(dx), n, rows, 0:128] * (own[dx][j] + near[n][j])
                        entry = entry.astype(BF16).astype(F32)
                        tile[number, x + 1 - dx, rows, lanes] = entry
                        entries.append(entry)
                    total = totals[dx]
                    total[0] = tuple(total[0][j] + entries[j] for j in range(2))
                    for f in range(4):
                        total[f + 1] = tuple(total[f + 1][j] + entries[j] * fields[f][n][j] for j in range(2))
        return tuple(totals[1]), tuple(totals[0]), tuple(totals[-1])

    def finish(place, done, side):
        lanes = slice(128 * side, 128 * side + 128)
        scale = [1.0 / part for part in done[0]]
        for j, rows in enumerate(halves):
            inverse[place, rows, lanes] = scale[j]
        for f in range(4):
            field = [done[f + 1][j] * scale[j] for j in range(2)]
            for n, pair in enumerate(shifted_pairs(field, row8)):
                for j, rows in enumerate(halves):
                    values[f, n, place, rows, lanes] = pair[j]

    for side in range(2):

        def source(x, carry):
            done, active, begun = built(x, *carry, side)

            @pl.when(x > 0)
            def _():
                finish(x, done, side)

            return active, begun

        lanes = slice(128 * side, 128 * side + 128)
        start_at = (ones,) + tuple(tuple(state[SWEEPS, f, 1, rows, lanes] for rows in halves) for f in range(4))
        last, _ = lax.fori_loop(0, EDGE, source, ((ones,) * 5, start_at))
        finish(EDGE, last, side)

    def smoothed(x):
        totals = [state[SWEEPS, f, x + 1] for f in range(4)]
        for number, (dx, dy, dz) in enumerate(OFFSETS):
            entry = tile[number, x + 1]
            for f in range(4):
                totals[f] = totals[f] + entry * values[f, plane_number(dy, dz), x + 1 + dx]
        scale = inverse[x + 1]
        return [total * scale for total in totals]

    def send_plane(m):
        pltpu.make_async_remote_copy(
            send_one.at[m, pl.ds(0, 33)], recv_one.at[s, pl.ds(0, 33)], one_send, one_recv,
            device_id=(m, b), device_id_type=MESH,
        ).start()

    def second_plane(x):
        codes = []
        for f, field in enumerate(smoothed(x)):
            part = jnp.abs(field) * scales[f]
            part = jnp.minimum(part * lax.rsqrt(part + 1e-37), 1.0) * 32767.0
            codes.append((jnp.where(field < 0.0, -part, part) + 32768.5).astype(I32))
        words = [(codes[0] << 16) | codes[1], (codes[2] << 16) | codes[3]]
        tiles = [
            words[w][8 * half : 8 * half + 8, 128 * side : 128 * side + 128]
            for half in range(2)
            for w in range(2)
            for side in range(2)
        ]
        tiles = swap_rows_and_groups(tiles, group8, swap_a, swap_b)
        for half in range(2):
            m = 2 * x + half
            for k in range(4):
                send_one[m, 8 * k : 8 * k + 8, :] = tiles[4 * half + k]
            send_one[m, 32:33, :] = exponent_row

    def second(step, carry):
        x = lax.rem(step + chip, EDGE)
        second_plane(x)
        send_plane(2 * x)
        send_plane(2 * x + 1)
        return carry

    second_plane(chip)
    send_plane(sibling)
    recv_one[s, 0:33, :] = send_one[s, 0:33, :]
    lax.fori_loop(1, EDGE, second, 0)
    wait_all(recv_one.at[pl.ds(0, N_SLAB - 1), pl.ds(0, 33)], one_recv)

    def unpack(g, carry):
        place = pl.ds(pl.multiple_of(64 * g, 64), 64)
        for w in range(2):
            words = recv_one[pl.ds(4 * g, 4), 16 * w : 16 * w + 16, :].reshape(64, 128)
            for number in range(4):
                at = 128 * (4 * w + number)
                table[place, at : at + 128] = byte_of(words, number)
        return carry

    lax.fori_loop(0, 8, unpack, 0)

    def onward_group(g):
        place = pl.ds(pl.multiple_of(128 * g, 128), 128)
        rows = jnp.dot(one_hot[place, :], table[...], preferred_element_type=F32)
        for w in range(2):
            parts = [rows[:, 128 * (4 * w + n) : 128 * (4 * w + n) + 128] for n in range(4)]
            words = joined(parts[0], parts[1]) | (joined(parts[2], parts[3]) << 16)
            send_two[pl.ds(8 * g, 8), 16 * w : 16 * w + 16, :] = words.reshape(8, P_DEV, 128)

    def pass_on(d):
        pltpu.make_async_remote_copy(
            send_two.at[d], out_words.at[s], two_send, two_recv,
            device_id=(d, b), device_id_type=MESH,
        ).start()

    def onward(step, carry):
        g = lax.rem(step + s // 8, 4)
        onward_group(g)
        for k in range(8):
            pass_on(8 * g + lax.rem(s + k, 8))
        return carry

    onward_group(s // 8)
    pltpu.make_async_copy(send_two.at[s], out_words.at[s], own_sem.at[1]).start()
    for k in range(1, 8):
        pass_on(8 * (s // 8) + lax.rem(s + k, 8))
    lax.fori_loop(1, 4, onward, 0)

    sources = jnp.concatenate(
        [jnp.broadcast_to(recv_one[k, 32:33, :].astype(F32), (P_DEV, 128)) for k in range(N_SLAB)], axis=0
    ).astype(BF16)
    mine = one_hot[pl.ds(pl.multiple_of(s * P_DEV, P_DEV), P_DEV), :]
    out_exponents[...] = jnp.dot(mine, sources, preferred_element_type=F32)

    for kind in (0, 1, 2, 3, 4, 5):
        wait_send(x_copies(kind), has_down, has_up)
    for kind in (0, 1, 2, 3, 4):
        wait_send(y_copies(kind), has_left, has_right)
    wait_all(plastic_one.at[pl.ds(0, N_SLAB - 1), pl.ds(0, 9)], pl_one_send)
    wait_all(send_one.at[pl.ds(0, N_SLAB - 1), pl.ds(0, 33)], one_send)
    wait_all(plastic_two.at[pl.ds(0, N_SLAB - 1)], pl_two_send)
    wait_all(send_two.at[pl.ds(0, N_SLAB - 1)], two_send)
    pltpu.make_async_copy(plastic_two.at[s], out_plastic.at[s], own_sem.at[0]).wait()
    pltpu.make_async_copy(send_two.at[s], out_words.at[s], own_sem.at[1]).wait()
    wait_all(out_plastic.at[pl.ds(0, N_SLAB - 1)], pl_two_recv)
    wait_all(out_words.at[pl.ds(0, N_SLAB - 1)], two_recv)


def move(thermal, deform, modulus, plastic, flag, holder, position):
    anywhere = pl.BlockSpec(memory_space=pl.ANY)
    vmem = pl.BlockSpec(memory_space=pltpu.VMEM)
    smem = pl.BlockSpec(memory_space=pltpu.SMEM)
    plane = (EDGE, DEPTH)
    dma = pltpu.SemaphoreType.DMA
    return pl.pallas_call(
        move_kernel,
        name="sweep_solve_move",
        out_shape=(
            jax.ShapeDtypeStruct((N_SLAB, 32, 128), I32),
            jax.ShapeDtypeStruct((N_SLAB, 8, 128), I32),
            jax.ShapeDtypeStruct((P_DEV, 128), F32),
        ),
        in_specs=[anywhere, anywhere, anywhere, vmem, smem, smem, smem],
        out_specs=(anywhere, anywhere, vmem),
        scratch_shapes=[
            pltpu.VMEM((SWEEPS + 1, 4, EDGE + 2) + plane, F32),
            pltpu.VMEM((SWEEPS, 2, 4) + plane, F32),
            pltpu.VMEM((SWEEPS, 2, 4) + plane, F32),
            pltpu.VMEM((EDGE + 2,) + plane, F32),
            pltpu.VMEM((2,) + plane, F32),
            pltpu.VMEM((2,) + plane, F32),
            pltpu.VMEM((EDGE + 1,) + plane, F32),
            pltpu.VMEM((EDGE,) + plane, F32),
            pltpu.VMEM((EDGE,) + plane, F32),
            pltpu.VMEM((EDGE,) + plane, F32),
            pltpu.VMEM((EDGE,) + plane, F32),
            pltpu.VMEM((EDGE,) + plane, F32),
            pltpu.VMEM((EDGE + 2,) + plane, F32),
            pltpu.VMEM((2, 9) + plane, F32),
            pltpu.VMEM((26, EDGE + 2) + plane, F32),
            pltpu.VMEM((EDGE + 1,) + plane, F32),
            pltpu.VMEM((4, 9, EDGE + 2) + plane, F32),
            pltpu.VMEM((N_SLAB, 40, 128), I32),
            pltpu.VMEM((N_SLAB, 40, 128), I32),
            pltpu.VMEM((N_SLAB, 32, 128), I32),
            pltpu.VMEM((N_SLAB, 16, 128), I32),
            pltpu.VMEM((N_SLAB, 16, 128), I32),
            pltpu.VMEM((N_SLAB, 8, 128), I32),
            pltpu.VMEM((ROWS, ROWS), BF16),
            pltpu.VMEM((ROWS, 1024), BF16),
            pltpu.VMEM((ROWS, 256), BF16),
            pltpu.VMEM((64, 128), I32),
            pltpu.VMEM((64, 128), I32),
            dma((3,)),
            dma((6, 2)),
            dma((6, 2)),
            dma((5, 2)),
            dma((5, 2)),
            dma(()),
            dma(()),
            dma(()),
            dma(()),
            dma(()),
            dma(()),
            dma(()),
            dma(()),
            dma((2,)),
        ],
        compiler_params=pltpu.CompilerParams(
            collective_id=0, has_side_effects=True, vmem_limit_bytes=56 * 1024 * 1024
        ),
    )(thermal, deform, modulus, plastic, flag, holder, position)


def decode_kernel(
    words_in, plastic_in, exponents, heat_out, moved_out, plastic_out, words, strain, heat, moved, straight, got, put
):
    pieces = N_SLAB // 4
    fetch = [
        pltpu.make_async_copy(words_in.at[pl.ds(pieces * k, pieces)], words.at[pl.ds(pieces * k, pieces)], got.at[k])
        for k in range(4)
    ]
    fetch.append(pltpu.make_async_copy(plastic_in, strain, got.at[4]))
    for copy in fetch:
        copy.start()
    scales = [
        jnp.broadcast_to(jnp.exp2(exponents[:, f : f + 1]) * (1.0 / (32767.0 * 32767.0)), (P_DEV, 128))
        for f in range(4)
    ]
    length = 128 * pieces
    writes = []
    for k in range(4):
        fetch[k].wait()
        for m in range(pieces * k, pieces * k + pieces):
            at = slice(128 * m, 128 * m + 128)
            for w in range(2):
                word = words[m, 16 * w : 16 * w + 16, :]
                for part in range(2):
                    code = lax.shift_right_logical(word, 16) if part == 0 else word & 65535
                    root = (code - 32768).astype(F32)
                    field = root * jnp.abs(root) * scales[2 * w + part]
                    if w == 0 and part == 0:
                        heat[:, at] = field
                    else:
                        moved[2 * w + part - 1, :, at] = field
        at = pl.ds(length * k, length)
        writes.append(pltpu.make_async_copy(heat.at[:, at], heat_out.at[0, 0, :, at], put.at[3 * k]))
        writes.append(pltpu.make_async_copy(moved.at[:, :, at], moved_out.at[0, 0, :, :, at], put.at[3 * k + 1]))
        for copy in writes[-2:]:
            copy.start()
        if k == 0:
            fetch[4].wait()
        for m in range(pieces * k, pieces * k + pieces):
            word = strain[m]
            for part in range(2):
                code = lax.shift_right_logical(word, 16) if part == 0 else word & 65535
                root = code.astype(F32) * (1.0 / PLASTIC_STEPS) + PLASTIC_LOW
                straight[8 * part : 8 * part + 8, 128 * m : 128 * m + 128] = root * root
        writes.append(pltpu.make_async_copy(straight.at[:, at], plastic_out.at[0, 0, :, at], put.at[3 * k + 2]))
        writes[-1].start()
    for copy in writes:
        copy.wait()


def decode(words, plastic, exponents):
    vmem = pl.BlockSpec(memory_space=pltpu.VMEM)
    anywhere = pl.BlockSpec(memory_space=pl.ANY)
    length = EDGE**3
    heat, moved, strain = pl.pallas_call(
        decode_kernel,
        name="decode",
        out_shape=(
            jax.ShapeDtypeStruct((1, 1, P_DEV, length), F32),
            jax.ShapeDtypeStruct((1, 1, 3, P_DEV, length), F32),
            jax.ShapeDtypeStruct((1, 1, P_DEV, length), F32),
        ),
        in_specs=[anywhere, anywhere, vmem],
        out_specs=(anywhere,) * 3,
        scratch_shapes=[
            pltpu.VMEM((N_SLAB, 32, 128), I32),
            pltpu.VMEM((N_SLAB, 8, 128), I32),
            pltpu.VMEM((P_DEV, length), F32),
            pltpu.VMEM((3, P_DEV, length), F32),
            pltpu.VMEM((P_DEV, length), F32),
            pltpu.SemaphoreType.DMA((5,)),
            pltpu.SemaphoreType.DMA((12,)),
        ],
        compiler_params=pltpu.CompilerParams(vmem_limit_bytes=56 * 1024 * 1024),
    )(words, plastic, exponents)
    return heat, moved.transpose(0, 1, 3, 2, 4), strain


def on_device(thermal, deform, modulus, plastic, flag, holder, position):
    return decode(*move(thermal, deform, modulus, plastic, flag, holder, position))


def solution(mesh):
    placed = (
        P("slab", "blk", None),
        P(None, "slab", "blk", None),
        P("slab", "blk", None),
        P("slab", "blk", None),
        P("slab", "blk", None),
        P("slab", "blk", None),
        P("slab", "blk", None),
    )
    return jax.shard_map(
        on_device,
        mesh=mesh,
        in_specs=placed,
        out_specs=(
            P("slab", "blk", None, None),
            P("slab", "blk", None, None, None),
            P("slab", "blk", None, None),
        ),
        check_vma=False,
    )
```

```python
import jax
import jax.numpy as jnp
from jax import lax
from jax.experimental import pallas as pl
from jax.experimental.pallas import tpu as pltpu
from jax.sharding import PartitionSpec as P

EDGE = 16
DEPTH = 256
SWEEPS = 4
N_SLAB = 32
N_BLK = 4
P_DEV = 16
ROWS = N_SLAB * P_DEV
MESH = pl.DeviceIdType.MESH
F32 = jnp.float32
I32 = jnp.int32
BF16 = jnp.bfloat16

PLASTIC_LOW = 0.2235
PLASTIC_STEPS = 65535.0 / (1.4145 - PLASTIC_LOW)

OFFSETS = [
    (dx, dy, dz)
    for dx in (-1, 0, 1)
    for dy in (-1, 0, 1)
    for dz in (-1, 0, 1)
    if (dx, dy, dz) != (0, 0, 0)
]
WEIGHTS = [0.0, 0.1, 0.04, 0.02]


def plane_number(dy, dz):
    return (dy + 1) * 3 + dz + 1


def lane_of(shape):
    return lax.broadcasted_iota(I32, shape, 1)


def row_of(shape):
    return lax.broadcasted_iota(I32, shape, 0)


def shifted_pairs(three, row8):
    out = [None] * 9
    for dz, (a, b) in zip((-1, 0, 1), three):
        a_down, b_down = pltpu.roll(a, 1, 0), pltpu.roll(b, 1, 0)
        a_up, b_up = pltpu.roll(a, 7, 0), pltpu.roll(b, 7, 0)
        out[plane_number(-1, dz)] = (a_down, jnp.where(row8 == 0, a_down, b_down))
        out[plane_number(0, dz)] = (a, b)
        out[plane_number(1, dz)] = (jnp.where(row8 == 7, b_up, a_up), b_up)
    return out


def swap_rows_and_groups(tiles, group, first, second):
    for k in range(8):
        first[8 * k : 8 * k + 8, :] = tiles[k]
    parts = [first[pl.ds(k, 8, stride=8), :] for k in range(8)]
    for bit in (4, 2, 1):
        low_group = (group & bit) == 0
        for k in range(8):
            if k & bit == 0:
                low, high = parts[k], parts[k | bit]
                parts[k] = jnp.where(low_group, low, pltpu.roll(high, 16 * bit, 1))
                parts[k | bit] = jnp.where(low_group, pltpu.roll(low, 128 - 16 * bit, 1), high)
    for k in range(8):
        second[8 * k : 8 * k + 8, :] = parts[k]
    return [second[pl.ds(k, 8, stride=8), :] for k in range(8)]


def byte_of(words, number):
    part = words if number == 0 else lax.shift_right_logical(words, 8 * number)
    return (part & 255).astype(F32).astype(BF16)


def joined(low, high):
    return (low + 256.0 * high).astype(I32)


def move_kernel(
    thermal, deform, modulus, plastic_in, flag, holder, position,
    out_words, out_plastic, out_exponents,
    plastic, state, halo_y, stage_y, cond, cond_y, cond_stage,
    face_x, face_ym, face_yp, face_zm, face_zp, centre,
    stiff, turned, stepped, coded, weights, tile, inverse, values,
    send_one, recv_one, send_two, plastic_one, plastic_got, plastic_two,
    one_hot, table, plastic_table, swap_a, swap_b,
    load_sem, x_send, x_recv, y_send, y_recv,
    one_send, one_recv, two_send, two_recv, pl_one_send, pl_one_recv, pl_two_send, pl_two_recv, own_sem,
):
    s = lax.axis_index("slab")
    b = lax.axis_index("blk")
    chip = s // 2
    up, down = lax.rem(s + 1, N_SLAB), lax.rem(s + N_SLAB - 1, N_SLAB)
    right, left = lax.rem(b + 1, N_BLK), lax.rem(b + N_BLK - 1, N_BLK)
    has_up, has_down = s < N_SLAB - 1, s > 0
    has_right, has_left = b < N_BLK - 1, b > 0

    barrier = pltpu.get_barrier_semaphore()

    for step in range(1, N_SLAB):
        peer = lax.rem(s + step, N_SLAB)
        pl.semaphore_signal(barrier, inc=1, device_id=(peer, b), device_id_type=MESH)

    @pl.when(has_right)
    def _():
        pl.semaphore_signal(barrier, inc=1, device_id=(s, right), device_id_type=MESH)

    @pl.when(has_left)
    def _():
        pl.semaphore_signal(barrier, inc=1, device_id=(s, left), device_id_type=MESH)

    loads = [
        pltpu.make_async_copy(thermal, state.at[0, 0, pl.ds(1, EDGE)], load_sem.at[0]),
        pltpu.make_async_copy(deform, state.at[0, pl.ds(1, 3), pl.ds(1, EDGE)], load_sem.at[1]),
        pltpu.make_async_copy(modulus, cond.at[pl.ds(1, EDGE)], load_sem.at[2]),
        pltpu.make_async_copy(plastic_in, plastic, load_sem.at[3]),
    ]
    for load in loads:
        load.start()

    zero_plane = jnp.zeros((EDGE, DEPTH), F32)

    for has, place, side in ((has_down, 0, 0), (has_up, EDGE + 1, 1)):

        @pl.when(jnp.logical_not(has))
        def _():
            cond[place] = zero_plane
            for t in range(SWEEPS):
                for f in range(4):
                    state[t, f, place] = zero_plane

    for has, side in ((has_left, 0), (has_right, 1)):

        @pl.when(jnp.logical_not(has))
        def _():
            cond_y[side] = zero_plane
            for t in range(SWEEPS):
                for f in range(4):
                    halo_y[t, side, f] = zero_plane

    neighbours = 31 + has_right.astype(I32) + has_left.astype(I32)
    pl.semaphore_wait(barrier, neighbours)

    def x_copies(kind):
        out = []
        for direction, peer in ((0, down), (1, up)):
            mine = 0 if direction == 0 else EDGE - 1
            there = EDGE + 1 if direction == 0 else 0
            if kind == 0:
                source, target = thermal.at[mine], state.at[0, 0, there]
            elif kind == 4:
                source, target = deform.at[:, mine], state.at[0, pl.ds(1, 3), there]
            elif kind == 5:
                source, target = modulus.at[mine], cond.at[there]
            else:
                source, target = state.at[kind, :, mine + 1], state.at[kind, :, there]
            out.append(
                pltpu.make_async_remote_copy(
                    source, target, x_send.at[kind, direction], x_recv.at[kind, direction],
                    device_id=(peer, b), device_id_type=MESH,
                )
            )
        return out

    def y_copies(kind):
        out = []
        for direction, peer in ((0, left), (1, right)):
            if kind == 4:
                source, target = cond_stage.at[direction], cond_y.at[1 - direction]
            elif kind == 0:
                source, target = stage_y.at[0, direction], halo_y.at[0, 1 - direction]
            else:
                part = pl.ds(8 * (kind // 4), 8)
                source = stage_y.at[kind % 4, direction, :, part]
                target = halo_y.at[kind % 4, 1 - direction, :, part]
            out.append(
                pltpu.make_async_remote_copy(
                    source, target, y_send.at[kind, direction], y_recv.at[kind, direction],
                    device_id=(s, peer), device_id_type=MESH,
                )
            )
        return out

    def start(copies, to_low, to_high):
        @pl.when(to_low)
        def _():
            copies[0].start()

        @pl.when(to_high)
        def _():
            copies[1].start()

    def wait_recv(copies, from_high, from_low):
        @pl.when(from_high)
        def _():
            copies[0].wait_recv()

        @pl.when(from_low)
        def _():
            copies[1].wait_recv()

    def four_at_a_time(work):
        def step(k, carry):
            for j in range(4):
                work(4 * k + j)
            return carry

        lax.fori_loop(0, EDGE // 4, step, 0)

    def wait_send(copies, to_low, to_high):
        @pl.when(to_low)
        def _():
            copies[0].wait_send()

        @pl.when(to_high)
        def _():
            copies[1].wait_send()

    for kind in (5, 0, 4):
        start(x_copies(kind), has_down, has_up)
    for load in loads:
        load.wait()

    def stage_first(x, carry):
        for side, y in ((0, 0), (1, EDGE - 1)):
            cond_stage[side, pl.ds(x, 1), :] = cond[x + 1, y : y + 1, :]
            for f in range(4):
                stage_y[0, side, f, pl.ds(x, 1), :] = state[0, f, x + 1, y : y + 1, :]
        return carry

    lax.fori_loop(0, EDGE, stage_first, 0)
    start(y_copies(4), has_left, has_right)
    start(y_copies(0), has_left, has_right)

    row8 = row_of((8, 128))
    group8 = lane_of((8, 128)) // EDGE
    row = row_of((EDGE, DEPTH))
    lane = lane_of((EDGE, DEPTH))
    inner = lane & (EDGE - 1)

    slot_lane = lane_of((1, 128))
    slot_row = jnp.zeros((1, 128), I32)
    for p in range(P_DEV):
        code = holder[0, 0, p] * P_DEV + position[0, 0, p]
        slot_row = jnp.where(slot_lane == lax.rem(s, 8) * P_DEV + p, code, slot_row)

    sibling = lax.bitwise_xor(s, 1)

    def send_plastic(m):
        pltpu.make_async_remote_copy(
            plastic_one.at[m, pl.ds(0, 9)], plastic_got.at[s, pl.ds(0, 9)], pl_one_send, pl_one_recv,
            device_id=(m, b), device_id_type=MESH,
        ).start()

    def plastic_planes(planes):
        tiles = []
        for x in planes:
            root = plastic[x]
            root = root * lax.rsqrt(root)
            codes = jnp.clip((root - PLASTIC_LOW) * PLASTIC_STEPS + 0.5, 0.0, 65535.0).astype(I32)
            words = (codes[:, 0:128] << 16) | codes[:, 128:256]
            tiles += [words[0:8], words[8:16]]
        tiles = swap_rows_and_groups(tiles, group8, swap_a, swap_b)
        for k in range(8):
            m = 2 * planes[k // 2] + k % 2
            plastic_one[m, 0:8, :] = tiles[k]
            plastic_one[m, 8:9, :] = slot_row

    def plastic_out(step, carry):
        planes = [lax.rem(chip + 4 * step + j, EDGE) for j in range(4)]
        plastic_planes(planes)
        for x in planes:
            send_plastic(2 * x)
            send_plastic(2 * x + 1)
        return carry

    planes = [lax.rem(chip + j, EDGE) for j in range(4)]
    plastic_planes(planes)
    send_plastic(sibling)
    plastic_got[s, 0:9, :] = plastic_one[s, 0:9, :]
    for x in planes[1:]:
        send_plastic(2 * x)
        send_plastic(2 * x + 1)
    lax.fori_loop(1, 4, plastic_out, 0)

    for dy in (-1, 0, 1):
        for dz in (-1, 0, 1):
            inside = (row + dy >= 0) & (row + dy < EDGE) & (inner + dz >= 0) & (inner + dz < EDGE)
            reach = abs(dy) + abs(dz)
            weights[0, plane_number(dy, dz)] = jnp.where(inside, 0.5 * WEIGHTS[reach], 0.0)
            weights[1, plane_number(dy, dz)] = jnp.where(inside, 0.5 * WEIGHTS[reach + 1], 0.0)
    for n in range(9):
        for f in range(4):
            values[f, n, 0] = zero_plane
            values[f, n, EDGE + 1] = zero_plane
    for number, (dx, dy, dz) in enumerate(OFFSETS):
        if dx != 0:
            tile[number, 1 if dx < 0 else EDGE] = zero_plane

    factor = jnp.ones((1, DEPTH), F32)
    lane_row = lane_of((1, DEPTH)) // EDGE
    for p in range(P_DEV):
        factor = jnp.where(lane_row == p, 1.0 + 3.0 * flag[0, 0, p].astype(F32), factor)

    wait_recv(x_copies(5), has_up, has_down)
    wait_recv(y_copies(4), has_right, has_left)

    def face(x):
        here = cond[x + 1]
        ym = jnp.where(row == 0, cond_y[0, pl.ds(x, 1), :], pltpu.roll(here, 1, 0))
        yp = jnp.where(row == EDGE - 1, cond_y[1, pl.ds(x, 1), :], pltpu.roll(here, EDGE - 1, 0))
        zm = jnp.where(lane == 0, 0.0, pltpu.roll(here, 1, 1))
        zp = jnp.where(lane == DEPTH - 1, 0.0, pltpu.roll(here, DEPTH - 1, 1))
        low = 0.06 * (cond[x] + here)
        high = 0.06 * (here + cond[x + 2])
        face_x[x] = low
        face_x[x + 1] = high
        ym, yp, zm, zp = (0.06 * (here + beside) for beside in (ym, yp, zm, zp))
        face_ym[x] = ym
        face_yp[x] = yp
        face_zm[x] = zm
        face_zp[x] = zp
        centre[x] = 1.0 - (low + high + ym + yp + zm + zp)

    four_at_a_time(face)

    def sweep_plane(t, x):
        around = []
        for f in range(4):
            here = state[t, f, x + 1]
            around.append(
                (
                    here,
                    state[t, f, x],
                    state[t, f, x + 2],
                    jnp.where(row == 0, halo_y[t, 0, f, pl.ds(x, 1), :], pltpu.roll(here, 1, 0)),
                    jnp.where(row == EDGE - 1, halo_y[t, 1, f, pl.ds(x, 1), :], pltpu.roll(here, EDGE - 1, 0)),
                    jnp.where(lane == 0, 0.0, pltpu.roll(here, 1, 1)),
                    jnp.where(lane == DEPTH - 1, 0.0, pltpu.roll(here, DEPTH - 1, 1)),
                )
            )
        h, xm, xp, ym, yp, zm, zp = around[0]
        fresh = [
            centre[x] * h
            + face_x[x] * xm
            + face_x[x + 1] * xp
            + face_ym[x] * ym
            + face_yp[x] * yp
            + face_zm[x] * zm
            + face_zp[x] * zp
        ]
        slopes = (xp - xm, yp - ym, zp - zm)
        for c in range(3):
            u, *six = around[c + 1]
            total = (six[0] + six[1]) + (six[2] + six[3]) + (six[4] + six[5])
            fresh.append(0.28 * u + 0.12 * total - 0.06 * slopes[c])
        for f in range(4):
            state[t + 1, f, x + 1] = fresh[f]
            if t + 1 < SWEEPS:
                stage_y[t + 1, 0, f, pl.ds(x, 1), :] = fresh[f][0:1]
                stage_y[t + 1, 1, f, pl.ds(x, 1), :] = fresh[f][EDGE - 1 : EDGE]

    def sweep(t):
        def four(first):
            for x in range(first, first + 4):
                sweep_plane(t, x)

        onward_x = x_copies(t + 1) if t + 1 < SWEEPS else None
        if t > 0:
            arrived = x_copies(t)

            @pl.when(has_down)
            def _():
                arrived[1].wait_recv()

            wait_recv(y_copies(t), has_right, has_left)
        four(0)
        if onward_x:

            @pl.when(has_down)
            def _():
                onward_x[0].start()

        four(4)
        if onward_x:
            start(y_copies(t + 1), has_left, has_right)
        if t > 0:

            @pl.when(has_up)
            def _():
                arrived[0].wait_recv()

            wait_recv(y_copies(t + 4), has_right, has_left)
        four(12)
        if onward_x:

            @pl.when(has_up)
            def _():
                onward_x[1].start()

        four(8)
        if onward_x:
            start(y_copies(t + 5), has_left, has_right)

    wait_recv(x_copies(0), has_up, has_down)
    wait_recv(x_copies(4), has_up, has_down)
    wait_recv(y_copies(0), has_right, has_left)
    sweep(0)

    def wait_all(ref, semaphore):
        pltpu.make_async_copy(ref, ref, semaphore).wait()

    wait_all(plastic_got.at[pl.ds(0, N_SLAB - 1), pl.ds(0, 9)], pl_one_recv)
    slot_id = row_of((ROWS, 128))
    for g in range(4):
        codes = plastic_got[8 * g, 8:9, :]
        for k in range(1, 8):
            codes = codes + plastic_got[8 * g + k, 8:9, :]
        one_hot[:, 128 * g : 128 * g + 128] = jnp.where(slot_id == codes, 1.0, 0.0).astype(BF16)

    def plastic_unpack(g, carry):
        words = plastic_got[pl.ds(4 * g, 4), 0:8, :]
        both = jnp.concatenate([lax.shift_right_logical(words, 16), words & 65535], axis=1).reshape(64, 128)
        place = pl.ds(pl.multiple_of(64 * g, 64), 64)
        plastic_table[place, 0:128] = byte_of(both, 0)
        plastic_table[place, 128:256] = byte_of(both, 1)
        return carry

    lax.fori_loop(0, 8, plastic_unpack, 0)

    def plastic_group(g):
        place = pl.ds(pl.multiple_of(128 * g, 128), 128)
        rows = jnp.dot(one_hot[place, :], plastic_table[...], preferred_element_type=F32)
        codes = joined(rows[:, 0:128], rows[:, 128:256]).reshape(8, P_DEV, 128)
        plastic_two[pl.ds(8 * g, 8)] = (codes[:, 0:8] << 16) | codes[:, 8:16]

    def pass_plastic(d):
        pltpu.make_async_remote_copy(
            plastic_two.at[d], out_plastic.at[s], pl_two_send, pl_two_recv,
            device_id=(d, b), device_id_type=MESH,
        ).start()

    def plastic_on(step):
        g = lax.rem(step + s // 8, 4)
        plastic_group(g)
        for k in range(8):
            pass_plastic(8 * g + lax.rem(s + k, 8))

    plastic_group(s // 8)
    pltpu.make_async_copy(plastic_two.at[s], out_plastic.at[s], own_sem.at[0]).start()
    for k in range(1, 8):
        pass_plastic(8 * (s // 8) + lax.rem(s + k, 8))

    sweep(1)
    plastic_on(1)
    sweep(2)
    plastic_on(2)
    sweep(3)

    def beside(plane):
        parts = [plane[:, 0:128], plane[:, 128:256]]
        return [jnp.concatenate([pltpu.roll(part, turn, 1) for part in parts], axis=1) for turn in (1, 127)]

    def prepare(k, most):
        most = list(most)
        for j in range(4):
            x = 4 * k + j
            fields = [state[SWEEPS, f, x + 1] for f in range(4)]
            squared = fields[0] * fields[0]
            stiffness = cond[x + 1] * (1.0 + 0.5 * squared / (1.0 + squared)) / (1.0 + plastic[x]) * factor
            stiff[x + 1] = stiffness
            for f, plane in enumerate([stiffness] + fields):
                turned[f, 0, x], turned[f, 1, x] = beside(plane)
            most = [jnp.maximum(most[f], jnp.abs(fields[f])) for f in range(4)]
        return tuple(most)

    most = lax.fori_loop(0, EDGE // 4, prepare, (zero_plane,) * 4)
    exponents = []
    exponent_row = jnp.zeros((1, 128), I32)
    scales = []
    for f in range(4):
        largest = jnp.max(jnp.max(most[f], axis=0, keepdims=True), axis=1, keepdims=True)
        exponent = jnp.ceil(jnp.log2(jnp.maximum(largest, 1e-30)) + 0.001)
        scales.append(jnp.exp2(-exponent))
        exponent_row = jnp.where(slot_lane == f, exponent.astype(I32), exponent_row)

    numbers = {offset: number for number, offset in enumerate(OFFSETS)}
    halves = (slice(0, 8), slice(8, 16))
    ones = (jnp.ones((8, 128), F32),) * 2

    def built(x, done, active, side):
        lanes = slice(128 * side, 128 * side + 128)
        begun = [ones] + [tuple(state[SWEEPS, f, x + 2, rows, lanes] for rows in halves) for f in range(4)]
        totals = {1: list(done), 0: list(active), -1: begun}
        own = {dx: [stiff[x + 1 - dx, rows, lanes] for rows in halves] for dx in (-1, 0, 1)}
        centres = [own[0]] + [[state[SWEEPS, f, x + 1, rows, lanes] for rows in halves] for f in range(4)]
        near, *fields = [
            shifted_pairs(
                (
                    [turned[f, 0, x, rows, lanes] for rows in halves],
                    centres[f],
                    [turned[f, 1, x, rows, lanes] for rows in halves],
                ),
                row8,
            )
            for f in range(5)
        ]
        for dz in (-1, 0, 1):
            for dy in (-1, 0, 1):
                n = plane_number(dy, dz)
                for dx in (-1, 0, 1):
                    if (dx, dy, dz) == (0, 0, 0):
                        continue
                    number = numbers[dx, dy, dz]
                    entries = []
                    for j, rows in enumerate(halves):
                        entry = weights[abs(dx), n, rows, 0:128] * (own[dx][j] + near[n][j])
                        entry = entry.astype(BF16).astype(F32)
                        tile[number, x + 1 - dx, rows, lanes] = entry
                        entries.append(entry)
                    total = totals[dx]
                    total[0] = tuple(total[0][j] + entries[j] for j in range(2))
                    for f in range(4):
                        total[f + 1] = tuple(total[f + 1][j] + entries[j] * fields[f][n][j] for j in range(2))
        return tuple(totals[1]), tuple(totals[0]), tuple(totals[-1])

    def finish(place, done, side):
        lanes = slice(128 * side, 128 * side + 128)
        scale = [1.0 / part for part in done[0]]
        for j, rows in enumerate(halves):
            inverse[place, rows, lanes] = scale[j]
        for f in range(4):
            for j, rows in enumerate(halves):
                stepped[f, place, rows, lanes] = done[f + 1][j] * scale[j]

    for side in range(2):

        def source(k, carry):
            for j in range(2):
                done, *carry = built(2 * k + j, *carry, side)
                finish(2 * k + j, done, side)
            return tuple(carry)

        lanes = slice(128 * side, 128 * side + 128)
        start_at = (ones,) + tuple(tuple(state[SWEEPS, f, 1, rows, lanes] for rows in halves) for f in range(4))
        last, _ = lax.fori_loop(0, EDGE // 2, source, ((ones,) * 5, start_at))
        finish(EDGE, last, side)

    def spread(k, carry):
        for j in range(2):
            x = 2 * k + j
            for f in range(4):
                plane = stepped[f, x + 1]
                minus, plus = beside(plane)
                for side in range(2):
                    lanes = slice(128 * side, 128 * side + 128)
                    three = [[part[rows, lanes] for rows in halves] for part in (minus, plane, plus)]
                    for n, pair in enumerate(shifted_pairs(three, row8)):
                        for i, rows in enumerate(halves):
                            values[f, n, x + 1, rows, lanes] = pair[i]
        return carry

    lax.fori_loop(0, EDGE // 2, spread, 0)

    def smoothed(x):
        totals = [state[SWEEPS, f, x + 1] for f in range(4)]
        for number, (dx, dy, dz) in enumerate(OFFSETS):
            entry = tile[number, x + 1]
            for f in range(4):
                totals[f] = totals[f] + entry * values[f, plane_number(dy, dz), x + 1 + dx]
        scale = inverse[x + 1]
        return [total * scale for total in totals]

    def send_plane(m):
        pltpu.make_async_remote_copy(
            send_one.at[m, pl.ds(0, 33)], recv_one.at[s, pl.ds(0, 33)], one_send, one_recv,
            device_id=(m, b), device_id_type=MESH,
        ).start()

    def encode_plane(x, slot):
        codes = []
        for f, field in enumerate(smoothed(x)):
            part = jnp.abs(field) * scales[f]
            part = jnp.minimum(part * lax.rsqrt(part + 1e-37), 1.0) * 32767.0
            codes.append((jnp.where(field < 0.0, -part, part) + 32768.5).astype(I32))
        coded[slot, 0] = (codes[0] << 16) | codes[1]
        coded[slot, 1] = (codes[2] << 16) | codes[3]

    def turn_plane(x, slot):
        tiles = [
            coded[slot, w, 8 * half : 8 * half + 8, 128 * side : 128 * side + 128]
            for half in range(2)
            for w in range(2)
            for side in range(2)
        ]
        tiles = swap_rows_and_groups(tiles, group8, swap_a, swap_b)
        for half in range(2):
            m = 2 * x + half
            for k in range(4):
                send_one[m, 8 * k : 8 * k + 8, :] = tiles[4 * half + k]
            send_one[m, 32:33, :] = exponent_row

    def second(step, carry):
        x, later = lax.rem(step + chip, EDGE), lax.rem(step + 1 + chip, EDGE)
        slot = lax.rem(step, 2)
        turn_plane(x, slot)
        encode_plane(later, 1 - slot)
        send_plane(2 * x)
        send_plane(2 * x + 1)
        return carry

    encode_plane(chip, 0)
    turn_plane(chip, 0)
    send_plane(sibling)
    recv_one[s, 0:33, :] = send_one[s, 0:33, :]
    encode_plane(lax.rem(chip + 1, EDGE), 1)
    lax.fori_loop(1, EDGE - 1, second, 0)
    turn_plane(lax.rem(chip + EDGE - 1, EDGE), 1)
    send_plane(2 * lax.rem(chip + EDGE - 1, EDGE))
    send_plane(2 * lax.rem(chip + EDGE - 1, EDGE) + 1)
    plastic_on(3)
    wait_all(recv_one.at[pl.ds(0, N_SLAB - 1), pl.ds(0, 33)], one_recv)

    def unpack(g, carry):
        place = pl.ds(pl.multiple_of(64 * g, 64), 64)
        for w in range(2):
            words = recv_one[pl.ds(4 * g, 4), 16 * w : 16 * w + 16, :].reshape(64, 128)
            for number in range(4):
                at = 128 * (4 * w + number)
                table[place, at : at + 128] = byte_of(words, number)
        return carry

    lax.fori_loop(0, 8, unpack, 0)

    def onward_group(g):
        place = pl.ds(pl.multiple_of(256 * g, 256), 256)
        rows = jnp.dot(one_hot[place, :], table[...], preferred_element_type=F32)
        for w in range(2):
            parts = [rows[:, 128 * (4 * w + n) : 128 * (4 * w + n) + 128] for n in range(4)]
            words = joined(parts[0], parts[1]) | (joined(parts[2], parts[3]) << 16)
            send_two[pl.ds(16 * g, 16), 16 * w : 16 * w + 16, :] = words.reshape(16, P_DEV, 128)

    def pass_on(d):
        pltpu.make_async_remote_copy(
            send_two.at[d], out_words.at[s], two_send, two_recv,
            device_id=(d, b), device_id_type=MESH,
        ).start()

    for step in range(2):
        g = lax.bitwise_xor(step, s // 16)
        onward_group(g)
        if step == 0:
            pltpu.make_async_copy(send_two.at[s], out_words.at[s], own_sem.at[1]).start()
        for k in range(1 - step, 16):
            pass_on(16 * g + lax.rem(s + k, 16))

    sources = jnp.concatenate(
        [jnp.broadcast_to(recv_one[k, 32:33, :].astype(F32), (P_DEV, 128)) for k in range(N_SLAB)], axis=0
    ).astype(BF16)
    mine = one_hot[pl.ds(pl.multiple_of(s * P_DEV, P_DEV), P_DEV), :]
    out_exponents[...] = jnp.dot(mine, sources, preferred_element_type=F32)

    for kind in (0, 1, 2, 3, 4, 5):
        wait_send(x_copies(kind), has_down, has_up)
    for kind in range(8):
        wait_send(y_copies(kind), has_left, has_right)
    wait_all(plastic_one.at[pl.ds(0, N_SLAB - 1), pl.ds(0, 9)], pl_one_send)
    wait_all(send_one.at[pl.ds(0, N_SLAB - 1), pl.ds(0, 33)], one_send)
    wait_all(plastic_two.at[pl.ds(0, N_SLAB - 1)], pl_two_send)
    wait_all(send_two.at[pl.ds(0, N_SLAB - 1)], two_send)
    pltpu.make_async_copy(plastic_two.at[s], out_plastic.at[s], own_sem.at[0]).wait()
    pltpu.make_async_copy(send_two.at[s], out_words.at[s], own_sem.at[1]).wait()
    wait_all(out_plastic.at[pl.ds(0, N_SLAB - 1)], pl_two_recv)
    wait_all(out_words.at[pl.ds(0, N_SLAB - 1)], two_recv)


def move(thermal, deform, modulus, plastic, flag, holder, position):
    anywhere = pl.BlockSpec(memory_space=pl.ANY)
    vmem = pl.BlockSpec(memory_space=pltpu.VMEM)
    smem = pl.BlockSpec(memory_space=pltpu.SMEM)
    plane = (EDGE, DEPTH)
    dma = pltpu.SemaphoreType.DMA
    return pl.pallas_call(
        move_kernel,
        name="sweep_solve_move",
        out_shape=(
            jax.ShapeDtypeStruct((N_SLAB, 32, 128), I32),
            jax.ShapeDtypeStruct((N_SLAB, 8, 128), I32),
            jax.ShapeDtypeStruct((P_DEV, 128), F32),
        ),
        in_specs=[anywhere] * 4 + [smem] * 3,
        out_specs=(anywhere, anywhere, vmem),
        scratch_shapes=[
            pltpu.VMEM((EDGE,) + plane, F32),
            pltpu.VMEM((SWEEPS + 1, 4, EDGE + 2) + plane, F32),
            pltpu.VMEM((SWEEPS, 2, 4) + plane, F32),
            pltpu.VMEM((SWEEPS, 2, 4) + plane, F32),
            pltpu.VMEM((EDGE + 2,) + plane, F32),
            pltpu.VMEM((2,) + plane, F32),
            pltpu.VMEM((2,) + plane, F32),
            pltpu.VMEM((EDGE + 1,) + plane, F32),
            pltpu.VMEM((EDGE,) + plane, F32),
            pltpu.VMEM((EDGE,) + plane, F32),
            pltpu.VMEM((EDGE,) + plane, F32),
            pltpu.VMEM((EDGE,) + plane, F32),
            pltpu.VMEM((EDGE,) + plane, F32),
            pltpu.VMEM((EDGE + 2,) + plane, F32),
            pltpu.VMEM((5, 2, EDGE) + plane, F32),
            pltpu.VMEM((4, EDGE + 1) + plane, F32),
            pltpu.VMEM((2, 2) + plane, I32),
            pltpu.VMEM((2, 9) + plane, F32),
            pltpu.VMEM((26, EDGE + 2) + plane, F32),
            pltpu.VMEM((EDGE + 1,) + plane, F32),
            pltpu.VMEM((4, 9, EDGE + 2) + plane, F32),
            pltpu.VMEM((N_SLAB, 40, 128), I32),
            pltpu.VMEM((N_SLAB, 40, 128), I32),
            pltpu.VMEM((N_SLAB, 32, 128), I32),
            pltpu.VMEM((N_SLAB, 16, 128), I32),
            pltpu.VMEM((N_SLAB, 16, 128), I32),
            pltpu.VMEM((N_SLAB, 8, 128), I32),
            pltpu.VMEM((ROWS, ROWS), BF16),
            pltpu.VMEM((ROWS, 1024), BF16),
            pltpu.VMEM((ROWS, 256), BF16),
            pltpu.VMEM((64, 128), I32),
            pltpu.VMEM((64, 128), I32),
            dma((4,)),
            dma((6, 2)),
            dma((6, 2)),
            dma((8, 2)),
            dma((8, 2)),
            dma(()),
            dma(()),
            dma(()),
            dma(()),
            dma(()),
            dma(()),
            dma(()),
            dma(()),
            dma((2,)),
        ],
        compiler_params=pltpu.CompilerParams(
            collective_id=0, has_side_effects=True, vmem_limit_bytes=56 * 1024 * 1024
        ),
    )(thermal, deform, modulus, plastic, flag, holder, position)


def decode_kernel(
    words_in, plastic_in, exponents, heat_out, moved_out, plastic_out, words, strain, heat, moved, straight, got, put
):
    pieces = N_SLAB // 4
    fetch = [
        pltpu.make_async_copy(words_in.at[pl.ds(pieces * k, pieces)], words.at[pl.ds(pieces * k, pieces)], got.at[k])
        for k in range(4)
    ]
    fetch.append(pltpu.make_async_copy(plastic_in, strain, got.at[4]))
    for copy in fetch:
        copy.start()
    scales = [
        jnp.broadcast_to(jnp.exp2(exponents[:, f : f + 1]) * (1.0 / (32767.0 * 32767.0)), (P_DEV, 128))
        for f in range(4)
    ]
    length = 128 * pieces
    writes = []
    for k in range(4):
        fetch[k].wait()
        for m in range(pieces * k, pieces * k + pieces):
            at = slice(128 * m, 128 * m + 128)
            for w in range(2):
                word = words[m, 16 * w : 16 * w + 16, :]
                for part in range(2):
                    code = lax.shift_right_logical(word, 16) if part == 0 else word & 65535
                    root = (code - 32768).astype(F32)
                    field = root * jnp.abs(root) * scales[2 * w + part]
                    if w == 0 and part == 0:
                        heat[:, at] = field
                    else:
                        moved[2 * w + part - 1, :, at] = field
        at = pl.ds(length * k, length)
        writes.append(pltpu.make_async_copy(heat.at[:, at], heat_out.at[0, 0, :, at], put.at[3 * k]))
        writes.append(pltpu.make_async_copy(moved.at[:, :, at], moved_out.at[0, 0, :, :, at], put.at[3 * k + 1]))
        for copy in writes[-2:]:
            copy.start()
        if k == 0:
            fetch[4].wait()
        for m in range(pieces * k, pieces * k + pieces):
            word = strain[m]
            for part in range(2):
                code = lax.shift_right_logical(word, 16) if part == 0 else word & 65535
                root = code.astype(F32) * (1.0 / PLASTIC_STEPS) + PLASTIC_LOW
                straight[8 * part : 8 * part + 8, 128 * m : 128 * m + 128] = root * root
        writes.append(pltpu.make_async_copy(straight.at[:, at], plastic_out.at[0, 0, :, at], put.at[3 * k + 2]))
        writes[-1].start()
    for copy in writes:
        copy.wait()


def decode(words, plastic, exponents):
    vmem = pl.BlockSpec(memory_space=pltpu.VMEM)
    anywhere = pl.BlockSpec(memory_space=pl.ANY)
    length = EDGE**3
    heat, moved, strain = pl.pallas_call(
        decode_kernel,
        name="decode",
        out_shape=(
            jax.ShapeDtypeStruct((1, 1, P_DEV, length), F32),
            jax.ShapeDtypeStruct((1, 1, 3, P_DEV, length), F32),
            jax.ShapeDtypeStruct((1, 1, P_DEV, length), F32),
        ),
        in_specs=[anywhere, anywhere, vmem],
        out_specs=(anywhere,) * 3,
        scratch_shapes=[
            pltpu.VMEM((N_SLAB, 32, 128), I32),
            pltpu.VMEM((N_SLAB, 8, 128), I32),
            pltpu.VMEM((P_DEV, length), F32),
            pltpu.VMEM((3, P_DEV, length), F32),
            pltpu.VMEM((P_DEV, length), F32),
            pltpu.SemaphoreType.DMA((5,)),
            pltpu.SemaphoreType.DMA((12,)),
        ],
        compiler_params=pltpu.CompilerParams(vmem_limit_bytes=56 * 1024 * 1024),
    )(words, plastic, exponents)
    return heat, moved.transpose(0, 1, 3, 2, 4), strain


def on_device(thermal, deform, modulus, plastic, flag, holder, position):
    return decode(*move(thermal, deform, modulus, plastic, flag, holder, position))


def solution(mesh):
    placed = (
        P("slab", "blk", None),
        P(None, "slab", "blk", None),
        P("slab", "blk", None),
        P("slab", "blk", None),
        P("slab", "blk", None),
        P("slab", "blk", None),
        P("slab", "blk", None),
    )
    return jax.shard_map(
        on_device,
        mesh=mesh,
        in_specs=placed,
        out_specs=(
            P("slab", "blk", None, None),
            P("slab", "blk", None, None, None),
            P("slab", "blk", None, None),
        ),
        check_vma=False,
    )
```

```python
import jax
import jax.numpy as jnp
from jax import lax
from jax.experimental import pallas as pl
from jax.experimental.pallas import tpu as pltpu
from jax.sharding import PartitionSpec as P

EDGE = 16
DEPTH = 256
SWEEPS = 4
N_SLAB = 32
N_BLK = 4
P_DEV = 16
ROWS = N_SLAB * P_DEV
MESH = pl.DeviceIdType.MESH
F32 = jnp.float32
I32 = jnp.int32
BF16 = jnp.bfloat16

PLASTIC_LOW = 0.2235
PLASTIC_STEPS = 65535.0 / (1.4145 - PLASTIC_LOW)

OFFSETS = [
    (dx, dy, dz)
    for dx in (-1, 0, 1)
    for dy in (-1, 0, 1)
    for dz in (-1, 0, 1)
    if (dx, dy, dz) != (0, 0, 0)
]
WEIGHTS = [0.0, 0.1, 0.04, 0.02]


def plane_number(dy, dz):
    return (dy + 1) * 3 + dz + 1


def lane_of(shape):
    return lax.broadcasted_iota(I32, shape, 1)


def row_of(shape):
    return lax.broadcasted_iota(I32, shape, 0)


def shifted_pairs(three, row8):
    out = [None] * 9
    for dz, (a, b) in zip((-1, 0, 1), three):
        a_down, b_down = pltpu.roll(a, 1, 0), pltpu.roll(b, 1, 0)
        a_up, b_up = pltpu.roll(a, 7, 0), pltpu.roll(b, 7, 0)
        out[plane_number(-1, dz)] = (a_down, jnp.where(row8 == 0, a_down, b_down))
        out[plane_number(0, dz)] = (a, b)
        out[plane_number(1, dz)] = (jnp.where(row8 == 7, b_up, a_up), b_up)
    return out


def swap_rows_and_groups(tiles, group, first, second):
    for k in range(8):
        first[8 * k : 8 * k + 8, :] = tiles[k]
    parts = [first[pl.ds(k, 8, stride=8), :] for k in range(8)]
    for bit in (4, 2, 1):
        low_group = (group & bit) == 0
        for k in range(8):
            if k & bit == 0:
                low, high = parts[k], parts[k | bit]
                parts[k] = jnp.where(low_group, low, pltpu.roll(high, 16 * bit, 1))
                parts[k | bit] = jnp.where(low_group, pltpu.roll(low, 128 - 16 * bit, 1), high)
    for k in range(8):
        second[8 * k : 8 * k + 8, :] = parts[k]
    return [second[pl.ds(k, 8, stride=8), :] for k in range(8)]


def byte_of(words, number):
    part = words if number == 0 else lax.shift_right_logical(words, 8 * number)
    return (part & 255).astype(F32).astype(BF16)


def joined(low, high):
    return (low + 256.0 * high).astype(I32)


def move_kernel(
    thermal, deform, modulus, plastic_in, flag, holder, position,
    out_words, out_exponents,
    plastic, state, halo_y, stage_y, cond, cond_y, cond_stage,
    face_x, face_ym, face_yp, face_zm, face_zp, centre,
    stiff, turned, stepped, coded, weights, tile, inverse, values,
    send_one, recv_one, send_two, plastic_one, plastic_got,
    one_hot, table, plastic_table, swap_a, swap_b, exponents_here,
    load_sem, x_send, x_recv, y_send, y_recv,
    one_send, one_recv, two_send, two_recv, pl_one_send, pl_one_recv, own_sem, exponents_sem,
):
    s = lax.axis_index("slab")
    b = lax.axis_index("blk")
    chip = s // 2
    up, down = lax.rem(s + 1, N_SLAB), lax.rem(s + N_SLAB - 1, N_SLAB)
    right, left = lax.rem(b + 1, N_BLK), lax.rem(b + N_BLK - 1, N_BLK)
    has_up, has_down = s < N_SLAB - 1, s > 0
    has_right, has_left = b < N_BLK - 1, b > 0

    loads = [
        pltpu.make_async_copy(thermal, state.at[0, 0, pl.ds(1, EDGE)], load_sem.at[0]),
        pltpu.make_async_copy(deform, state.at[0, pl.ds(1, 3), pl.ds(1, EDGE)], load_sem.at[1]),
        pltpu.make_async_copy(modulus, cond.at[pl.ds(1, EDGE)], load_sem.at[2]),
        pltpu.make_async_copy(plastic_in, plastic, load_sem.at[3]),
    ]
    for load in loads:
        load.start()

    barrier = pltpu.get_barrier_semaphore()

    for step in range(1, N_SLAB):
        peer = lax.rem(s + step, N_SLAB)
        pl.semaphore_signal(barrier, inc=1, device_id=(peer, b), device_id_type=MESH)

    @pl.when(has_right)
    def _():
        pl.semaphore_signal(barrier, inc=1, device_id=(s, right), device_id_type=MESH)

    @pl.when(has_left)
    def _():
        pl.semaphore_signal(barrier, inc=1, device_id=(s, left), device_id_type=MESH)

    zero_plane = jnp.zeros((EDGE, DEPTH), F32)

    for has, place, side in ((has_down, 0, 0), (has_up, EDGE + 1, 1)):

        @pl.when(jnp.logical_not(has))
        def _():
            cond[place] = zero_plane
            for t in range(SWEEPS):
                for f in range(4):
                    state[t, f, place] = zero_plane

    for has, side in ((has_left, 0), (has_right, 1)):

        @pl.when(jnp.logical_not(has))
        def _():
            cond_y[side] = zero_plane
            for t in range(SWEEPS):
                for f in range(4):
                    halo_y[t, side, f] = zero_plane

    row8 = row_of((8, 128))
    group8 = lane_of((8, 128)) // EDGE
    row = row_of((EDGE, DEPTH))
    lane = lane_of((EDGE, DEPTH))
    inner = lane & (EDGE - 1)

    for dy in (-1, 0, 1):
        for dz in (-1, 0, 1):
            inside = (row + dy >= 0) & (row + dy < EDGE) & (inner + dz >= 0) & (inner + dz < EDGE)
            reach = abs(dy) + abs(dz)
            weights[0, plane_number(dy, dz)] = jnp.where(inside, 0.5 * WEIGHTS[reach], 0.0)
            weights[1, plane_number(dy, dz)] = jnp.where(inside, 0.5 * WEIGHTS[reach + 1], 0.0)
    for n in range(9):
        for f in range(4):
            values[f, n, 0] = zero_plane
            values[f, n, EDGE + 1] = zero_plane
    for number, (dx, dy, dz) in enumerate(OFFSETS):
        if dx != 0:
            tile[number, 1 if dx < 0 else EDGE] = zero_plane

    factor = jnp.ones((1, DEPTH), F32)
    lane_row = lane_of((1, DEPTH)) // EDGE
    for p in range(P_DEV):
        factor = jnp.where(lane_row == p, 1.0 + 3.0 * flag[0, 0, p].astype(F32), factor)

    for load in loads:
        load.wait()

    def stage_first(x, carry):
        for side, y in ((0, 0), (1, EDGE - 1)):
            cond_stage[side, pl.ds(x, 1), :] = cond[x + 1, y : y + 1, :]
            for f in range(4):
                stage_y[0, side, f, pl.ds(x, 1), :] = state[0, f, x + 1, y : y + 1, :]
        return carry

    lax.fori_loop(0, EDGE, stage_first, 0)
    slot_lane = lane_of((1, 128))
    slot_row = jnp.zeros((1, 128), I32)
    for p in range(P_DEV):
        code = holder[0, 0, p] * P_DEV + position[0, 0, p]
        slot_row = jnp.where(slot_lane == lax.rem(s, 8) * P_DEV + p, code, slot_row)

    def plastic_planes(planes):
        tiles = []
        for x in planes:
            root = plastic[x]
            root = root * lax.rsqrt(root)
            codes = jnp.clip((root - PLASTIC_LOW) * PLASTIC_STEPS + 0.5, 0.0, 65535.0).astype(I32)
            words = (codes[:, 0:128] << 16) | codes[:, 128:256]
            tiles += [words[0:8], words[8:16]]
        tiles = swap_rows_and_groups(tiles, group8, swap_a, swap_b)
        for k in range(8):
            m = 2 * planes[k // 2] + k % 2
            plastic_one[m, 0:8, :] = tiles[k]
            plastic_one[m, 8:9, :] = slot_row

    def plastic_turn(k, carry):
        plastic_planes([4 * k + j for j in range(4)])
        return carry

    lax.fori_loop(0, 4, plastic_turn, 0)
    plastic_got[s, 0:9, :] = plastic_one[s, 0:9, :]

    neighbours = 31 + has_right.astype(I32) + has_left.astype(I32)
    pl.semaphore_wait(barrier, neighbours)

    def x_copies(kind):
        out = []
        for direction, peer in ((0, down), (1, up)):
            mine = 0 if direction == 0 else EDGE - 1
            there = EDGE + 1 if direction == 0 else 0
            if kind == 0:
                source, target = thermal.at[mine], state.at[0, 0, there]
            elif kind == 4:
                source, target = deform.at[:, mine], state.at[0, pl.ds(1, 3), there]
            elif kind == 5:
                source, target = modulus.at[mine], cond.at[there]
            else:
                source, target = state.at[kind, :, mine + 1], state.at[kind, :, there]
            out.append(
                pltpu.make_async_remote_copy(
                    source, target, x_send.at[kind, direction], x_recv.at[kind, direction],
                    device_id=(peer, b), device_id_type=MESH,
                )
            )
        return out

    def y_copies(kind):
        out = []
        for direction, peer in ((0, left), (1, right)):
            if kind == 4:
                source, target = cond_stage.at[direction], cond_y.at[1 - direction]
            elif kind == 0:
                source, target = stage_y.at[0, direction], halo_y.at[0, 1 - direction]
            else:
                part = pl.ds(8 * (kind // 4), 8)
                source = stage_y.at[kind % 4, direction, :, part]
                target = halo_y.at[kind % 4, 1 - direction, :, part]
            out.append(
                pltpu.make_async_remote_copy(
                    source, target, y_send.at[kind, direction], y_recv.at[kind, direction],
                    device_id=(s, peer), device_id_type=MESH,
                )
            )
        return out

    def start(copies, to_low, to_high):
        @pl.when(to_low)
        def _():
            copies[0].start()

        @pl.when(to_high)
        def _():
            copies[1].start()

    def wait_recv(copies, from_high, from_low):
        @pl.when(from_high)
        def _():
            copies[0].wait_recv()

        @pl.when(from_low)
        def _():
            copies[1].wait_recv()

    def four_at_a_time(work):
        def step(k, carry):
            for j in range(4):
                work(4 * k + j)
            return carry

        lax.fori_loop(0, EDGE // 4, step, 0)

    def wait_send(copies, to_low, to_high):
        @pl.when(to_low)
        def _():
            copies[0].wait_send()

        @pl.when(to_high)
        def _():
            copies[1].wait_send()

    for kind in (5, 0, 4):
        start(x_copies(kind), has_down, has_up)
    start(y_copies(4), has_left, has_right)
    start(y_copies(0), has_left, has_right)

    sibling = lax.bitwise_xor(s, 1)

    def send_plastic(m):
        pltpu.make_async_remote_copy(
            plastic_one.at[m, pl.ds(0, 9)], plastic_got.at[s, pl.ds(0, 9)], pl_one_send, pl_one_recv,
            device_id=(m, b), device_id_type=MESH,
        ).start()

    def plastic_out(step):
        planes = [lax.rem(chip + 4 * step + j, EDGE) for j in range(4)]
        if step == 0:
            send_plastic(sibling)
        for x in planes[step == 0 :]:
            send_plastic(2 * x)
            send_plastic(2 * x + 1)

    plastic_out(0)
    plastic_out(1)

    wait_recv(x_copies(5), has_up, has_down)
    wait_recv(y_copies(4), has_right, has_left)

    def face(x):
        here = cond[x + 1]
        ym = jnp.where(row == 0, cond_y[0, pl.ds(x, 1), :], pltpu.roll(here, 1, 0))
        yp = jnp.where(row == EDGE - 1, cond_y[1, pl.ds(x, 1), :], pltpu.roll(here, EDGE - 1, 0))
        zm = jnp.where(lane == 0, 0.0, pltpu.roll(here, 1, 1))
        zp = jnp.where(lane == DEPTH - 1, 0.0, pltpu.roll(here, DEPTH - 1, 1))
        low = 0.06 * (cond[x] + here)
        high = 0.06 * (here + cond[x + 2])
        face_x[x] = low
        face_x[x + 1] = high
        ym, yp, zm, zp = (0.06 * (here + beside) for beside in (ym, yp, zm, zp))
        face_ym[x] = ym
        face_yp[x] = yp
        face_zm[x] = zm
        face_zp[x] = zp
        centre[x] = 1.0 - (low + high + ym + yp + zm + zp)

    four_at_a_time(face)

    def sweep_plane(t, x):
        around = []
        for f in range(4):
            here = state[t, f, x + 1]
            around.append(
                (
                    here,
                    state[t, f, x],
                    state[t, f, x + 2],
                    jnp.where(row == 0, halo_y[t, 0, f, pl.ds(x, 1), :], pltpu.roll(here, 1, 0)),
                    jnp.where(row == EDGE - 1, halo_y[t, 1, f, pl.ds(x, 1), :], pltpu.roll(here, EDGE - 1, 0)),
                    jnp.where(lane == 0, 0.0, pltpu.roll(here, 1, 1)),
                    jnp.where(lane == DEPTH - 1, 0.0, pltpu.roll(here, DEPTH - 1, 1)),
                )
            )
        h, xm, xp, ym, yp, zm, zp = around[0]
        fresh = [
            centre[x] * h
            + face_x[x] * xm
            + face_x[x + 1] * xp
            + face_ym[x] * ym
            + face_yp[x] * yp
            + face_zm[x] * zm
            + face_zp[x] * zp
        ]
        slopes = (xp - xm, yp - ym, zp - zm)
        for c in range(3):
            u, *six = around[c + 1]
            total = (six[0] + six[1]) + (six[2] + six[3]) + (six[4] + six[5])
            fresh.append(0.28 * u + 0.12 * total - 0.06 * slopes[c])
        for f in range(4):
            state[t + 1, f, x + 1] = fresh[f]
            if t + 1 < SWEEPS:
                stage_y[t + 1, 0, f, pl.ds(x, 1), :] = fresh[f][0:1]
                stage_y[t + 1, 1, f, pl.ds(x, 1), :] = fresh[f][EDGE - 1 : EDGE]

    def sweep(t):
        def four(first):
            for x in range(first, first + 4):
                sweep_plane(t, x)

        onward_x = x_copies(t + 1) if t + 1 < SWEEPS else None
        if t > 0:
            arrived = x_copies(t)

            @pl.when(has_down)
            def _():
                arrived[1].wait_recv()

            wait_recv(y_copies(t), has_right, has_left)
        four(0)
        if onward_x:

            @pl.when(has_down)
            def _():
                onward_x[0].start()

        four(4)
        if onward_x:
            start(y_copies(t + 1), has_left, has_right)
        if t > 0:

            @pl.when(has_up)
            def _():
                arrived[0].wait_recv()

            wait_recv(y_copies(t + 4), has_right, has_left)
        four(12)
        if onward_x:

            @pl.when(has_up)
            def _():
                onward_x[1].start()

        four(8)
        if onward_x:
            start(y_copies(t + 5), has_left, has_right)

    wait_recv(x_copies(0), has_up, has_down)
    wait_recv(x_copies(4), has_up, has_down)
    wait_recv(y_copies(0), has_right, has_left)
    sweep(0)

    def wait_all(ref, semaphore):
        pltpu.make_async_copy(ref, ref, semaphore).wait()

    plastic_out(2)
    sweep(1)
    plastic_out(3)
    sweep(2)

    wait_all(plastic_got.at[pl.ds(0, N_SLAB - 1), pl.ds(0, 9)], pl_one_recv)
    slot_id = row_of((ROWS, 128))
    for g in range(4):
        codes = plastic_got[8 * g, 8:9, :]
        for k in range(1, 8):
            codes = codes + plastic_got[8 * g + k, 8:9, :]
        one_hot[:, 128 * g : 128 * g + 128] = jnp.where(slot_id == codes, 1.0, 0.0).astype(BF16)

    def plastic_unpack(g, carry):
        words = plastic_got[pl.ds(4 * g, 4), 0:8, :]
        both = jnp.concatenate([lax.shift_right_logical(words, 16), words & 65535], axis=1).reshape(64, 128)
        place = pl.ds(pl.multiple_of(64 * g, 64), 64)
        plastic_table[place, 0:128] = byte_of(both, 0)
        plastic_table[place, 128:256] = byte_of(both, 1)
        return carry

    lax.fori_loop(0, 8, plastic_unpack, 0)

    def plastic_group(g, carry):
        place = pl.ds(pl.multiple_of(128 * g, 128), 128)
        rows = jnp.dot(one_hot[place, :], plastic_table[...], preferred_element_type=F32)
        codes = joined(rows[:, 0:128], rows[:, 128:256]).reshape(8, P_DEV, 128)
        send_two[pl.ds(8 * g, 8), 32:40, :] = (codes[:, 0:8] << 16) | codes[:, 8:16]
        return carry

    lax.fori_loop(0, 4, plastic_group, 0)
    sweep(3)

    def beside(plane):
        parts = [plane[:, 0:128], plane[:, 128:256]]
        return [jnp.concatenate([pltpu.roll(part, turn, 1) for part in parts], axis=1) for turn in (1, 127)]

    def prepare(k, most):
        most = list(most)
        for j in range(4):
            x = 4 * k + j
            fields = [state[SWEEPS, f, x + 1] for f in range(4)]
            squared = fields[0] * fields[0]
            stiffness = cond[x + 1] * (1.0 + 0.5 * squared / (1.0 + squared)) / (1.0 + plastic[x]) * factor
            stiff[x + 1] = stiffness
            for f, plane in enumerate([stiffness] + fields):
                turned[f, 0, x], turned[f, 1, x] = beside(plane)
            most = [jnp.maximum(most[f], jnp.abs(fields[f])) for f in range(4)]
        return tuple(most)

    most = lax.fori_loop(0, EDGE // 4, prepare, (zero_plane,) * 4)
    exponents = []
    exponent_row = jnp.zeros((1, 128), I32)
    scales = []
    for f in range(4):
        largest = jnp.max(jnp.max(most[f], axis=0, keepdims=True), axis=1, keepdims=True)
        exponent = jnp.ceil(jnp.log2(jnp.maximum(largest, 1e-30)) + 0.001)
        scales.append(jnp.exp2(-exponent))
        exponent_row = jnp.where(slot_lane == f, exponent.astype(I32), exponent_row)

    numbers = {offset: number for number, offset in enumerate(OFFSETS)}
    halves = (slice(0, 8), slice(8, 16))
    ones = (jnp.ones((8, 128), F32),) * 2

    def built(x, done, active, side):
        lanes = slice(128 * side, 128 * side + 128)
        begun = [ones] + [tuple(state[SWEEPS, f, x + 2, rows, lanes] for rows in halves) for f in range(4)]
        totals = {1: list(done), 0: list(active), -1: begun}
        own = {dx: [stiff[x + 1 - dx, rows, lanes] for rows in halves] for dx in (-1, 0, 1)}
        centres = [own[0]] + [[state[SWEEPS, f, x + 1, rows, lanes] for rows in halves] for f in range(4)]
        near, *fields = [
            shifted_pairs(
                (
                    [turned[f, 0, x, rows, lanes] for rows in halves],
                    centres[f],
                    [turned[f, 1, x, rows, lanes] for rows in halves],
                ),
                row8,
            )
            for f in range(5)
        ]
        for dz in (-1, 0, 1):
            for dy in (-1, 0, 1):
                n = plane_number(dy, dz)
                for dx in (-1, 0, 1):
                    if (dx, dy, dz) == (0, 0, 0):
                        continue
                    number = numbers[dx, dy, dz]
                    entries = []
                    for j, rows in enumerate(halves):
                        entry = weights[abs(dx), n, rows, 0:128] * (own[dx][j] + near[n][j])
                        entry = entry.astype(BF16).astype(F32)
                        tile[number, x + 1 - dx, rows, lanes] = entry
                        entries.append(entry)
                    total = totals[dx]
                    total[0] = tuple(total[0][j] + entries[j] for j in range(2))
                    for f in range(4):
                        total[f + 1] = tuple(total[f + 1][j] + entries[j] * fields[f][n][j] for j in range(2))
        return tuple(totals[1]), tuple(totals[0]), tuple(totals[-1])

    def finish(place, done, side):
        lanes = slice(128 * side, 128 * side + 128)
        scale = [1.0 / part for part in done[0]]
        for j, rows in enumerate(halves):
            inverse[place, rows, lanes] = scale[j]
        for f in range(4):
            for j, rows in enumerate(halves):
                stepped[f, place, rows, lanes] = done[f + 1][j] * scale[j]

    for side in range(2):

        def source(k, carry):
            for j in range(2):
                done, *carry = built(2 * k + j, *carry, side)
                finish(2 * k + j, done, side)
            return tuple(carry)

        lanes = slice(128 * side, 128 * side + 128)
        start_at = (ones,) + tuple(tuple(state[SWEEPS, f, 1, rows, lanes] for rows in halves) for f in range(4))
        last, _ = lax.fori_loop(0, EDGE // 2, source, ((ones,) * 5, start_at))
        finish(EDGE, last, side)

    def spread(k, carry):
        for j in range(2):
            x = 2 * k + j
            for f in range(4):
                plane = stepped[f, x + 1]
                minus, plus = beside(plane)
                for side in range(2):
                    lanes = slice(128 * side, 128 * side + 128)
                    three = [[part[rows, lanes] for rows in halves] for part in (minus, plane, plus)]
                    for n, pair in enumerate(shifted_pairs(three, row8)):
                        for i, rows in enumerate(halves):
                            values[f, n, x + 1, rows, lanes] = pair[i]
        return carry

    lax.fori_loop(0, EDGE // 2, spread, 0)

    def smoothed(x):
        totals = [state[SWEEPS, f, x + 1] for f in range(4)]
        for number, (dx, dy, dz) in enumerate(OFFSETS):
            entry = tile[number, x + 1]
            for f in range(4):
                totals[f] = totals[f] + entry * values[f, plane_number(dy, dz), x + 1 + dx]
        scale = inverse[x + 1]
        return [total * scale for total in totals]

    def send_plane(m):
        pltpu.make_async_remote_copy(
            send_one.at[m, pl.ds(0, 33)], recv_one.at[s, pl.ds(0, 33)], one_send, one_recv,
            device_id=(m, b), device_id_type=MESH,
        ).start()

    def encode_plane(x, slot):
        codes = []
        for f, field in enumerate(smoothed(x)):
            part = jnp.abs(field) * scales[f]
            part = jnp.minimum(part * lax.rsqrt(part + 1e-37), 1.0) * 32767.0
            codes.append((jnp.where(field < 0.0, -part, part) + 32768.5).astype(I32))
        coded[slot, 0] = (codes[0] << 16) | codes[1]
        coded[slot, 1] = (codes[2] << 16) | codes[3]

    def turn_plane(x, slot):
        tiles = [
            coded[slot, w, 8 * half : 8 * half + 8, 128 * side : 128 * side + 128]
            for half in range(2)
            for w in range(2)
            for side in range(2)
        ]
        tiles = swap_rows_and_groups(tiles, group8, swap_a, swap_b)
        for half in range(2):
            m = 2 * x + half
            for k in range(4):
                send_one[m, 8 * k : 8 * k + 8, :] = tiles[4 * half + k]
            send_one[m, 32:33, :] = exponent_row

    def second(step, carry):
        x, later = lax.rem(step + chip, EDGE), lax.rem(step + 1 + chip, EDGE)
        slot = lax.rem(step, 2)
        turn_plane(x, slot)
        encode_plane(later, 1 - slot)
        send_plane(2 * x)
        send_plane(2 * x + 1)
        return carry

    encode_plane(chip, 0)
    turn_plane(chip, 0)
    send_plane(sibling)
    recv_one[s, 0:33, :] = send_one[s, 0:33, :]
    encode_plane(lax.rem(chip + 1, EDGE), 1)
    lax.fori_loop(1, EDGE - 1, second, 0)
    turn_plane(lax.rem(chip + EDGE - 1, EDGE), 1)
    send_plane(2 * lax.rem(chip + EDGE - 1, EDGE))
    send_plane(2 * lax.rem(chip + EDGE - 1, EDGE) + 1)
    wait_all(recv_one.at[pl.ds(0, N_SLAB - 1), pl.ds(0, 33)], one_recv)

    def unpack(g, carry):
        place = pl.ds(pl.multiple_of(64 * g, 64), 64)
        for w in range(2):
            words = recv_one[pl.ds(4 * g, 4), 16 * w : 16 * w + 16, :].reshape(64, 128)
            for number in range(4):
                at = 128 * (4 * w + number)
                table[place, at : at + 128] = byte_of(words, number)
        return carry

    lax.fori_loop(0, 8, unpack, 0)

    def onward_group(g):
        place = pl.ds(pl.multiple_of(256 * g, 256), 256)
        rows = jnp.dot(one_hot[place, :], table[...], preferred_element_type=F32)
        for w in range(2):
            parts = [rows[:, 128 * (4 * w + n) : 128 * (4 * w + n) + 128] for n in range(4)]
            words = joined(parts[0], parts[1]) | (joined(parts[2], parts[3]) << 16)
            send_two[pl.ds(16 * g, 16), 16 * w : 16 * w + 16, :] = words.reshape(16, P_DEV, 128)

    def pass_on(d):
        pltpu.make_async_remote_copy(
            send_two.at[d], out_words.at[s], two_send, two_recv,
            device_id=(d, b), device_id_type=MESH,
        ).start()

    onward_group(0)
    onward_group(1)
    pltpu.make_async_copy(send_two.at[s], out_words.at[s], own_sem).start()
    pass_on(sibling)
    for k in range(1, EDGE):
        d = 2 * lax.rem(chip + k, EDGE)
        pass_on(d)
        pass_on(d + 1)

    sources = jnp.concatenate(
        [jnp.broadcast_to(recv_one[k, 32:33, :].astype(F32), (P_DEV, 128)) for k in range(N_SLAB)], axis=0
    ).astype(BF16)
    mine = one_hot[pl.ds(pl.multiple_of(s * P_DEV, P_DEV), P_DEV), :]
    exponents_here[...] = jnp.dot(mine, sources, preferred_element_type=F32)
    exponents_out = pltpu.make_async_copy(exponents_here, out_exponents, exponents_sem)
    exponents_out.start()

    for kind in (0, 1, 2, 3, 4, 5):
        wait_send(x_copies(kind), has_down, has_up)
    for kind in range(8):
        wait_send(y_copies(kind), has_left, has_right)
    wait_all(plastic_one.at[pl.ds(0, N_SLAB - 1), pl.ds(0, 9)], pl_one_send)
    wait_all(send_one.at[pl.ds(0, N_SLAB - 1), pl.ds(0, 33)], one_send)
    wait_all(send_two.at[pl.ds(0, N_SLAB - 1)], two_send)
    pltpu.make_async_copy(send_two.at[s], out_words.at[s], own_sem).wait()
    exponents_out.wait()
    wait_all(out_words.at[pl.ds(0, N_SLAB - 1)], two_recv)


def move(thermal, deform, modulus, plastic, flag, holder, position):
    anywhere = pl.BlockSpec(memory_space=pl.ANY)
    smem = pl.BlockSpec(memory_space=pltpu.SMEM)
    plane = (EDGE, DEPTH)
    dma = pltpu.SemaphoreType.DMA
    return pl.pallas_call(
        move_kernel,
        name="sweep_solve_move",
        out_shape=(
            jax.ShapeDtypeStruct((N_SLAB, 40, 128), I32),
            jax.ShapeDtypeStruct((P_DEV, 128), F32),
        ),
        in_specs=[anywhere] * 4 + [smem] * 3,
        out_specs=(anywhere, anywhere),
        scratch_shapes=[
            pltpu.VMEM((EDGE,) + plane, F32),
            pltpu.VMEM((SWEEPS + 1, 4, EDGE + 2) + plane, F32),
            pltpu.VMEM((SWEEPS, 2, 4) + plane, F32),
            pltpu.VMEM((SWEEPS, 2, 4) + plane, F32),
            pltpu.VMEM((EDGE + 2,) + plane, F32),
            pltpu.VMEM((2,) + plane, F32),
            pltpu.VMEM((2,) + plane, F32),
            pltpu.VMEM((EDGE + 1,) + plane, F32),
            pltpu.VMEM((EDGE,) + plane, F32),
            pltpu.VMEM((EDGE,) + plane, F32),
            pltpu.VMEM((EDGE,) + plane, F32),
            pltpu.VMEM((EDGE,) + plane, F32),
            pltpu.VMEM((EDGE,) + plane, F32),
            pltpu.VMEM((EDGE + 2,) + plane, F32),
            pltpu.VMEM((5, 2, EDGE) + plane, F32),
            pltpu.VMEM((4, EDGE + 1) + plane, F32),
            pltpu.VMEM((2, 2) + plane, I32),
            pltpu.VMEM((2, 9) + plane, F32),
            pltpu.VMEM((26, EDGE + 2) + plane, F32),
            pltpu.VMEM((EDGE + 1,) + plane, F32),
            pltpu.VMEM((4, 9, EDGE + 2) + plane, F32),
            pltpu.VMEM((N_SLAB, 40, 128), I32),
            pltpu.VMEM((N_SLAB, 40, 128), I32),
            pltpu.VMEM((N_SLAB, 40, 128), I32),
            pltpu.VMEM((N_SLAB, 16, 128), I32),
            pltpu.VMEM((N_SLAB, 16, 128), I32),
            pltpu.VMEM((ROWS, ROWS), BF16),
            pltpu.VMEM((ROWS, 1024), BF16),
            pltpu.VMEM((ROWS, 256), BF16),
            pltpu.VMEM((64, 128), I32),
            pltpu.VMEM((64, 128), I32),
            pltpu.VMEM((P_DEV, 128), F32),
            dma((4,)),
            dma((6, 2)),
            dma((6, 2)),
            dma((8, 2)),
            dma((8, 2)),
            dma(()),
            dma(()),
            dma(()),
            dma(()),
            dma(()),
            dma(()),
            dma(()),
            dma(()),
        ],
        compiler_params=pltpu.CompilerParams(
            collective_id=0, has_side_effects=True, vmem_limit_bytes=56 * 1024 * 1024
        ),
    )(thermal, deform, modulus, plastic, flag, holder, position)


def decode_kernel(
    words_in, exponents_in, heat_out, moved_out, plastic_out, words, exponents, heat, moved, straight, got, put
):
    pieces = N_SLAB // 4
    fetch = [
        pltpu.make_async_copy(words_in.at[pl.ds(pieces * k, pieces)], words.at[pl.ds(pieces * k, pieces)], got.at[k])
        for k in range(4)
    ]
    fetch.insert(0, pltpu.make_async_copy(exponents_in, exponents, got.at[4]))
    for copy in fetch:
        copy.start()
    fetch.pop(0).wait()
    scales = [
        jnp.broadcast_to(jnp.exp2(exponents[:, f : f + 1]) * (1.0 / (32767.0 * 32767.0)), (P_DEV, 128))
        for f in range(4)
    ]
    length = 128 * pieces
    writes = []
    for k in range(4):
        fetch[k].wait()
        for m in range(pieces * k, pieces * k + pieces):
            at = slice(128 * m, 128 * m + 128)
            for w in range(2):
                word = words[m, 16 * w : 16 * w + 16, :]
                for part in range(2):
                    code = lax.shift_right_logical(word, 16) if part == 0 else word & 65535
                    root = (code - 32768).astype(F32)
                    field = root * jnp.abs(root) * scales[2 * w + part]
                    if w == 0 and part == 0:
                        heat[:, at] = field
                    else:
                        moved[2 * w + part - 1, :, at] = field
        at = pl.ds(length * k, length)
        writes.append(pltpu.make_async_copy(heat.at[:, at], heat_out.at[0, 0, :, at], put.at[3 * k]))
        writes.append(pltpu.make_async_copy(moved.at[:, :, at], moved_out.at[0, 0, :, :, at], put.at[3 * k + 1]))
        for copy in writes[-2:]:
            copy.start()
        for m in range(pieces * k, pieces * k + pieces):
            word = words[m, 32:40, :]
            for part in range(2):
                code = lax.shift_right_logical(word, 16) if part == 0 else word & 65535
                root = code.astype(F32) * (1.0 / PLASTIC_STEPS) + PLASTIC_LOW
                straight[8 * part : 8 * part + 8, 128 * m : 128 * m + 128] = root * root
        writes.append(pltpu.make_async_copy(straight.at[:, at], plastic_out.at[0, 0, :, at], put.at[3 * k + 2]))
        writes[-1].start()
    for copy in writes:
        copy.wait()


def decode(words, exponents):
    anywhere = pl.BlockSpec(memory_space=pl.ANY)
    length = EDGE**3
    heat, moved, strain = pl.pallas_call(
        decode_kernel,
        name="decode",
        out_shape=(
            jax.ShapeDtypeStruct((1, 1, P_DEV, length), F32),
            jax.ShapeDtypeStruct((1, 1, 3, P_DEV, length), F32),
            jax.ShapeDtypeStruct((1, 1, P_DEV, length), F32),
        ),
        in_specs=[anywhere, anywhere],
        out_specs=(anywhere,) * 3,
        scratch_shapes=[
            pltpu.VMEM((N_SLAB, 40, 128), I32),
            pltpu.VMEM((P_DEV, 128), F32),
            pltpu.VMEM((P_DEV, length), F32),
            pltpu.VMEM((3, P_DEV, length), F32),
            pltpu.VMEM((P_DEV, length), F32),
            pltpu.SemaphoreType.DMA((5,)),
            pltpu.SemaphoreType.DMA((12,)),
        ],
        compiler_params=pltpu.CompilerParams(vmem_limit_bytes=56 * 1024 * 1024),
    )(words, exponents)
    return heat, moved.transpose(0, 1, 3, 2, 4), strain


def on_device(thermal, deform, modulus, plastic, flag, holder, position):
    return decode(*move(thermal, deform, modulus, plastic, flag, holder, position))


def solution(mesh):
    placed = (
        P("slab", "blk", None),
        P(None, "slab", "blk", None),
        P("slab", "blk", None),
        P("slab", "blk", None),
        P("slab", "blk", None),
        P("slab", "blk", None),
        P("slab", "blk", None),
    )
    return jax.shard_map(
        on_device,
        mesh=mesh,
        in_specs=placed,
        out_specs=(
            P("slab", "blk", None, None),
            P("slab", "blk", None, None, None),
            P("slab", "blk", None, None),
        ),
        check_vma=False,
    )
```

```python
import jax
import jax.numpy as jnp
from jax import lax
from jax.experimental import pallas as pl
from jax.experimental.pallas import tpu as pltpu
from jax.sharding import PartitionSpec as P

EDGE = 16
DEPTH = 256
SWEEPS = 4
N_SLAB = 32
N_BLK = 4
P_DEV = 16
ROWS = N_SLAB * P_DEV
MESH = pl.DeviceIdType.MESH
F32 = jnp.float32
I32 = jnp.int32
BF16 = jnp.bfloat16

PLASTIC_LOW = 0.2235
PLASTIC_STEPS = 65535.0 / (1.4145 - PLASTIC_LOW)

OFFSETS = [
    (dx, dy, dz)
    for dx in (-1, 0, 1)
    for dy in (-1, 0, 1)
    for dz in (-1, 0, 1)
    if (dx, dy, dz) != (0, 0, 0)
]
WEIGHTS = [0.0, 0.1, 0.04, 0.02]


def plane_number(dy, dz):
    return (dy + 1) * 3 + dz + 1


def lane_of(shape):
    return lax.broadcasted_iota(I32, shape, 1)


def row_of(shape):
    return lax.broadcasted_iota(I32, shape, 0)


def shifted_pairs(three, row8):
    out = [None] * 9
    for dz, (a, b) in zip((-1, 0, 1), three):
        a_down, b_down = pltpu.roll(a, 1, 0), pltpu.roll(b, 1, 0)
        a_up, b_up = pltpu.roll(a, 7, 0), pltpu.roll(b, 7, 0)
        out[plane_number(-1, dz)] = (a_down, jnp.where(row8 == 0, a_down, b_down))
        out[plane_number(0, dz)] = (a, b)
        out[plane_number(1, dz)] = (jnp.where(row8 == 7, b_up, a_up), b_up)
    return out


def swap_rows_and_groups(tiles, group, first, second):
    for k in range(8):
        first[8 * k : 8 * k + 8, :] = tiles[k]
    parts = [first[pl.ds(k, 8, stride=8), :] for k in range(8)]
    for bit in (4, 2, 1):
        low_group = (group & bit) == 0
        for k in range(8):
            if k & bit == 0:
                low, high = parts[k], parts[k | bit]
                parts[k] = jnp.where(low_group, low, pltpu.roll(high, 16 * bit, 1))
                parts[k | bit] = jnp.where(low_group, pltpu.roll(low, 128 - 16 * bit, 1), high)
    for k in range(8):
        second[8 * k : 8 * k + 8, :] = parts[k]
    return [second[pl.ds(k, 8, stride=8), :] for k in range(8)]


def byte_of(words, number):
    part = words if number == 0 else lax.shift_right_logical(words, 8 * number)
    return (part & 255).astype(F32).astype(BF16)


def joined(low, high):
    return (low + 256.0 * high).astype(I32)


def move_kernel(
    thermal, deform, modulus, plastic_in, flag, holder, position,
    out_words, out_plastic, out_exponents,
    plastic, state, halo_y, stage_y, cond, cond_y, cond_stage,
    face_x, face_ym, face_yp, face_zm, face_zp, centre,
    stiff, turned, stepped, coded, weights, tile, inverse, values,
    send_one, recv_one, send_two, plastic_one, plastic_got, plastic_two,
    one_hot, table, plastic_table, swap_a, swap_b, exponents_here,
    load_sem, x_send, x_recv, y_send, y_recv,
    one_send, one_recv, two_send, two_recv, pl_one_send, pl_one_recv, pl_two_send, pl_two_recv, own_sem, own_plastic_sem, exponents_sem,
):
    s = lax.axis_index("slab")
    b = lax.axis_index("blk")
    chip = s // 2
    up, down = lax.rem(s + 1, N_SLAB), lax.rem(s + N_SLAB - 1, N_SLAB)
    right, left = lax.rem(b + 1, N_BLK), lax.rem(b + N_BLK - 1, N_BLK)
    has_up, has_down = s < N_SLAB - 1, s > 0
    has_right, has_left = b < N_BLK - 1, b > 0

    loads = [
        pltpu.make_async_copy(thermal, state.at[0, 0, pl.ds(1, EDGE)], load_sem.at[0]),
        pltpu.make_async_copy(deform, state.at[0, pl.ds(1, 3), pl.ds(1, EDGE)], load_sem.at[1]),
        pltpu.make_async_copy(modulus, cond.at[pl.ds(1, EDGE)], load_sem.at[2]),
        pltpu.make_async_copy(plastic_in, plastic, load_sem.at[3]),
    ]
    for load in loads:
        load.start()

    barrier = pltpu.get_barrier_semaphore()

    for step in range(1, N_SLAB):
        peer = lax.rem(s + step, N_SLAB)
        pl.semaphore_signal(barrier, inc=1, device_id=(peer, b), device_id_type=MESH)

    @pl.when(has_right)
    def _():
        pl.semaphore_signal(barrier, inc=1, device_id=(s, right), device_id_type=MESH)

    @pl.when(has_left)
    def _():
        pl.semaphore_signal(barrier, inc=1, device_id=(s, left), device_id_type=MESH)

    zero_plane = jnp.zeros((EDGE, DEPTH), F32)

    for has, place, side in ((has_down, 0, 0), (has_up, EDGE + 1, 1)):

        @pl.when(jnp.logical_not(has))
        def _():
            cond[place] = zero_plane
            for t in range(SWEEPS):
                for f in range(4):
                    state[t, f, place] = zero_plane

    for has, side in ((has_left, 0), (has_right, 1)):

        @pl.when(jnp.logical_not(has))
        def _():
            cond_y[side] = zero_plane
            for t in range(SWEEPS):
                for f in range(4):
                    halo_y[t, side, f] = zero_plane

    row8 = row_of((8, 128))
    group8 = lane_of((8, 128)) // EDGE
    row = row_of((EDGE, DEPTH))
    lane = lane_of((EDGE, DEPTH))
    inner = lane & (EDGE - 1)

    for dy in (-1, 0, 1):
        for dz in (-1, 0, 1):
            inside = (row + dy >= 0) & (row + dy < EDGE) & (inner + dz >= 0) & (inner + dz < EDGE)
            reach = abs(dy) + abs(dz)
            weights[0, plane_number(dy, dz)] = jnp.where(inside, 0.5 * WEIGHTS[reach], 0.0)
            weights[1, plane_number(dy, dz)] = jnp.where(inside, 0.5 * WEIGHTS[reach + 1], 0.0)
    for n in range(9):
        for f in range(4):
            values[f, n, 0] = zero_plane
            values[f, n, EDGE + 1] = zero_plane
    for number, (dx, dy, dz) in enumerate(OFFSETS):
        if dx != 0:
            tile[number, 1 if dx < 0 else EDGE] = zero_plane

    factor = jnp.ones((1, DEPTH), F32)
    lane_row = lane_of((1, DEPTH)) // EDGE
    for p in range(P_DEV):
        factor = jnp.where(lane_row == p, 1.0 + 3.0 * flag[0, 0, p].astype(F32), factor)

    for load in loads:
        load.wait()

    def stage_first(x, carry):
        for side, y in ((0, 0), (1, EDGE - 1)):
            cond_stage[side, pl.ds(x, 1), :] = cond[x + 1, y : y + 1, :]
            for f in range(4):
                stage_y[0, side, f, pl.ds(x, 1), :] = state[0, f, x + 1, y : y + 1, :]
        return carry

    lax.fori_loop(0, EDGE, stage_first, 0)
    slot_lane = lane_of((1, 128))
    slot_row = jnp.zeros((1, 128), I32)
    for p in range(P_DEV):
        code = holder[0, 0, p] * P_DEV + position[0, 0, p]
        slot_row = jnp.where(slot_lane == lax.rem(s, 8) * P_DEV + p, code, slot_row)

    def plastic_planes(planes):
        tiles = []
        for x in planes:
            root = plastic[x]
            root = root * lax.rsqrt(root)
            codes = jnp.clip((root - PLASTIC_LOW) * PLASTIC_STEPS + 0.5, 0.0, 65535.0).astype(I32)
            words = (codes[:, 0:128] << 16) | codes[:, 128:256]
            tiles += [words[0:8], words[8:16]]
        tiles = swap_rows_and_groups(tiles, group8, swap_a, swap_b)
        for k in range(8):
            m = 2 * planes[k // 2] + k % 2
            plastic_one[m, 0:8, :] = tiles[k]
            plastic_one[m, 8:9, :] = slot_row

    def plastic_turn(k, carry):
        plastic_planes([4 * k + j for j in range(4)])
        return carry

    lax.fori_loop(0, 4, plastic_turn, 0)
    plastic_got[s, 0:9, :] = plastic_one[s, 0:9, :]

    neighbours = 31 + has_right.astype(I32) + has_left.astype(I32)
    pl.semaphore_wait(barrier, neighbours)

    def x_copies(kind):
        out = []
        for direction, peer in ((0, down), (1, up)):
            mine = 0 if direction == 0 else EDGE - 1
            there = EDGE + 1 if direction == 0 else 0
            if kind == 0:
                source, target = thermal.at[mine], state.at[0, 0, there]
            elif kind == 4:
                source, target = deform.at[:, mine], state.at[0, pl.ds(1, 3), there]
            elif kind == 5:
                source, target = modulus.at[mine], cond.at[there]
            else:
                source, target = state.at[kind, :, mine + 1], state.at[kind, :, there]
            out.append(
                pltpu.make_async_remote_copy(
                    source, target, x_send.at[kind, direction], x_recv.at[kind, direction],
                    device_id=(peer, b), device_id_type=MESH,
                )
            )
        return out

    def y_copies(kind):
        out = []
        for direction, peer in ((0, left), (1, right)):
            if kind == 4:
                source, target = cond_stage.at[direction], cond_y.at[1 - direction]
            elif kind == 0:
                source, target = stage_y.at[0, direction], halo_y.at[0, 1 - direction]
            else:
                part = pl.ds(8 * (kind // 4), 8)
                source = stage_y.at[kind % 4, direction, :, part]
                target = halo_y.at[kind % 4, 1 - direction, :, part]
            out.append(
                pltpu.make_async_remote_copy(
                    source, target, y_send.at[kind, direction], y_recv.at[kind, direction],
                    device_id=(s, peer), device_id_type=MESH,
                )
            )
        return out

    def start(copies, to_low, to_high):
        @pl.when(to_low)
        def _():
            copies[0].start()

        @pl.when(to_high)
        def _():
            copies[1].start()

    def wait_recv(copies, from_high, from_low):
        @pl.when(from_high)
        def _():
            copies[0].wait_recv()

        @pl.when(from_low)
        def _():
            copies[1].wait_recv()

    def four_at_a_time(work):
        def step(k, carry):
            for j in range(4):
                work(4 * k + j)
            return carry

        lax.fori_loop(0, EDGE // 4, step, 0)

    def wait_send(copies, to_low, to_high):
        @pl.when(to_low)
        def _():
            copies[0].wait_send()

        @pl.when(to_high)
        def _():
            copies[1].wait_send()

    for kind in (5, 0, 4):
        start(x_copies(kind), has_down, has_up)
    start(y_copies(4), has_left, has_right)
    start(y_copies(0), has_left, has_right)

    sibling = lax.bitwise_xor(s, 1)

    def send_plastic(m):
        pltpu.make_async_remote_copy(
            plastic_one.at[m, pl.ds(0, 9)], plastic_got.at[s, pl.ds(0, 9)], pl_one_send, pl_one_recv,
            device_id=(m, b), device_id_type=MESH,
        ).start()

    def plastic_out(step):
        planes = [lax.rem(chip + 4 * step + j, EDGE) for j in range(4)]
        if step == 0:
            send_plastic(sibling)
        for x in planes[step == 0 :]:
            send_plastic(2 * x)
            send_plastic(2 * x + 1)

    plastic_out(0)
    plastic_out(1)

    wait_recv(x_copies(5), has_up, has_down)
    wait_recv(y_copies(4), has_right, has_left)

    def face(x):
        here = cond[x + 1]
        ym = jnp.where(row == 0, cond_y[0, pl.ds(x, 1), :], pltpu.roll(here, 1, 0))
        yp = jnp.where(row == EDGE - 1, cond_y[1, pl.ds(x, 1), :], pltpu.roll(here, EDGE - 1, 0))
        zm = jnp.where(lane == 0, 0.0, pltpu.roll(here, 1, 1))
        zp = jnp.where(lane == DEPTH - 1, 0.0, pltpu.roll(here, DEPTH - 1, 1))
        low = 0.06 * (cond[x] + here)
        high = 0.06 * (here + cond[x + 2])
        face_x[x] = low
        face_x[x + 1] = high
        ym, yp, zm, zp = (0.06 * (here + beside) for beside in (ym, yp, zm, zp))
        face_ym[x] = ym
        face_yp[x] = yp
        face_zm[x] = zm
        face_zp[x] = zp
        centre[x] = 1.0 - (low + high + ym + yp + zm + zp)

    four_at_a_time(face)

    def sweep_plane(t, x):
        around = []
        for f in range(4):
            here = state[t, f, x + 1]
            around.append(
                (
                    here,
                    state[t, f, x],
                    state[t, f, x + 2],
                    jnp.where(row == 0, halo_y[t, 0, f, pl.ds(x, 1), :], pltpu.roll(here, 1, 0)),
                    jnp.where(row == EDGE - 1, halo_y[t, 1, f, pl.ds(x, 1), :], pltpu.roll(here, EDGE - 1, 0)),
                    jnp.where(lane == 0, 0.0, pltpu.roll(here, 1, 1)),
                    jnp.where(lane == DEPTH - 1, 0.0, pltpu.roll(here, DEPTH - 1, 1)),
                )
            )
        h, xm, xp, ym, yp, zm, zp = around[0]
        fresh = [
            centre[x] * h
            + face_x[x] * xm
            + face_x[x + 1] * xp
            + face_ym[x] * ym
            + face_yp[x] * yp
            + face_zm[x] * zm
            + face_zp[x] * zp
        ]
        slopes = (xp - xm, yp - ym, zp - zm)
        for c in range(3):
            u, *six = around[c + 1]
            total = (six[0] + six[1]) + (six[2] + six[3]) + (six[4] + six[5])
            fresh.append(0.28 * u + 0.12 * total - 0.06 * slopes[c])
        for f in range(4):
            state[t + 1, f, x + 1] = fresh[f]
            if t + 1 < SWEEPS:
                stage_y[t + 1, 0, f, pl.ds(x, 1), :] = fresh[f][0:1]
                stage_y[t + 1, 1, f, pl.ds(x, 1), :] = fresh[f][EDGE - 1 : EDGE]

    def sweep(t):
        def four(first):
            for x in range(first, first + 4):
                sweep_plane(t, x)

        onward_x = x_copies(t + 1) if t + 1 < SWEEPS else None
        if t > 0:
            arrived = x_copies(t)

            @pl.when(has_down)
            def _():
                arrived[1].wait_recv()

            wait_recv(y_copies(t), has_right, has_left)
        four(0)
        if onward_x:

            @pl.when(has_down)
            def _():
                onward_x[0].start()

        four(4)
        if onward_x:
            start(y_copies(t + 1), has_left, has_right)
        if t > 0:

            @pl.when(has_up)
            def _():
                arrived[0].wait_recv()

            wait_recv(y_copies(t + 4), has_right, has_left)
        four(12)
        if onward_x:

            @pl.when(has_up)
            def _():
                onward_x[1].start()

        four(8)
        if onward_x:
            start(y_copies(t + 5), has_left, has_right)

    wait_recv(x_copies(0), has_up, has_down)
    wait_recv(x_copies(4), has_up, has_down)
    wait_recv(y_copies(0), has_right, has_left)
    sweep(0)

    def wait_all(ref, semaphore):
        pltpu.make_async_copy(ref, ref, semaphore).wait()

    plastic_out(2)
    sweep(1)
    plastic_out(3)
    sweep(2)

    wait_all(plastic_got.at[pl.ds(0, N_SLAB - 1), pl.ds(0, 9)], pl_one_recv)
    slot_id = row_of((ROWS, 128))
    for g in range(4):
        codes = plastic_got[8 * g, 8:9, :]
        for k in range(1, 8):
            codes = codes + plastic_got[8 * g + k, 8:9, :]
        one_hot[:, 128 * g : 128 * g + 128] = jnp.where(slot_id == codes, 1.0, 0.0).astype(BF16)

    def plastic_unpack(g, carry):
        words = plastic_got[pl.ds(4 * g, 4), 0:8, :]
        both = jnp.concatenate([lax.shift_right_logical(words, 16), words & 65535], axis=1).reshape(64, 128)
        place = pl.ds(pl.multiple_of(64 * g, 64), 64)
        plastic_table[place, 0:128] = byte_of(both, 0)
        plastic_table[place, 128:256] = byte_of(both, 1)
        return carry

    lax.fori_loop(0, 8, plastic_unpack, 0)

    def plastic_group(g, carry):
        place = pl.ds(pl.multiple_of(128 * g, 128), 128)
        rows = jnp.dot(one_hot[place, :], plastic_table[...], preferred_element_type=F32)
        codes = joined(rows[:, 0:128], rows[:, 128:256]).reshape(8, P_DEV, 128)
        plastic_two[pl.ds(8 * g, 8)] = (codes[:, 0:8] << 16) | codes[:, 8:16]
        return carry

    lax.fori_loop(0, 4, plastic_group, 0)

    def pass_plastic(number):
        d = 2 * lax.rem(chip + 1 + number // 2, EDGE) + lax.rem(number, 2)
        start_plastic(d)

    def start_plastic(d):
        pltpu.make_async_remote_copy(
            plastic_two.at[d], out_plastic.at[s], pl_two_send, pl_two_recv,
            device_id=(d, b), device_id_type=MESH,
        ).start()

    own_plastic = pltpu.make_async_copy(plastic_two.at[s], out_plastic.at[s], own_plastic_sem)
    own_plastic.start()
    start_plastic(sibling)
    sweep(3)

    def beside(plane):
        parts = [plane[:, 0:128], plane[:, 128:256]]
        return [jnp.concatenate([pltpu.roll(part, turn, 1) for part in parts], axis=1) for turn in (1, 127)]

    def prepare(k, most):
        most = list(most)
        for j in range(4):
            x = 4 * k + j
            fields = [state[SWEEPS, f, x + 1] for f in range(4)]
            squared = fields[0] * fields[0]
            stiffness = cond[x + 1] * (1.0 + 0.5 * squared / (1.0 + squared)) / (1.0 + plastic[x]) * factor
            stiff[x + 1] = stiffness
            for f, plane in enumerate([stiffness] + fields):
                turned[f, 0, x], turned[f, 1, x] = beside(plane)
            most = [jnp.maximum(most[f], jnp.abs(fields[f])) for f in range(4)]
        return tuple(most)

    most = lax.fori_loop(0, EDGE // 4, prepare, (zero_plane,) * 4)
    exponents = []
    exponent_row = jnp.zeros((1, 128), I32)
    scales = []
    for f in range(4):
        largest = jnp.max(jnp.max(most[f], axis=0, keepdims=True), axis=1, keepdims=True)
        exponent = jnp.ceil(jnp.log2(jnp.maximum(largest, 1e-30)) + 0.001)
        scales.append(jnp.exp2(-exponent))
        exponent_row = jnp.where(slot_lane == f, exponent.astype(I32), exponent_row)

    numbers = {offset: number for number, offset in enumerate(OFFSETS)}
    halves = (slice(0, 8), slice(8, 16))
    ones = (jnp.ones((8, 128), F32),) * 2

    def built(x, done, active, side):
        lanes = slice(128 * side, 128 * side + 128)
        begun = [ones] + [tuple(state[SWEEPS, f, x + 2, rows, lanes] for rows in halves) for f in range(4)]
        totals = {1: list(done), 0: list(active), -1: begun}
        own = {dx: [stiff[x + 1 - dx, rows, lanes] for rows in halves] for dx in (-1, 0, 1)}
        centres = [own[0]] + [[state[SWEEPS, f, x + 1, rows, lanes] for rows in halves] for f in range(4)]
        near, *fields = [
            shifted_pairs(
                (
                    [turned[f, 0, x, rows, lanes] for rows in halves],
                    centres[f],
                    [turned[f, 1, x, rows, lanes] for rows in halves],
                ),
                row8,
            )
            for f in range(5)
        ]
        for dz in (-1, 0, 1):
            for dy in (-1, 0, 1):
                n = plane_number(dy, dz)
                for dx in (-1, 0, 1):
                    if (dx, dy, dz) == (0, 0, 0):
                        continue
                    number = numbers[dx, dy, dz]
                    entries = []
                    for j, rows in enumerate(halves):
                        entry = weights[abs(dx), n, rows, 0:128] * (own[dx][j] + near[n][j])
                        entry = entry.astype(BF16).astype(F32)
                        tile[number, x + 1 - dx, rows, lanes] = entry
                        entries.append(entry)
                    total = totals[dx]
                    total[0] = tuple(total[0][j] + entries[j] for j in range(2))
                    for f in range(4):
                        total[f + 1] = tuple(total[f + 1][j] + entries[j] * fields[f][n][j] for j in range(2))
        return tuple(totals[1]), tuple(totals[0]), tuple(totals[-1])

    def finish(place, done, side):
        lanes = slice(128 * side, 128 * side + 128)
        scale = [1.0 / part for part in done[0]]
        for j, rows in enumerate(halves):
            inverse[place, rows, lanes] = scale[j]
        for f in range(4):
            for j, rows in enumerate(halves):
                stepped[f, place, rows, lanes] = done[f + 1][j] * scale[j]

    for side in range(2):

        def source(k, carry):
            if side == 0:
                pass_plastic(2 * k)
                pass_plastic(2 * k + 1)
            else:
                pass_plastic(16 + k)
            for j in range(2):
                done, *carry = built(2 * k + j, *carry, side)
                finish(2 * k + j, done, side)
            return tuple(carry)

        lanes = slice(128 * side, 128 * side + 128)
        start_at = (ones,) + tuple(tuple(state[SWEEPS, f, 1, rows, lanes] for rows in halves) for f in range(4))
        last, _ = lax.fori_loop(0, EDGE // 2, source, ((ones,) * 5, start_at))
        finish(EDGE, last, side)

    pass_plastic(28)
    pass_plastic(29)

    def spread(k, carry):
        pass_plastic(24 + k)
        for j in range(4):
            x = 4 * k + j
            for f in range(4):
                plane = stepped[f, x + 1]
                minus, plus = beside(plane)
                for side in range(2):
                    lanes = slice(128 * side, 128 * side + 128)
                    three = [[part[rows, lanes] for rows in halves] for part in (minus, plane, plus)]
                    for n, pair in enumerate(shifted_pairs(three, row8)):
                        for i, rows in enumerate(halves):
                            values[f, n, x + 1, rows, lanes] = pair[i]
        return carry

    lax.fori_loop(0, EDGE // 4, spread, 0)

    def smoothed(x):
        totals = [state[SWEEPS, f, x + 1] for f in range(4)]
        for number, (dx, dy, dz) in enumerate(OFFSETS):
            entry = tile[number, x + 1]
            for f in range(4):
                totals[f] = totals[f] + entry * values[f, plane_number(dy, dz), x + 1 + dx]
        scale = inverse[x + 1]
        return [total * scale for total in totals]

    def send_plane(m):
        pltpu.make_async_remote_copy(
            send_one.at[m, pl.ds(0, 33)], recv_one.at[s, pl.ds(0, 33)], one_send, one_recv,
            device_id=(m, b), device_id_type=MESH,
        ).start()

    def encode_plane(x, slot):
        codes = []
        for f, field in enumerate(smoothed(x)):
            part = jnp.abs(field) * scales[f]
            part = jnp.minimum(part * lax.rsqrt(part + 1e-37), 1.0) * 32767.0
            codes.append((jnp.where(field < 0.0, -part, part) + 32768.5).astype(I32))
        coded[slot, 0] = (codes[0] << 16) | codes[1]
        coded[slot, 1] = (codes[2] << 16) | codes[3]

    def turn_plane(x, slot):
        tiles = [
            coded[slot, w, 8 * half : 8 * half + 8, 128 * side : 128 * side + 128]
            for half in range(2)
            for w in range(2)
            for side in range(2)
        ]
        tiles = swap_rows_and_groups(tiles, group8, swap_a, swap_b)
        for half in range(2):
            m = 2 * x + half
            for k in range(4):
                send_one[m, 8 * k : 8 * k + 8, :] = tiles[4 * half + k]
            send_one[m, 32:33, :] = exponent_row

    def second(step, carry):
        x, later = lax.rem(step + chip, EDGE), lax.rem(step + 1 + chip, EDGE)
        slot = lax.rem(step, 2)
        turn_plane(x, slot)
        encode_plane(later, 1 - slot)
        send_plane(2 * x)
        send_plane(2 * x + 1)
        return carry

    encode_plane(chip, 0)
    turn_plane(chip, 0)
    send_plane(sibling)
    recv_one[s, 0:33, :] = send_one[s, 0:33, :]
    encode_plane(lax.rem(chip + 1, EDGE), 1)
    lax.fori_loop(1, EDGE - 1, second, 0)
    turn_plane(lax.rem(chip + EDGE - 1, EDGE), 1)
    send_plane(2 * lax.rem(chip + EDGE - 1, EDGE))
    send_plane(2 * lax.rem(chip + EDGE - 1, EDGE) + 1)
    wait_all(recv_one.at[pl.ds(0, N_SLAB - 1), pl.ds(0, 33)], one_recv)

    def unpack(g, carry):
        place = pl.ds(pl.multiple_of(64 * g, 64), 64)
        for w in range(2):
            words = recv_one[pl.ds(4 * g, 4), 16 * w : 16 * w + 16, :].reshape(64, 128)
            for number in range(4):
                at = 128 * (4 * w + number)
                table[place, at : at + 128] = byte_of(words, number)
        return carry

    lax.fori_loop(0, 8, unpack, 0)

    def onward_group(g):
        place = pl.ds(pl.multiple_of(256 * g, 256), 256)
        rows = jnp.dot(one_hot[place, :], table[...], preferred_element_type=F32)
        for w in range(2):
            parts = [rows[:, 128 * (4 * w + n) : 128 * (4 * w + n) + 128] for n in range(4)]
            words = joined(parts[0], parts[1]) | (joined(parts[2], parts[3]) << 16)
            send_two[pl.ds(16 * g, 16), 16 * w : 16 * w + 16, :] = words.reshape(16, P_DEV, 128)

    def pass_on(d):
        pltpu.make_async_remote_copy(
            send_two.at[d], out_words.at[s], two_send, two_recv,
            device_id=(d, b), device_id_type=MESH,
        ).start()

    onward_group(0)
    onward_group(1)
    pltpu.make_async_copy(send_two.at[s], out_words.at[s], own_sem).start()
    pass_on(sibling)
    for k in range(1, EDGE):
        d = 2 * lax.rem(chip + k, EDGE)
        pass_on(d)
        pass_on(d + 1)

    sources = jnp.concatenate(
        [jnp.broadcast_to(recv_one[k, 32:33, :].astype(F32), (P_DEV, 128)) for k in range(N_SLAB)], axis=0
    ).astype(BF16)
    mine = one_hot[pl.ds(pl.multiple_of(s * P_DEV, P_DEV), P_DEV), :]
    exponents_here[...] = jnp.dot(mine, sources, preferred_element_type=F32)
    exponents_out = pltpu.make_async_copy(exponents_here, out_exponents, exponents_sem)
    exponents_out.start()

    for kind in (0, 1, 2, 3, 4, 5):
        wait_send(x_copies(kind), has_down, has_up)
    for kind in range(8):
        wait_send(y_copies(kind), has_left, has_right)
    wait_all(plastic_one.at[pl.ds(0, N_SLAB - 1), pl.ds(0, 9)], pl_one_send)
    wait_all(send_one.at[pl.ds(0, N_SLAB - 1), pl.ds(0, 33)], one_send)
    wait_all(send_two.at[pl.ds(0, N_SLAB - 1)], two_send)
    wait_all(plastic_two.at[pl.ds(0, N_SLAB - 1)], pl_two_send)
    own_plastic.wait()
    wait_all(out_plastic.at[pl.ds(0, N_SLAB - 1)], pl_two_recv)
    pltpu.make_async_copy(send_two.at[s], out_words.at[s], own_sem).wait()
    exponents_out.wait()
    wait_all(out_words.at[pl.ds(0, N_SLAB - 1)], two_recv)


def move(thermal, deform, modulus, plastic, flag, holder, position):
    anywhere = pl.BlockSpec(memory_space=pl.ANY)
    smem = pl.BlockSpec(memory_space=pltpu.SMEM)
    plane = (EDGE, DEPTH)
    dma = pltpu.SemaphoreType.DMA
    return pl.pallas_call(
        move_kernel,
        name="sweep_solve_move",
        out_shape=(
            jax.ShapeDtypeStruct((N_SLAB, 32, 128), I32),
            jax.ShapeDtypeStruct((N_SLAB, 8, 128), I32),
            jax.ShapeDtypeStruct((P_DEV, 128), F32),
        ),
        in_specs=[anywhere] * 4 + [smem] * 3,
        out_specs=(anywhere,) * 3,
        scratch_shapes=[
            pltpu.VMEM((EDGE,) + plane, F32),
            pltpu.VMEM((SWEEPS + 1, 4, EDGE + 2) + plane, F32),
            pltpu.VMEM((SWEEPS, 2, 4) + plane, F32),
            pltpu.VMEM((SWEEPS, 2, 4) + plane, F32),
            pltpu.VMEM((EDGE + 2,) + plane, F32),
            pltpu.VMEM((2,) + plane, F32),
            pltpu.VMEM((2,) + plane, F32),
            pltpu.VMEM((EDGE + 1,) + plane, F32),
            pltpu.VMEM((EDGE,) + plane, F32),
            pltpu.VMEM((EDGE,) + plane, F32),
            pltpu.VMEM((EDGE,) + plane, F32),
            pltpu.VMEM((EDGE,) + plane, F32),
            pltpu.VMEM((EDGE,) + plane, F32),
            pltpu.VMEM((EDGE + 2,) + plane, F32),
            pltpu.VMEM((5, 2, EDGE) + plane, F32),
            pltpu.VMEM((4, EDGE + 1) + plane, F32),
            pltpu.VMEM((2, 2) + plane, I32),
            pltpu.VMEM((2, 9) + plane, F32),
            pltpu.VMEM((26, EDGE + 2) + plane, F32),
            pltpu.VMEM((EDGE + 1,) + plane, F32),
            pltpu.VMEM((4, 9, EDGE + 2) + plane, F32),
            pltpu.VMEM((N_SLAB, 40, 128), I32),
            pltpu.VMEM((N_SLAB, 40, 128), I32),
            pltpu.VMEM((N_SLAB, 32, 128), I32),
            pltpu.VMEM((N_SLAB, 16, 128), I32),
            pltpu.VMEM((N_SLAB, 16, 128), I32),
            pltpu.VMEM((N_SLAB, 8, 128), I32),
            pltpu.VMEM((ROWS, ROWS), BF16),
            pltpu.VMEM((ROWS, 1024), BF16),
            pltpu.VMEM((ROWS, 256), BF16),
            pltpu.VMEM((64, 128), I32),
            pltpu.VMEM((64, 128), I32),
            pltpu.VMEM((P_DEV, 128), F32),
            dma((4,)),
            dma((6, 2)),
            dma((6, 2)),
            dma((8, 2)),
            dma((8, 2)),
            dma(()),
            dma(()),
            dma(()),
            dma(()),
            dma(()),
            dma(()),
            dma(()),
            dma(()),
            dma(()),
            dma(()),
            dma(()),
        ],
        compiler_params=pltpu.CompilerParams(
            collective_id=0, has_side_effects=True, vmem_limit_bytes=56 * 1024 * 1024
        ),
    )(thermal, deform, modulus, plastic, flag, holder, position)


def decode_kernel(
    words_in, plastic_in, exponents_in, heat_out, moved_out, plastic_out, words, strain, exponents, heat, moved, straight, got, put
):
    pieces = N_SLAB // 4
    fetch = [
        pltpu.make_async_copy(words_in.at[pl.ds(pieces * k, pieces)], words.at[pl.ds(pieces * k, pieces)], got.at[k])
        for k in range(4)
    ]
    fetch.append(pltpu.make_async_copy(plastic_in, strain, got.at[5]))
    fetch.insert(0, pltpu.make_async_copy(exponents_in, exponents, got.at[4]))
    for copy in fetch:
        copy.start()
    fetch.pop(0).wait()
    scales = [
        jnp.broadcast_to(jnp.exp2(exponents[:, f : f + 1]) * (1.0 / (32767.0 * 32767.0)), (P_DEV, 128))
        for f in range(4)
    ]
    length = 128 * pieces
    writes = []
    for k in range(4):
        fetch[k].wait()
        for m in range(pieces * k, pieces * k + pieces):
            at = slice(128 * m, 128 * m + 128)
            for w in range(2):
                word = words[m, 16 * w : 16 * w + 16, :]
                for part in range(2):
                    code = lax.shift_right_logical(word, 16) if part == 0 else word & 65535
                    root = (code - 32768).astype(F32)
                    field = root * jnp.abs(root) * scales[2 * w + part]
                    if w == 0 and part == 0:
                        heat[:, at] = field
                    else:
                        moved[2 * w + part - 1, :, at] = field
        at = pl.ds(length * k, length)
        writes.append(pltpu.make_async_copy(heat.at[:, at], heat_out.at[0, 0, :, at], put.at[3 * k]))
        writes.append(pltpu.make_async_copy(moved.at[:, :, at], moved_out.at[0, 0, :, :, at], put.at[3 * k + 1]))
        for copy in writes[-2:]:
            copy.start()
        if k == 0:
            fetch[4].wait()
        for m in range(pieces * k, pieces * k + pieces):
            word = strain[m]
            for part in range(2):
                code = lax.shift_right_logical(word, 16) if part == 0 else word & 65535
                root = code.astype(F32) * (1.0 / PLASTIC_STEPS) + PLASTIC_LOW
                straight[8 * part : 8 * part + 8, 128 * m : 128 * m + 128] = root * root
        writes.append(pltpu.make_async_copy(straight.at[:, at], plastic_out.at[0, 0, :, at], put.at[3 * k + 2]))
        writes[-1].start()
    for copy in writes:
        copy.wait()


def decode(words, plastic, exponents):
    anywhere = pl.BlockSpec(memory_space=pl.ANY)
    length = EDGE**3
    heat, moved, strain = pl.pallas_call(
        decode_kernel,
        name="decode",
        out_shape=(
            jax.ShapeDtypeStruct((1, 1, P_DEV, length), F32),
            jax.ShapeDtypeStruct((1, 1, 3, P_DEV, length), F32),
            jax.ShapeDtypeStruct((1, 1, P_DEV, length), F32),
        ),
        in_specs=[anywhere] * 3,
        out_specs=(anywhere,) * 3,
        scratch_shapes=[
            pltpu.VMEM((N_SLAB, 32, 128), I32),
            pltpu.VMEM((N_SLAB, 8, 128), I32),
            pltpu.VMEM((P_DEV, 128), F32),
            pltpu.VMEM((P_DEV, length), F32),
            pltpu.VMEM((3, P_DEV, length), F32),
            pltpu.VMEM((P_DEV, length), F32),
            pltpu.SemaphoreType.DMA((6,)),
            pltpu.SemaphoreType.DMA((12,)),
        ],
        compiler_params=pltpu.CompilerParams(vmem_limit_bytes=56 * 1024 * 1024),
    )(words, plastic, exponents)
    return heat, moved.transpose(0, 1, 3, 2, 4), strain


def on_device(thermal, deform, modulus, plastic, flag, holder, position):
    return decode(*move(thermal, deform, modulus, plastic, flag, holder, position))


def solution(mesh):
    placed = (
        P("slab", "blk", None),
        P(None, "slab", "blk", None),
        P("slab", "blk", None),
        P("slab", "blk", None),
        P("slab", "blk", None),
        P("slab", "blk", None),
        P("slab", "blk", None),
    )
    return jax.shard_map(
        on_device,
        mesh=mesh,
        in_specs=placed,
        out_specs=(
            P("slab", "blk", None, None),
            P("slab", "blk", None, None, None),
            P("slab", "blk", None, None),
        ),
        check_vma=False,
    )
```

```python
import jax
import jax.numpy as jnp
from jax import lax
from jax.experimental import pallas as pl
from jax.experimental.pallas import tpu as pltpu
from jax.sharding import PartitionSpec as P

EDGE = 16
DEPTH = 256
SWEEPS = 4
N_SLAB = 32
N_BLK = 4
P_DEV = 16
ROWS = N_SLAB * P_DEV
MESH = pl.DeviceIdType.MESH
F32 = jnp.float32
I32 = jnp.int32
BF16 = jnp.bfloat16

PLASTIC_LOW = 0.2235
PLASTIC_STEPS = 65535.0 / (1.4145 - PLASTIC_LOW)

OFFSETS = [
    (dx, dy, dz)
    for dx in (-1, 0, 1)
    for dy in (-1, 0, 1)
    for dz in (-1, 0, 1)
    if (dx, dy, dz) != (0, 0, 0)
]
WEIGHTS = [0.0, 0.1, 0.04, 0.02]


def plane_number(dy, dz):
    return (dy + 1) * 3 + dz + 1


def lane_of(shape):
    return lax.broadcasted_iota(I32, shape, 1)


def row_of(shape):
    return lax.broadcasted_iota(I32, shape, 0)


def shifted_pairs(three, row8):
    out = [None] * 9
    for dz, (a, b) in zip((-1, 0, 1), three):
        a_down, b_down = pltpu.roll(a, 1, 0), pltpu.roll(b, 1, 0)
        a_up, b_up = pltpu.roll(a, 7, 0), pltpu.roll(b, 7, 0)
        out[plane_number(-1, dz)] = (a_down, jnp.where(row8 == 0, a_down, b_down))
        out[plane_number(0, dz)] = (a, b)
        out[plane_number(1, dz)] = (jnp.where(row8 == 7, b_up, a_up), b_up)
    return out


def swap_rows_and_groups(tiles, group, first, second):
    for k in range(8):
        first[8 * k : 8 * k + 8, :] = tiles[k]
    parts = [first[pl.ds(k, 8, stride=8), :] for k in range(8)]
    for bit in (4, 2, 1):
        low_group = (group & bit) == 0
        for k in range(8):
            if k & bit == 0:
                low, high = parts[k], parts[k | bit]
                parts[k] = jnp.where(low_group, low, pltpu.roll(high, 16 * bit, 1))
                parts[k | bit] = jnp.where(low_group, pltpu.roll(low, 128 - 16 * bit, 1), high)
    for k in range(8):
        second[8 * k : 8 * k + 8, :] = parts[k]
    return [second[pl.ds(k, 8, stride=8), :] for k in range(8)]


def byte_of(words, number):
    part = words if number == 0 else lax.shift_right_logical(words, 8 * number)
    return (part & 255).astype(F32).astype(BF16)


def joined(low, high):
    return (low + 256.0 * high).astype(I32)


def move_kernel(
    thermal, deform, modulus, plastic_in, flag, holder, position,
    out_words, out_plastic, out_exponents,
    plastic, state, halo_y, stage_y, cond, cond_y, cond_stage,
    face_x, face_ym, face_yp, face_zm, face_zp, centre,
    stiff, turned, stepped, coded, weights, tile, inverse, values,
    send_one, recv_one, send_two, plastic_one, plastic_got, plastic_two,
    one_hot, table, plastic_table, swap_a, swap_b, exponents_here,
    load_sem, x_send, x_recv, y_send, y_recv,
    one_send, one_recv, two_send, two_recv, pl_one_send, pl_one_recv, pl_two_send, pl_two_recv, own_sem, own_plastic_sem, exponents_sem,
):
    s = lax.axis_index("slab")
    b = lax.axis_index("blk")
    chip = s // 2
    up, down = lax.rem(s + 1, N_SLAB), lax.rem(s + N_SLAB - 1, N_SLAB)
    right, left = lax.rem(b + 1, N_BLK), lax.rem(b + N_BLK - 1, N_BLK)
    has_up, has_down = s < N_SLAB - 1, s > 0
    has_right, has_left = b < N_BLK - 1, b > 0

    loads = [
        pltpu.make_async_copy(thermal, state.at[0, 0, pl.ds(1, EDGE)], load_sem.at[0]),
        pltpu.make_async_copy(deform, state.at[0, pl.ds(1, 3), pl.ds(1, EDGE)], load_sem.at[1]),
        pltpu.make_async_copy(modulus, cond.at[pl.ds(1, EDGE)], load_sem.at[2]),
        pltpu.make_async_copy(plastic_in, plastic, load_sem.at[3]),
    ]
    for load in loads:
        load.start()

    barrier = pltpu.get_barrier_semaphore()

    for step in range(1, N_SLAB):
        peer = lax.rem(s + step, N_SLAB)
        pl.semaphore_signal(barrier, inc=1, device_id=(peer, b), device_id_type=MESH)

    @pl.when(has_right)
    def _():
        pl.semaphore_signal(barrier, inc=1, device_id=(s, right), device_id_type=MESH)

    @pl.when(has_left)
    def _():
        pl.semaphore_signal(barrier, inc=1, device_id=(s, left), device_id_type=MESH)

    zero_plane = jnp.zeros((EDGE, DEPTH), F32)

    for has, place, side in ((has_down, 0, 0), (has_up, EDGE + 1, 1)):

        @pl.when(jnp.logical_not(has))
        def _():
            cond[place] = zero_plane
            for t in range(SWEEPS):
                for f in range(4):
                    state[t, f, place] = zero_plane

    for has, side in ((has_left, 0), (has_right, 1)):

        @pl.when(jnp.logical_not(has))
        def _():
            cond_y[side] = zero_plane
            for t in range(SWEEPS):
                for f in range(4):
                    halo_y[t, side, f] = zero_plane

    row8 = row_of((8, 128))
    group8 = lane_of((8, 128)) // EDGE
    row = row_of((EDGE, DEPTH))
    lane = lane_of((EDGE, DEPTH))
    inner = lane & (EDGE - 1)

    for load in loads:
        load.wait()

    def stage_first(x, carry):
        for side, y in ((0, 0), (1, EDGE - 1)):
            cond_stage[side, pl.ds(x, 1), :] = cond[x + 1, y : y + 1, :]
            for f in range(4):
                stage_y[0, side, f, pl.ds(x, 1), :] = state[0, f, x + 1, y : y + 1, :]
        return carry

    lax.fori_loop(0, EDGE, stage_first, 0)
    neighbours = 31 + has_right.astype(I32) + has_left.astype(I32)
    pl.semaphore_wait(barrier, neighbours)

    def x_copies(kind):
        out = []
        for direction, peer in ((0, down), (1, up)):
            mine = 0 if direction == 0 else EDGE - 1
            there = EDGE + 1 if direction == 0 else 0
            if kind == 0:
                source, target = thermal.at[mine], state.at[0, 0, there]
            elif kind == 4:
                source, target = deform.at[:, mine], state.at[0, pl.ds(1, 3), there]
            elif kind == 5:
                source, target = modulus.at[mine], cond.at[there]
            else:
                source, target = state.at[kind, :, mine + 1], state.at[kind, :, there]
            out.append(
                pltpu.make_async_remote_copy(
                    source, target, x_send.at[kind, direction], x_recv.at[kind, direction],
                    device_id=(peer, b), device_id_type=MESH,
                )
            )
        return out

    def y_copies(kind):
        out = []
        for direction, peer in ((0, left), (1, right)):
            if kind == 4:
                source, target = cond_stage.at[direction], cond_y.at[1 - direction]
            elif kind == 0:
                source, target = stage_y.at[0, direction], halo_y.at[0, 1 - direction]
            else:
                part = pl.ds(8 * (kind // 4), 8)
                source = stage_y.at[kind % 4, direction, :, part]
                target = halo_y.at[kind % 4, 1 - direction, :, part]
            out.append(
                pltpu.make_async_remote_copy(
                    source, target, y_send.at[kind, direction], y_recv.at[kind, direction],
                    device_id=(s, peer), device_id_type=MESH,
                )
            )
        return out

    def start(copies, to_low, to_high):
        @pl.when(to_low)
        def _():
            copies[0].start()

        @pl.when(to_high)
        def _():
            copies[1].start()

    def wait_recv(copies, from_high, from_low):
        @pl.when(from_high)
        def _():
            copies[0].wait_recv()

        @pl.when(from_low)
        def _():
            copies[1].wait_recv()

    def four_at_a_time(work):
        def step(k, carry):
            for j in range(4):
                work(4 * k + j)
            return carry

        lax.fori_loop(0, EDGE // 4, step, 0)

    def wait_send(copies, to_low, to_high):
        @pl.when(to_low)
        def _():
            copies[0].wait_send()

        @pl.when(to_high)
        def _():
            copies[1].wait_send()

    for kind in (5, 0, 4):
        start(x_copies(kind), has_down, has_up)
    start(y_copies(4), has_left, has_right)
    start(y_copies(0), has_left, has_right)

    slot_lane = lane_of((1, 128))
    slot_row = jnp.zeros((1, 128), I32)
    for p in range(P_DEV):
        code = holder[0, 0, p] * P_DEV + position[0, 0, p]
        slot_row = jnp.where(slot_lane == lax.rem(s, 8) * P_DEV + p, code, slot_row)

    def plastic_planes(planes):
        tiles = []
        for x in planes:
            root = plastic[x]
            root = root * lax.rsqrt(root)
            codes = jnp.clip((root - PLASTIC_LOW) * PLASTIC_STEPS + 0.5, 0.0, 65535.0).astype(I32)
            words = (codes[:, 0:128] << 16) | codes[:, 128:256]
            tiles += [words[0:8], words[8:16]]
        tiles = swap_rows_and_groups(tiles, group8, swap_a, swap_b)
        for k in range(8):
            m = 2 * planes[k // 2] + k % 2
            plastic_one[m, 0:8, :] = tiles[k]
            plastic_one[m, 8:9, :] = slot_row

    def plastic_turn(k, carry):
        plastic_planes([4 * k + j for j in range(4)])
        return carry

    lax.fori_loop(0, 4, plastic_turn, 0)
    plastic_got[s, 0:9, :] = plastic_one[s, 0:9, :]

    sibling = lax.bitwise_xor(s, 1)

    def send_plastic(m):
        pltpu.make_async_remote_copy(
            plastic_one.at[m, pl.ds(0, 9)], plastic_got.at[s, pl.ds(0, 9)], pl_one_send, pl_one_recv,
            device_id=(m, b), device_id_type=MESH,
        ).start()

    def plastic_out(step):
        planes = [lax.rem(chip + 4 * step + j, EDGE) for j in range(4)]
        if step == 0:
            send_plastic(sibling)
        for x in planes[step == 0 :]:
            send_plastic(2 * x)
            send_plastic(2 * x + 1)

    plastic_out(0)
    plastic_out(1)

    for dy in (-1, 0, 1):
        for dz in (-1, 0, 1):
            inside = (row + dy >= 0) & (row + dy < EDGE) & (inner + dz >= 0) & (inner + dz < EDGE)
            reach = abs(dy) + abs(dz)
            weights[0, plane_number(dy, dz)] = jnp.where(inside, 0.5 * WEIGHTS[reach], 0.0)
            weights[1, plane_number(dy, dz)] = jnp.where(inside, 0.5 * WEIGHTS[reach + 1], 0.0)
    for n in range(9):
        for f in range(4):
            values[f, n, 0] = zero_plane
            values[f, n, EDGE + 1] = zero_plane
    for number, (dx, dy, dz) in enumerate(OFFSETS):
        if dx != 0:
            tile[number, 1 if dx < 0 else EDGE] = zero_plane

    factor = jnp.ones((1, DEPTH), F32)
    lane_row = lane_of((1, DEPTH)) // EDGE
    for p in range(P_DEV):
        factor = jnp.where(lane_row == p, 1.0 + 3.0 * flag[0, 0, p].astype(F32), factor)

    wait_recv(x_copies(5), has_up, has_down)
    wait_recv(y_copies(4), has_right, has_left)

    def face(x):
        here = cond[x + 1]
        ym = jnp.where(row == 0, cond_y[0, pl.ds(x, 1), :], pltpu.roll(here, 1, 0))
        yp = jnp.where(row == EDGE - 1, cond_y[1, pl.ds(x, 1), :], pltpu.roll(here, EDGE - 1, 0))
        zm = jnp.where(lane == 0, 0.0, pltpu.roll(here, 1, 1))
        zp = jnp.where(lane == DEPTH - 1, 0.0, pltpu.roll(here, DEPTH - 1, 1))
        low = 0.06 * (cond[x] + here)
        high = 0.06 * (here + cond[x + 2])
        face_x[x] = low
        face_x[x + 1] = high
        ym, yp, zm, zp = (0.06 * (here + beside) for beside in (ym, yp, zm, zp))
        face_ym[x] = ym
        face_yp[x] = yp
        face_zm[x] = zm
        face_zp[x] = zp
        centre[x] = 1.0 - (low + high + ym + yp + zm + zp)

    four_at_a_time(face)

    def sweep_plane(t, x):
        around = []
        for f in range(4):
            here = state[t, f, x + 1]
            around.append(
                (
                    here,
                    state[t, f, x],
                    state[t, f, x + 2],
                    jnp.where(row == 0, halo_y[t, 0, f, pl.ds(x, 1), :], pltpu.roll(here, 1, 0)),
                    jnp.where(row == EDGE - 1, halo_y[t, 1, f, pl.ds(x, 1), :], pltpu.roll(here, EDGE - 1, 0)),
                    jnp.where(lane == 0, 0.0, pltpu.roll(here, 1, 1)),
                    jnp.where(lane == DEPTH - 1, 0.0, pltpu.roll(here, DEPTH - 1, 1)),
                )
            )
        h, xm, xp, ym, yp, zm, zp = around[0]
        fresh = [
            centre[x] * h
            + face_x[x] * xm
            + face_x[x + 1] * xp
            + face_ym[x] * ym
            + face_yp[x] * yp
            + face_zm[x] * zm
            + face_zp[x] * zp
        ]
        slopes = (xp - xm, yp - ym, zp - zm)
        for c in range(3):
            u, *six = around[c + 1]
            total = (six[0] + six[1]) + (six[2] + six[3]) + (six[4] + six[5])
            fresh.append(0.28 * u + 0.12 * total - 0.06 * slopes[c])
        for f in range(4):
            state[t + 1, f, x + 1] = fresh[f]
            if t + 1 < SWEEPS:
                stage_y[t + 1, 0, f, pl.ds(x, 1), :] = fresh[f][0:1]
                stage_y[t + 1, 1, f, pl.ds(x, 1), :] = fresh[f][EDGE - 1 : EDGE]

    def sweep(t):
        def four(first):
            for x in range(first, first + 4):
                sweep_plane(t, x)

        onward_x = x_copies(t + 1) if t + 1 < SWEEPS else None
        if t > 0:
            arrived = x_copies(t)

            @pl.when(has_down)
            def _():
                arrived[1].wait_recv()

            wait_recv(y_copies(t), has_right, has_left)
        four(0)
        if onward_x:

            @pl.when(has_down)
            def _():
                onward_x[0].start()

        four(4)
        if onward_x:
            start(y_copies(t + 1), has_left, has_right)
        if t > 0:

            @pl.when(has_up)
            def _():
                arrived[0].wait_recv()

            wait_recv(y_copies(t + 4), has_right, has_left)
        four(12)
        if onward_x:

            @pl.when(has_up)
            def _():
                onward_x[1].start()

        four(8)
        if onward_x:
            start(y_copies(t + 5), has_left, has_right)

    wait_recv(x_copies(0), has_up, has_down)
    wait_recv(x_copies(4), has_up, has_down)
    wait_recv(y_copies(0), has_right, has_left)
    sweep(0)

    def wait_all(ref, semaphore):
        pltpu.make_async_copy(ref, ref, semaphore).wait()

    plastic_out(2)
    sweep(1)
    plastic_out(3)
    sweep(2)

    wait_all(plastic_got.at[pl.ds(0, N_SLAB - 1), pl.ds(0, 9)], pl_one_recv)
    slot_id = row_of((ROWS, 128))
    for g in range(4):
        codes = plastic_got[8 * g, 8:9, :]
        for k in range(1, 8):
            codes = codes + plastic_got[8 * g + k, 8:9, :]
        one_hot[:, 128 * g : 128 * g + 128] = jnp.where(slot_id == codes, 1.0, 0.0).astype(BF16)

    def plastic_unpack(g, carry):
        words = plastic_got[pl.ds(4 * g, 4), 0:8, :]
        both = jnp.concatenate([lax.shift_right_logical(words, 16), words & 65535], axis=1).reshape(64, 128)
        place = pl.ds(pl.multiple_of(64 * g, 64), 64)
        plastic_table[place, 0:128] = byte_of(both, 0)
        plastic_table[place, 128:256] = byte_of(both, 1)
        return carry

    lax.fori_loop(0, 8, plastic_unpack, 0)

    def plastic_group(g, carry):
        place = pl.ds(pl.multiple_of(128 * g, 128), 128)
        rows = jnp.dot(one_hot[place, :], plastic_table[...], preferred_element_type=F32)
        codes = joined(rows[:, 0:128], rows[:, 128:256]).reshape(8, P_DEV, 128)
        plastic_two[pl.ds(8 * g, 8)] = (codes[:, 0:8] << 16) | codes[:, 8:16]
        return carry

    lax.fori_loop(0, 4, plastic_group, 0)

    def pass_plastic(number):
        d = 2 * lax.rem(chip + 1 + number // 2, EDGE) + lax.rem(number, 2)
        start_plastic(d)

    def start_plastic(d):
        pltpu.make_async_remote_copy(
            plastic_two.at[d], out_plastic.at[s], pl_two_send, pl_two_recv,
            device_id=(d, b), device_id_type=MESH,
        ).start()

    own_plastic = pltpu.make_async_copy(plastic_two.at[s], out_plastic.at[s], own_plastic_sem)
    own_plastic.start()
    start_plastic(sibling)
    sweep(3)

    def beside(plane):
        parts = [plane[:, 0:128], plane[:, 128:256]]
        return [jnp.concatenate([pltpu.roll(part, turn, 1) for part in parts], axis=1) for turn in (1, 127)]

    def prepare(k, most):
        most = list(most)
        for j in range(4):
            x = 4 * k + j
            fields = [state[SWEEPS, f, x + 1] for f in range(4)]
            squared = fields[0] * fields[0]
            stiffness = cond[x + 1] * (1.0 + 0.5 * squared / (1.0 + squared)) / (1.0 + plastic[x]) * factor
            stiff[x + 1] = stiffness
            for f, plane in enumerate([stiffness] + fields):
                turned[f, 0, x], turned[f, 1, x] = beside(plane)
            most = [jnp.maximum(most[f], jnp.abs(fields[f])) for f in range(4)]
        return tuple(most)

    most = lax.fori_loop(0, EDGE // 4, prepare, (zero_plane,) * 4)
    exponents = []
    exponent_row = jnp.zeros((1, 128), I32)
    scales = []
    for f in range(4):
        largest = jnp.max(jnp.max(most[f], axis=0, keepdims=True), axis=1, keepdims=True)
        exponent = jnp.ceil(jnp.log2(jnp.maximum(largest, 1e-30)) + 0.001)
        scales.append(jnp.exp2(-exponent))
        exponent_row = jnp.where(slot_lane == f, exponent.astype(I32), exponent_row)

    numbers = {offset: number for number, offset in enumerate(OFFSETS)}
    halves = (slice(0, 8), slice(8, 16))
    ones = (jnp.ones((8, 128), F32),) * 2

    def built(x, done, active, side):
        lanes = slice(128 * side, 128 * side + 128)
        begun = [ones] + [tuple(state[SWEEPS, f, x + 2, rows, lanes] for rows in halves) for f in range(4)]
        totals = {1: list(done), 0: list(active), -1: begun}
        own = {dx: [stiff[x + 1 - dx, rows, lanes] for rows in halves] for dx in (-1, 0, 1)}
        centres = [own[0]] + [[state[SWEEPS, f, x + 1, rows, lanes] for rows in halves] for f in range(4)]
        near, *fields = [
            shifted_pairs(
                (
                    [turned[f, 0, x, rows, lanes] for rows in halves],
                    centres[f],
                    [turned[f, 1, x, rows, lanes] for rows in halves],
                ),
                row8,
            )
            for f in range(5)
        ]
        for dz in (-1, 0, 1):
            for dy in (-1, 0, 1):
                n = plane_number(dy, dz)
                for dx in (-1, 0, 1):
                    if (dx, dy, dz) == (0, 0, 0):
                        continue
                    number = numbers[dx, dy, dz]
                    entries = []
                    for j, rows in enumerate(halves):
                        entry = weights[abs(dx), n, rows, 0:128] * (own[dx][j] + near[n][j])
                        entry = entry.astype(BF16).astype(F32)
                        tile[number, x + 1 - dx, rows, lanes] = entry
                        entries.append(entry)
                    total = totals[dx]
                    total[0] = tuple(total[0][j] + entries[j] for j in range(2))
                    for f in range(4):
                        total[f + 1] = tuple(total[f + 1][j] + entries[j] * fields[f][n][j] for j in range(2))
        return tuple(totals[1]), tuple(totals[0]), tuple(totals[-1])

    def finish(place, done, side):
        lanes = slice(128 * side, 128 * side + 128)
        scale = [1.0 / part for part in done[0]]
        for j, rows in enumerate(halves):
            inverse[place, rows, lanes] = scale[j]
        for f in range(4):
            for j, rows in enumerate(halves):
                stepped[f, place, rows, lanes] = done[f + 1][j] * scale[j]

    for side in range(2):

        def source(k, carry):
            for j in range(4 if side == 0 else 2):
                pass_plastic(4 * k + j if side == 0 else 16 + 2 * k + j)
            for j in range(4):
                done, *carry = built(4 * k + j, *carry, side)
                finish(4 * k + j, done, side)
            return tuple(carry)

        lanes = slice(128 * side, 128 * side + 128)
        start_at = (ones,) + tuple(tuple(state[SWEEPS, f, 1, rows, lanes] for rows in halves) for f in range(4))
        last, _ = lax.fori_loop(0, EDGE // 4, source, ((ones,) * 5, start_at))
        finish(EDGE, last, side)

    pass_plastic(28)
    pass_plastic(29)

    def spread(k, carry):
        pass_plastic(24 + k)
        for j in range(4):
            x = 4 * k + j
            for f in range(4):
                plane = stepped[f, x + 1]
                minus, plus = beside(plane)
                for side in range(2):
                    lanes = slice(128 * side, 128 * side + 128)
                    three = [[part[rows, lanes] for rows in halves] for part in (minus, plane, plus)]
                    for n, pair in enumerate(shifted_pairs(three, row8)):
                        for i, rows in enumerate(halves):
                            values[f, n, x + 1, rows, lanes] = pair[i]
        return carry

    lax.fori_loop(0, EDGE // 4, spread, 0)

    def smoothed(x):
        totals = [state[SWEEPS, f, x + 1] for f in range(4)]
        for number, (dx, dy, dz) in enumerate(OFFSETS):
            entry = tile[number, x + 1]
            for f in range(4):
                totals[f] = totals[f] + entry * values[f, plane_number(dy, dz), x + 1 + dx]
        scale = inverse[x + 1]
        return [total * scale for total in totals]

    def send_plane(m):
        pltpu.make_async_remote_copy(
            send_one.at[m, pl.ds(0, 33)], recv_one.at[s, pl.ds(0, 33)], one_send, one_recv,
            device_id=(m, b), device_id_type=MESH,
        ).start()

    def encode_plane(x, slot):
        codes = []
        for f, field in enumerate(smoothed(x)):
            part = jnp.abs(field) * scales[f]
            part = jnp.minimum(part * lax.rsqrt(part + 1e-37), 1.0) * 32767.0
            codes.append((jnp.where(field < 0.0, -part, part) + 32768.5).astype(I32))
        coded[slot, 0] = (codes[0] << 16) | codes[1]
        coded[slot, 1] = (codes[2] << 16) | codes[3]

    def turn_plane(x, slot):
        tiles = [
            coded[slot, w, 8 * half : 8 * half + 8, 128 * side : 128 * side + 128]
            for half in range(2)
            for w in range(2)
            for side in range(2)
        ]
        tiles = swap_rows_and_groups(tiles, group8, swap_a, swap_b)
        for half in range(2):
            m = 2 * x + half
            for k in range(4):
                send_one[m, 8 * k : 8 * k + 8, :] = tiles[4 * half + k]
            send_one[m, 32:33, :] = exponent_row

    def second(step, carry):
        x, later = lax.rem(step + chip, EDGE), lax.rem(step + 1 + chip, EDGE)
        slot = lax.rem(step, 2)
        turn_plane(x, slot)
        encode_plane(later, 1 - slot)
        send_plane(2 * x)
        send_plane(2 * x + 1)
        return carry

    encode_plane(chip, 0)
    turn_plane(chip, 0)
    send_plane(sibling)
    recv_one[s, 0:33, :] = send_one[s, 0:33, :]
    encode_plane(lax.rem(chip + 1, EDGE), 1)
    lax.fori_loop(1, EDGE - 1, second, 0)
    turn_plane(lax.rem(chip + EDGE - 1, EDGE), 1)
    send_plane(2 * lax.rem(chip + EDGE - 1, EDGE))
    send_plane(2 * lax.rem(chip + EDGE - 1, EDGE) + 1)
    wait_all(recv_one.at[pl.ds(0, N_SLAB - 1), pl.ds(0, 33)], one_recv)

    def unpack(g, carry):
        place = pl.ds(pl.multiple_of(64 * g, 64), 64)
        for w in range(2):
            words = recv_one[pl.ds(4 * g, 4), 16 * w : 16 * w + 16, :].reshape(64, 128)
            for number in range(4):
                at = 128 * (4 * w + number)
                table[place, at : at + 128] = byte_of(words, number)
        return carry

    lax.fori_loop(0, 8, unpack, 0)

    def onward_group(g):
        place = pl.ds(pl.multiple_of(256 * g, 256), 256)
        rows = jnp.dot(one_hot[place, :], table[...], preferred_element_type=F32)
        for w in range(2):
            parts = [rows[:, 128 * (4 * w + n) : 128 * (4 * w + n) + 128] for n in range(4)]
            words = joined(parts[0], parts[1]) | (joined(parts[2], parts[3]) << 16)
            send_two[pl.ds(16 * g, 16), 16 * w : 16 * w + 16, :] = words.reshape(16, P_DEV, 128)

    def pass_on(d):
        pltpu.make_async_remote_copy(
            send_two.at[d], out_words.at[s], two_send, two_recv,
            device_id=(d, b), device_id_type=MESH,
        ).start()

    onward_group(0)
    onward_group(1)
    pltpu.make_async_copy(send_two.at[s], out_words.at[s], own_sem).start()
    pass_on(sibling)
    for k in range(1, EDGE):
        d = 2 * lax.rem(chip + k, EDGE)
        pass_on(d)
        pass_on(d + 1)

    sources = jnp.concatenate(
        [jnp.broadcast_to(recv_one[k, 32:33, :].astype(F32), (P_DEV, 128)) for k in range(N_SLAB)], axis=0
    ).astype(BF16)
    mine = one_hot[pl.ds(pl.multiple_of(s * P_DEV, P_DEV), P_DEV), :]
    exponents_here[...] = jnp.dot(mine, sources, preferred_element_type=F32)
    exponents_out = pltpu.make_async_copy(exponents_here, out_exponents, exponents_sem)
    exponents_out.start()

    for kind in (0, 1, 2, 3, 4, 5):
        wait_send(x_copies(kind), has_down, has_up)
    for kind in range(8):
        wait_send(y_copies(kind), has_left, has_right)
    wait_all(plastic_one.at[pl.ds(0, N_SLAB - 1), pl.ds(0, 9)], pl_one_send)
    wait_all(send_one.at[pl.ds(0, N_SLAB - 1), pl.ds(0, 33)], one_send)
    wait_all(send_two.at[pl.ds(0, N_SLAB - 1)], two_send)
    wait_all(plastic_two.at[pl.ds(0, N_SLAB - 1)], pl_two_send)
    own_plastic.wait()
    wait_all(out_plastic.at[pl.ds(0, N_SLAB - 1)], pl_two_recv)
    pltpu.make_async_copy(send_two.at[s], out_words.at[s], own_sem).wait()
    exponents_out.wait()
    wait_all(out_words.at[pl.ds(0, N_SLAB - 1)], two_recv)


def move(thermal, deform, modulus, plastic, flag, holder, position):
    anywhere = pl.BlockSpec(memory_space=pl.ANY)
    smem = pl.BlockSpec(memory_space=pltpu.SMEM)
    plane = (EDGE, DEPTH)
    dma = pltpu.SemaphoreType.DMA
    return pl.pallas_call(
        move_kernel,
        name="sweep_solve_move",
        out_shape=(
            jax.ShapeDtypeStruct((N_SLAB, 32, 128), I32),
            jax.ShapeDtypeStruct((N_SLAB, 8, 128), I32),
            jax.ShapeDtypeStruct((P_DEV, 128), F32),
        ),
        in_specs=[anywhere] * 4 + [smem] * 3,
        out_specs=(anywhere,) * 3,
        scratch_shapes=[
            pltpu.VMEM((EDGE,) + plane, F32),
            pltpu.VMEM((SWEEPS + 1, 4, EDGE + 2) + plane, F32),
            pltpu.VMEM((SWEEPS, 2, 4) + plane, F32),
            pltpu.VMEM((SWEEPS, 2, 4) + plane, F32),
            pltpu.VMEM((EDGE + 2,) + plane, F32),
            pltpu.VMEM((2,) + plane, F32),
            pltpu.VMEM((2,) + plane, F32),
            pltpu.VMEM((EDGE + 1,) + plane, F32),
            pltpu.VMEM((EDGE,) + plane, F32),
            pltpu.VMEM((EDGE,) + plane, F32),
            pltpu.VMEM((EDGE,) + plane, F32),
            pltpu.VMEM((EDGE,) + plane, F32),
            pltpu.VMEM((EDGE,) + plane, F32),
            pltpu.VMEM((EDGE + 2,) + plane, F32),
            pltpu.VMEM((5, 2, EDGE) + plane, F32),
            pltpu.VMEM((4, EDGE + 1) + plane, F32),
            pltpu.VMEM((2, 2) + plane, I32),
            pltpu.VMEM((2, 9) + plane, F32),
            pltpu.VMEM((26, EDGE + 2) + plane, F32),
            pltpu.VMEM((EDGE + 1,) + plane, F32),
            pltpu.VMEM((4, 9, EDGE + 2) + plane, F32),
            pltpu.VMEM((N_SLAB, 40, 128), I32),
            pltpu.VMEM((N_SLAB, 40, 128), I32),
            pltpu.VMEM((N_SLAB, 32, 128), I32),
            pltpu.VMEM((N_SLAB, 16, 128), I32),
            pltpu.VMEM((N_SLAB, 16, 128), I32),
            pltpu.VMEM((N_SLAB, 8, 128), I32),
            pltpu.VMEM((ROWS, ROWS), BF16),
            pltpu.VMEM((ROWS, 1024), BF16),
            pltpu.VMEM((ROWS, 256), BF16),
            pltpu.VMEM((64, 128), I32),
            pltpu.VMEM((64, 128), I32),
            pltpu.VMEM((P_DEV, 128), F32),
            dma((4,)),
            dma((6, 2)),
            dma((6, 2)),
            dma((8, 2)),
            dma((8, 2)),
            dma(()),
            dma(()),
            dma(()),
            dma(()),
            dma(()),
            dma(()),
            dma(()),
            dma(()),
            dma(()),
            dma(()),
            dma(()),
        ],
        compiler_params=pltpu.CompilerParams(
            collective_id=0, has_side_effects=True, vmem_limit_bytes=56 * 1024 * 1024
        ),
    )(thermal, deform, modulus, plastic, flag, holder, position)


def decode_kernel(
    words_in, plastic_in, exponents_in, heat_out, moved_out, plastic_out, words, strain, exponents, heat, moved, straight, got, put
):
    pieces = N_SLAB // 4
    fetch = [
        pltpu.make_async_copy(words_in.at[pl.ds(pieces * k, pieces)], words.at[pl.ds(pieces * k, pieces)], got.at[k])
        for k in range(4)
    ]
    fetch.append(pltpu.make_async_copy(plastic_in, strain, got.at[5]))
    fetch.insert(0, pltpu.make_async_copy(exponents_in, exponents, got.at[4]))
    for copy in fetch:
        copy.start()
    fetch.pop(0).wait()
    scales = [
        jnp.broadcast_to(jnp.exp2(exponents[:, f : f + 1]) * (1.0 / (32767.0 * 32767.0)), (P_DEV, 128))
        for f in range(4)
    ]
    length = 128 * pieces
    writes = []
    for k in range(4):
        fetch[k].wait()
        for m in range(pieces * k, pieces * k + pieces):
            at = slice(128 * m, 128 * m + 128)
            for w in range(2):
                word = words[m, 16 * w : 16 * w + 16, :]
                for part in range(2):
                    code = lax.shift_right_logical(word, 16) if part == 0 else word & 65535
                    root = (code - 32768).astype(F32)
                    field = root * jnp.abs(root) * scales[2 * w + part]
                    if w == 0 and part == 0:
                        heat[:, at] = field
                    else:
                        moved[2 * w + part - 1, :, at] = field
        at = pl.ds(length * k, length)
        writes.append(pltpu.make_async_copy(heat.at[:, at], heat_out.at[0, 0, :, at], put.at[3 * k]))
        writes.append(pltpu.make_async_copy(moved.at[:, :, at], moved_out.at[0, 0, :, :, at], put.at[3 * k + 1]))
        for copy in writes[-2:]:
            copy.start()
        if k == 0:
            fetch[4].wait()
        for m in range(pieces * k, pieces * k + pieces):
            word = strain[m]
            for part in range(2):
                code = lax.shift_right_logical(word, 16) if part == 0 else word & 65535
                root = code.astype(F32) * (1.0 / PLASTIC_STEPS) + PLASTIC_LOW
                straight[8 * part : 8 * part + 8, 128 * m : 128 * m + 128] = root * root
        writes.append(pltpu.make_async_copy(straight.at[:, at], plastic_out.at[0, 0, :, at], put.at[3 * k + 2]))
        writes[-1].start()
    for copy in writes:
        copy.wait()


def decode(words, plastic, exponents):
    anywhere = pl.BlockSpec(memory_space=pl.ANY)
    length = EDGE**3
    heat, moved, strain = pl.pallas_call(
        decode_kernel,
        name="decode",
        out_shape=(
            jax.ShapeDtypeStruct((1, 1, P_DEV, length), F32),
            jax.ShapeDtypeStruct((1, 1, 3, P_DEV, length), F32),
            jax.ShapeDtypeStruct((1, 1, P_DEV, length), F32),
        ),
        in_specs=[anywhere] * 3,
        out_specs=(anywhere,) * 3,
        scratch_shapes=[
            pltpu.VMEM((N_SLAB, 32, 128), I32),
            pltpu.VMEM((N_SLAB, 8, 128), I32),
            pltpu.VMEM((P_DEV, 128), F32),
            pltpu.VMEM((P_DEV, length), F32),
            pltpu.VMEM((3, P_DEV, length), F32),
            pltpu.VMEM((P_DEV, length), F32),
            pltpu.SemaphoreType.DMA((6,)),
            pltpu.SemaphoreType.DMA((12,)),
        ],
        compiler_params=pltpu.CompilerParams(vmem_limit_bytes=56 * 1024 * 1024),
    )(words, plastic, exponents)
    return heat, moved.transpose(0, 1, 3, 2, 4), strain


def on_device(thermal, deform, modulus, plastic, flag, holder, position):
    return decode(*move(thermal, deform, modulus, plastic, flag, holder, position))


def solution(mesh):
    placed = (
        P("slab", "blk", None),
        P(None, "slab", "blk", None),
        P("slab", "blk", None),
        P("slab", "blk", None),
        P("slab", "blk", None),
        P("slab", "blk", None),
        P("slab", "blk", None),
    )
    return jax.shard_map(
        on_device,
        mesh=mesh,
        in_specs=placed,
        out_specs=(
            P("slab", "blk", None, None),
            P("slab", "blk", None, None, None),
            P("slab", "blk", None, None),
        ),
        check_vma=False,
    )
```

```python
import jax
import jax.numpy as jnp
from jax import lax
from jax.experimental import pallas as pl
from jax.experimental.pallas import tpu as pltpu
from jax.sharding import PartitionSpec as P

EDGE = 16
DEPTH = 256
SWEEPS = 4
N_SLAB = 32
N_BLK = 4
P_DEV = 16
ROWS = N_SLAB * P_DEV
MESH = pl.DeviceIdType.MESH
F32 = jnp.float32
I32 = jnp.int32
BF16 = jnp.bfloat16

PLASTIC_LOW = 0.2235
PLASTIC_STEPS = 65535.0 / (1.4145 - PLASTIC_LOW)

OFFSETS = [
    (dx, dy, dz)
    for dx in (-1, 0, 1)
    for dy in (-1, 0, 1)
    for dz in (-1, 0, 1)
    if (dx, dy, dz) != (0, 0, 0)
]
WEIGHTS = [0.0, 0.1, 0.04, 0.02]


def plane_number(dy, dz):
    return (dy + 1) * 3 + dz + 1


def lane_of(shape):
    return lax.broadcasted_iota(I32, shape, 1)


def row_of(shape):
    return lax.broadcasted_iota(I32, shape, 0)


def shifted_pairs(three, row8):
    out = [None] * 9
    for dz, (a, b) in zip((-1, 0, 1), three):
        a_down, b_down = pltpu.roll(a, 1, 0), pltpu.roll(b, 1, 0)
        a_up, b_up = pltpu.roll(a, 7, 0), pltpu.roll(b, 7, 0)
        out[plane_number(-1, dz)] = (a_down, jnp.where(row8 == 0, a_down, b_down))
        out[plane_number(0, dz)] = (a, b)
        out[plane_number(1, dz)] = (jnp.where(row8 == 7, b_up, a_up), b_up)
    return out


def swap_rows_and_groups(tiles, group, first, second):
    for k in range(8):
        first[8 * k : 8 * k + 8, :] = tiles[k]
    parts = [first[pl.ds(k, 8, stride=8), :] for k in range(8)]
    for bit in (4, 2, 1):
        low_group = (group & bit) == 0
        for k in range(8):
            if k & bit == 0:
                low, high = parts[k], parts[k | bit]
                parts[k] = jnp.where(low_group, low, pltpu.roll(high, 16 * bit, 1))
                parts[k | bit] = jnp.where(low_group, pltpu.roll(low, 128 - 16 * bit, 1), high)
    for k in range(8):
        second[8 * k : 8 * k + 8, :] = parts[k]
    return [second[pl.ds(k, 8, stride=8), :] for k in range(8)]


def byte_of(words, number):
    part = words if number == 0 else lax.shift_right_logical(words, 8 * number)
    return (part & 255).astype(F32).astype(BF16)


def joined(low, high):
    return (low + 256.0 * high).astype(I32)


def move_kernel(
    thermal, deform, modulus, plastic_in, flag, holder, position,
    out_words, out_plastic, out_exponents,
    plastic, state, halo_y, stage_y, cond, cond_y, cond_stage,
    face_x, face_ym, face_yp, face_zm, face_zp, centre,
    stiff, turned, stepped, coded, weights, tile, inverse, values,
    send_one, recv_one, send_two, plastic_one, plastic_got, plastic_two,
    one_hot, table, plastic_table, swap_a, swap_b, exponents_here,
    load_sem, x_send, x_recv, y_send, y_recv,
    one_send, one_recv, two_send, two_recv, pl_one_send, pl_one_recv, pl_two_send, pl_two_recv, own_sem, own_plastic_sem, exponents_sem,
):
    s = lax.axis_index("slab")
    b = lax.axis_index("blk")
    chip = s // 2
    up, down = lax.rem(s + 1, N_SLAB), lax.rem(s + N_SLAB - 1, N_SLAB)
    right, left = lax.rem(b + 1, N_BLK), lax.rem(b + N_BLK - 1, N_BLK)
    has_up, has_down = s < N_SLAB - 1, s > 0
    has_right, has_left = b < N_BLK - 1, b > 0

    loads = [
        pltpu.make_async_copy(thermal, state.at[0, 0, pl.ds(1, EDGE)], load_sem.at[0]),
        pltpu.make_async_copy(deform, state.at[0, pl.ds(1, 3), pl.ds(1, EDGE)], load_sem.at[1]),
        pltpu.make_async_copy(modulus, cond.at[pl.ds(1, EDGE)], load_sem.at[2]),
        pltpu.make_async_copy(plastic_in, plastic, load_sem.at[3]),
    ]
    for load in loads:
        load.start()

    barrier = pltpu.get_barrier_semaphore()

    for step in range(1, N_SLAB):
        peer = lax.rem(s + step, N_SLAB)
        pl.semaphore_signal(barrier, inc=1, device_id=(peer, b), device_id_type=MESH)

    @pl.when(has_right)
    def _():
        pl.semaphore_signal(barrier, inc=1, device_id=(s, right), device_id_type=MESH)

    @pl.when(has_left)
    def _():
        pl.semaphore_signal(barrier, inc=1, device_id=(s, left), device_id_type=MESH)

    zero_plane = jnp.zeros((EDGE, DEPTH), F32)

    for has, place, side in ((has_down, 0, 0), (has_up, EDGE + 1, 1)):

        @pl.when(jnp.logical_not(has))
        def _():
            cond[place] = zero_plane
            for t in range(SWEEPS):
                for f in range(4):
                    state[t, f, place] = zero_plane

    for has, side in ((has_left, 0), (has_right, 1)):

        @pl.when(jnp.logical_not(has))
        def _():
            cond_y[side] = zero_plane
            for t in range(SWEEPS):
                for f in range(4):
                    halo_y[t, side, f] = zero_plane

    row8 = row_of((8, 128))
    group8 = lane_of((8, 128)) // EDGE
    row = row_of((EDGE, DEPTH))
    lane = lane_of((EDGE, DEPTH))
    inner = lane & (EDGE - 1)

    for load in loads:
        load.wait()

    def stage_first(x, carry):
        for side, y in ((0, 0), (1, EDGE - 1)):
            cond_stage[side, pl.ds(x, 1), :] = cond[x + 1, y : y + 1, :]
            for f in range(4):
                stage_y[0, side, f, pl.ds(x, 1), :] = state[0, f, x + 1, y : y + 1, :]
        return carry

    lax.fori_loop(0, EDGE, stage_first, 0)
    neighbours = 31 + has_right.astype(I32) + has_left.astype(I32)
    pl.semaphore_wait(barrier, neighbours)

    def x_copies(kind):
        out = []
        for direction, peer in ((0, down), (1, up)):
            mine = 0 if direction == 0 else EDGE - 1
            there = EDGE + 1 if direction == 0 else 0
            if kind == 0:
                source, target = thermal.at[mine], state.at[0, 0, there]
            elif kind == 4:
                source, target = deform.at[:, mine], state.at[0, pl.ds(1, 3), there]
            elif kind == 5:
                source, target = modulus.at[mine], cond.at[there]
            else:
                source, target = state.at[kind, :, mine + 1], state.at[kind, :, there]
            out.append(
                pltpu.make_async_remote_copy(
                    source, target, x_send.at[kind, direction], x_recv.at[kind, direction],
                    device_id=(peer, b), device_id_type=MESH,
                )
            )
        return out

    def y_copies(kind):
        out = []
        for direction, peer in ((0, left), (1, right)):
            if kind == 4:
                source, target = cond_stage.at[direction], cond_y.at[1 - direction]
            elif kind == 0:
                source, target = stage_y.at[0, direction], halo_y.at[0, 1 - direction]
            else:
                part = pl.ds(8 * (kind // 4), 8)
                source = stage_y.at[kind % 4, direction, :, part]
                target = halo_y.at[kind % 4, 1 - direction, :, part]
            out.append(
                pltpu.make_async_remote_copy(
                    source, target, y_send.at[kind, direction], y_recv.at[kind, direction],
                    device_id=(s, peer), device_id_type=MESH,
                )
            )
        return out

    def start(copies, to_low, to_high):
        @pl.when(to_low)
        def _():
            copies[0].start()

        @pl.when(to_high)
        def _():
            copies[1].start()

    def wait_recv(copies, from_high, from_low):
        @pl.when(from_high)
        def _():
            copies[0].wait_recv()

        @pl.when(from_low)
        def _():
            copies[1].wait_recv()

    def four_at_a_time(work):
        def step(k, carry):
            for j in range(4):
                work(4 * k + j)
            return carry

        lax.fori_loop(0, EDGE // 4, step, 0)

    def wait_send(copies, to_low, to_high):
        @pl.when(to_low)
        def _():
            copies[0].wait_send()

        @pl.when(to_high)
        def _():
            copies[1].wait_send()

    for kind in (5, 0, 4):
        start(x_copies(kind), has_down, has_up)
    start(y_copies(4), has_left, has_right)
    start(y_copies(0), has_left, has_right)

    slot_lane = lane_of((1, 128))
    slot_row = jnp.zeros((1, 128), I32)
    for p in range(P_DEV):
        code = holder[0, 0, p] * P_DEV + position[0, 0, p]
        slot_row = jnp.where(slot_lane == lax.rem(s, 8) * P_DEV + p, code, slot_row)

    def plastic_planes(planes):
        tiles = []
        for x in planes:
            root = plastic[x]
            root = root * lax.rsqrt(root)
            codes = jnp.clip((root - PLASTIC_LOW) * PLASTIC_STEPS + 0.5, 0.0, 65535.0).astype(I32)
            words = (codes[:, 0:128] << 16) | codes[:, 128:256]
            tiles += [words[0:8], words[8:16]]
        tiles = swap_rows_and_groups(tiles, group8, swap_a, swap_b)
        for k in range(8):
            m = 2 * planes[k // 2] + k % 2
            plastic_one[m, 0:8, :] = tiles[k]
            plastic_one[m, 8:9, :] = slot_row

    def plastic_turn(k, carry):
        plastic_planes([4 * k + j for j in range(4)])
        return carry

    lax.fori_loop(0, 4, plastic_turn, 0)
    plastic_got[s, 0:9, :] = plastic_one[s, 0:9, :]

    sibling = lax.bitwise_xor(s, 1)

    def send_plastic(m):
        pltpu.make_async_remote_copy(
            plastic_one.at[m, pl.ds(0, 9)], plastic_got.at[s, pl.ds(0, 9)], pl_one_send, pl_one_recv,
            device_id=(m, b), device_id_type=MESH,
        ).start()

    def plastic_out(step):
        planes = [lax.rem(chip + 4 * step + j, EDGE) for j in range(4)]
        if step == 0:
            send_plastic(sibling)
        for x in planes[step == 0 :]:
            send_plastic(2 * x)
            send_plastic(2 * x + 1)

    plastic_out(0)
    plastic_out(1)

    for dy in (-1, 0, 1):
        for dz in (-1, 0, 1):
            inside = (row + dy >= 0) & (row + dy < EDGE) & (inner + dz >= 0) & (inner + dz < EDGE)
            reach = abs(dy) + abs(dz)
            weights[0, plane_number(dy, dz)] = jnp.where(inside, 0.5 * WEIGHTS[reach], 0.0)
            weights[1, plane_number(dy, dz)] = jnp.where(inside, 0.5 * WEIGHTS[reach + 1], 0.0)
    for n in range(9):
        for f in range(4):
            values[f, n, 0] = zero_plane
            values[f, n, EDGE + 1] = zero_plane
    for number, (dx, dy, dz) in enumerate(OFFSETS):
        if dx != 0:
            tile[number, 1 if dx < 0 else EDGE] = zero_plane

    factor = jnp.ones((1, DEPTH), F32)
    lane_row = lane_of((1, DEPTH)) // EDGE
    for p in range(P_DEV):
        factor = jnp.where(lane_row == p, 1.0 + 3.0 * flag[0, 0, p].astype(F32), factor)

    wait_recv(x_copies(5), has_up, has_down)
    wait_recv(y_copies(4), has_right, has_left)

    def face(x):
        here = cond[x + 1]
        ym = jnp.where(row == 0, cond_y[0, pl.ds(x, 1), :], pltpu.roll(here, 1, 0))
        yp = jnp.where(row == EDGE - 1, cond_y[1, pl.ds(x, 1), :], pltpu.roll(here, EDGE - 1, 0))
        zm = jnp.where(lane == 0, 0.0, pltpu.roll(here, 1, 1))
        zp = jnp.where(lane == DEPTH - 1, 0.0, pltpu.roll(here, DEPTH - 1, 1))
        low = 0.06 * (cond[x] + here)
        high = 0.06 * (here + cond[x + 2])
        face_x[x] = low
        face_x[x + 1] = high
        ym, yp, zm, zp = (0.06 * (here + beside) for beside in (ym, yp, zm, zp))
        face_ym[x] = ym
        face_yp[x] = yp
        face_zm[x] = zm
        face_zp[x] = zp
        centre[x] = 1.0 - (low + high + ym + yp + zm + zp)

    four_at_a_time(face)

    def sweep_plane(t, x):
        around = []
        for f in range(4):
            here = state[t, f, x + 1]
            around.append(
                (
                    here,
                    state[t, f, x],
                    state[t, f, x + 2],
                    jnp.where(row == 0, halo_y[t, 0, f, pl.ds(x, 1), :], pltpu.roll(here, 1, 0)),
                    jnp.where(row == EDGE - 1, halo_y[t, 1, f, pl.ds(x, 1), :], pltpu.roll(here, EDGE - 1, 0)),
                    jnp.where(lane == 0, 0.0, pltpu.roll(here, 1, 1)),
                    jnp.where(lane == DEPTH - 1, 0.0, pltpu.roll(here, DEPTH - 1, 1)),
                )
            )
        h, xm, xp, ym, yp, zm, zp = around[0]
        fresh = [
            centre[x] * h
            + face_x[x] * xm
            + face_x[x + 1] * xp
            + face_ym[x] * ym
            + face_yp[x] * yp
            + face_zm[x] * zm
            + face_zp[x] * zp
        ]
        slopes = (xp - xm, yp - ym, zp - zm)
        for c in range(3):
            u, *six = around[c + 1]
            total = (six[0] + six[1]) + (six[2] + six[3]) + (six[4] + six[5])
            fresh.append(0.28 * u + 0.12 * total - 0.06 * slopes[c])
        for f in range(4):
            state[t + 1, f, x + 1] = fresh[f]
            if t + 1 < SWEEPS:
                stage_y[t + 1, 0, f, pl.ds(x, 1), :] = fresh[f][0:1]
                stage_y[t + 1, 1, f, pl.ds(x, 1), :] = fresh[f][EDGE - 1 : EDGE]

    def sweep(t):
        def four(first):
            for x in range(first, first + 4):
                sweep_plane(t, x)

        onward_x = x_copies(t + 1) if t + 1 < SWEEPS else None
        if t > 0:
            arrived = x_copies(t)

            @pl.when(has_down)
            def _():
                arrived[1].wait_recv()

            wait_recv(y_copies(t), has_right, has_left)
        four(0)
        if onward_x:

            @pl.when(has_down)
            def _():
                onward_x[0].start()

        four(4)
        if onward_x:
            start(y_copies(t + 1), has_left, has_right)
        if t > 0:

            @pl.when(has_up)
            def _():
                arrived[0].wait_recv()

            wait_recv(y_copies(t + 4), has_right, has_left)
        four(12)
        if onward_x:

            @pl.when(has_up)
            def _():
                onward_x[1].start()

        four(8)
        if onward_x:
            start(y_copies(t + 5), has_left, has_right)

    wait_recv(x_copies(0), has_up, has_down)
    wait_recv(x_copies(4), has_up, has_down)
    wait_recv(y_copies(0), has_right, has_left)
    sweep(0)

    def wait_all(ref, semaphore):
        pltpu.make_async_copy(ref, ref, semaphore).wait()

    plastic_out(2)
    sweep(1)
    plastic_out(3)
    sweep(2)

    wait_all(plastic_got.at[pl.ds(0, N_SLAB - 1), pl.ds(0, 9)], pl_one_recv)
    slot_id = row_of((ROWS, 128))
    for g in range(4):
        codes = plastic_got[8 * g, 8:9, :]
        for k in range(1, 8):
            codes = codes + plastic_got[8 * g + k, 8:9, :]
        one_hot[:, 128 * g : 128 * g + 128] = jnp.where(slot_id == codes, 1.0, 0.0).astype(BF16)

    def plastic_unpack(g, carry):
        words = plastic_got[pl.ds(4 * g, 4), 0:8, :]
        both = jnp.concatenate([lax.shift_right_logical(words, 16), words & 65535], axis=1).reshape(64, 128)
        place = pl.ds(pl.multiple_of(64 * g, 64), 64)
        plastic_table[place, 0:128] = byte_of(both, 0)
        plastic_table[place, 128:256] = byte_of(both, 1)
        return carry

    lax.fori_loop(0, 8, plastic_unpack, 0)

    def plastic_group(g, carry):
        place = pl.ds(pl.multiple_of(128 * g, 128), 128)
        rows = jnp.dot(one_hot[place, :], plastic_table[...], preferred_element_type=F32)
        codes = joined(rows[:, 0:128], rows[:, 128:256]).reshape(8, P_DEV, 128)
        plastic_two[pl.ds(8 * g, 8)] = (codes[:, 0:8] << 16) | codes[:, 8:16]
        return carry

    lax.fori_loop(0, 4, plastic_group, 0)

    def pass_plastic(number):
        d = 2 * lax.rem(chip + 1 + number // 2, EDGE) + lax.rem(number, 2)
        start_plastic(d)

    def start_plastic(d):
        pltpu.make_async_remote_copy(
            plastic_two.at[d], out_plastic.at[s], pl_two_send, pl_two_recv,
            device_id=(d, b), device_id_type=MESH,
        ).start()

    own_plastic = pltpu.make_async_copy(plastic_two.at[s], out_plastic.at[s], own_plastic_sem)
    own_plastic.start()
    start_plastic(sibling)
    sweep(3)

    def beside(plane):
        parts = [plane[:, 0:128], plane[:, 128:256]]
        return [jnp.concatenate([pltpu.roll(part, turn, 1) for part in parts], axis=1) for turn in (1, 127)]

    def prepare(k, most):
        most = list(most)
        for j in range(4):
            x = 4 * k + j
            fields = [state[SWEEPS, f, x + 1] for f in range(4)]
            squared = fields[0] * fields[0]
            stiffness = cond[x + 1] * (1.0 + 0.5 * squared / (1.0 + squared)) / (1.0 + plastic[x]) * factor
            stiff[x + 1] = stiffness
            for f, plane in enumerate([stiffness] + fields):
                turned[f, 0, x], turned[f, 1, x] = beside(plane)
            most = [jnp.maximum(most[f], jnp.abs(fields[f])) for f in range(4)]
        return tuple(most)

    most = lax.fori_loop(0, EDGE // 4, prepare, (zero_plane,) * 4)
    exponents = []
    exponent_row = jnp.zeros((1, 128), I32)
    scales = []
    for f in range(4):
        largest = jnp.max(jnp.max(most[f], axis=0, keepdims=True), axis=1, keepdims=True)
        exponent = jnp.ceil(jnp.log2(jnp.maximum(largest, 1e-30)) + 0.001)
        scales.append(jnp.exp2(-exponent))
        exponent_row = jnp.where(slot_lane == f, exponent.astype(I32), exponent_row)

    numbers = {offset: number for number, offset in enumerate(OFFSETS)}
    halves = (slice(0, 8), slice(8, 16))
    ones = (jnp.ones((8, 128), F32),) * 2

    def built(x, done, active, side):
        lanes = slice(128 * side, 128 * side + 128)
        begun = [ones] + [tuple(state[SWEEPS, f, x + 2, rows, lanes] for rows in halves) for f in range(4)]
        totals = {1: list(done), 0: list(active), -1: begun}
        own = {dx: [stiff[x + 1 - dx, rows, lanes] for rows in halves] for dx in (-1, 0, 1)}
        centres = [own[0]] + [[state[SWEEPS, f, x + 1, rows, lanes] for rows in halves] for f in range(4)]
        near, *fields = [
            shifted_pairs(
                (
                    [turned[f, 0, x, rows, lanes] for rows in halves],
                    centres[f],
                    [turned[f, 1, x, rows, lanes] for rows in halves],
                ),
                row8,
            )
            for f in range(5)
        ]
        for dz in (-1, 0, 1):
            for dy in (-1, 0, 1):
                n = plane_number(dy, dz)
                for dx in (-1, 0, 1):
                    if (dx, dy, dz) == (0, 0, 0):
                        continue
                    number = numbers[dx, dy, dz]
                    entries = []
                    for j, rows in enumerate(halves):
                        entry = weights[abs(dx), n, rows, 0:128] * (own[dx][j] + near[n][j])
                        entry = entry.astype(BF16).astype(F32)
                        tile[number, x + 1 - dx, rows, lanes] = entry
                        entries.append(entry)
                    total = totals[dx]
                    total[0] = tuple(total[0][j] + entries[j] for j in range(2))
                    for f in range(4):
                        total[f + 1] = tuple(total[f + 1][j] + entries[j] * fields[f][n][j] for j in range(2))
        return tuple(totals[1]), tuple(totals[0]), tuple(totals[-1])

    def finish(place, done, side):
        lanes = slice(128 * side, 128 * side + 128)
        scale = [1.0 / part for part in done[0]]
        for j, rows in enumerate(halves):
            inverse[place, rows, lanes] = scale[j]
        for f in range(4):
            for j, rows in enumerate(halves):
                stepped[f, place, rows, lanes] = done[f + 1][j] * scale[j]

    for side in range(2):

        def source(k, carry):
            for j in range(4 if side == 0 else 2):
                pass_plastic(4 * k + j if side == 0 else 16 + 2 * k + j)
            for j in range(4):
                done, *carry = built(4 * k + j, *carry, side)
                finish(4 * k + j, done, side)
            return tuple(carry)

        lanes = slice(128 * side, 128 * side + 128)
        start_at = (ones,) + tuple(tuple(state[SWEEPS, f, 1, rows, lanes] for rows in halves) for f in range(4))
        last, _ = lax.fori_loop(0, EDGE // 4, source, ((ones,) * 5, start_at))
        finish(EDGE, last, side)

    pass_plastic(28)
    pass_plastic(29)

    def spread(k, carry):
        pass_plastic(24 + k)
        for j in range(4):
            x = 4 * k + j
            for f in range(4):
                plane = stepped[f, x + 1]
                minus, plus = beside(plane)
                for side in range(2):
                    lanes = slice(128 * side, 128 * side + 128)
                    three = [[part[rows, lanes] for rows in halves] for part in (minus, plane, plus)]
                    for n, pair in enumerate(shifted_pairs(three, row8)):
                        for i, rows in enumerate(halves):
                            values[f, n, x + 1, rows, lanes] = pair[i]
        return carry

    lax.fori_loop(0, EDGE // 4, spread, 0)

    def smoothed(x):
        totals = [state[SWEEPS, f, x + 1] for f in range(4)]
        for number, (dx, dy, dz) in enumerate(OFFSETS):
            entry = tile[number, x + 1]
            for f in range(4):
                totals[f] = totals[f] + entry * values[f, plane_number(dy, dz), x + 1 + dx]
        scale = inverse[x + 1]
        return [total * scale for total in totals]

    def send_plane(m):
        pltpu.make_async_remote_copy(
            send_one.at[m, pl.ds(0, 33)], recv_one.at[s, pl.ds(0, 33)], one_send, one_recv,
            device_id=(m, b), device_id_type=MESH,
        ).start()

    def encode_plane(x, slot):
        codes = []
        for f, field in enumerate(smoothed(x)):
            part = jnp.abs(field) * scales[f]
            part = jnp.minimum(part * lax.rsqrt(part + 1e-37), 1.0) * 32767.0
            codes.append((jnp.where(field < 0.0, -part, part) + 32768.5).astype(I32))
        coded[slot, 0] = (codes[0] << 16) | codes[1]
        coded[slot, 1] = (codes[2] << 16) | codes[3]

    def turn_plane(x, slot):
        tiles = [
            coded[slot, w, 8 * half : 8 * half + 8, 128 * side : 128 * side + 128]
            for half in range(2)
            for w in range(2)
            for side in range(2)
        ]
        tiles = swap_rows_and_groups(tiles, group8, swap_a, swap_b)
        for half in range(2):
            m = 2 * x + half
            for k in range(4):
                send_one[m, 8 * k : 8 * k + 8, :] = tiles[4 * half + k]
            send_one[m, 32:33, :] = exponent_row

    def second(step, carry):
        x, later = lax.rem(step + chip, EDGE), lax.rem(step + 1 + chip, EDGE)
        slot = lax.rem(step, 2)
        turn_plane(x, slot)
        encode_plane(later, 1 - slot)
        send_plane(2 * x)
        send_plane(2 * x + 1)
        return carry

    encode_plane(chip, 0)
    turn_plane(chip, 0)
    send_plane(sibling)
    recv_one[s, 0:33, :] = send_one[s, 0:33, :]
    encode_plane(lax.rem(chip + 1, EDGE), 1)
    lax.fori_loop(1, EDGE - 1, second, 0)
    turn_plane(lax.rem(chip + EDGE - 1, EDGE), 1)
    send_plane(2 * lax.rem(chip + EDGE - 1, EDGE))
    send_plane(2 * lax.rem(chip + EDGE - 1, EDGE) + 1)
    wait_all(recv_one.at[pl.ds(0, N_SLAB - 1), pl.ds(0, 33)], one_recv)

    def unpack(g, carry):
        place = pl.ds(pl.multiple_of(64 * g, 64), 64)
        for w in range(2):
            words = recv_one[pl.ds(4 * g, 4), 16 * w : 16 * w + 16, :].reshape(64, 128)
            for number in range(4):
                at = 128 * (4 * w + number)
                table[place, at : at + 128] = byte_of(words, number)
        return carry

    lax.fori_loop(0, 8, unpack, 0)

    def onward_word(w):
        rows = jnp.dot(one_hot[...], table[:, 512 * w : 512 * w + 512], preferred_element_type=F32)
        parts = [rows[:, 128 * n : 128 * n + 128] for n in range(4)]
        words = joined(parts[0], parts[1]) | (joined(parts[2], parts[3]) << 16)
        send_two[:, 16 * w : 16 * w + 16, :] = words.reshape(N_SLAB, P_DEV, 128)

    def pass_on(d):
        pltpu.make_async_remote_copy(
            send_two.at[d], out_words.at[s], two_send, two_recv,
            device_id=(d, b), device_id_type=MESH,
        ).start()

    onward_word(0)
    onward_word(1)
    pltpu.make_async_copy(send_two.at[s], out_words.at[s], own_sem).start()
    pass_on(sibling)
    for k in range(1, EDGE):
        d = 2 * lax.rem(chip + k, EDGE)
        pass_on(d)
        pass_on(d + 1)

    sources = jnp.concatenate(
        [jnp.broadcast_to(recv_one[k, 32:33, :].astype(F32), (P_DEV, 128)) for k in range(N_SLAB)], axis=0
    ).astype(BF16)
    mine = one_hot[pl.ds(pl.multiple_of(s * P_DEV, P_DEV), P_DEV), :]
    exponents_here[...] = jnp.dot(mine, sources, preferred_element_type=F32)
    exponents_out = pltpu.make_async_copy(exponents_here, out_exponents, exponents_sem)
    exponents_out.start()

    for kind in (0, 1, 2, 3, 4, 5):
        wait_send(x_copies(kind), has_down, has_up)
    for kind in range(8):
        wait_send(y_copies(kind), has_left, has_right)
    wait_all(plastic_one.at[pl.ds(0, N_SLAB - 1), pl.ds(0, 9)], pl_one_send)
    wait_all(send_one.at[pl.ds(0, N_SLAB - 1), pl.ds(0, 33)], one_send)
    wait_all(send_two.at[pl.ds(0, N_SLAB - 1)], two_send)
    wait_all(plastic_two.at[pl.ds(0, N_SLAB - 1)], pl_two_send)
    own_plastic.wait()
    wait_all(out_plastic.at[pl.ds(0, N_SLAB - 1)], pl_two_recv)
    pltpu.make_async_copy(send_two.at[s], out_words.at[s], own_sem).wait()
    exponents_out.wait()
    wait_all(out_words.at[pl.ds(0, N_SLAB - 1)], two_recv)


def move(thermal, deform, modulus, plastic, flag, holder, position):
    anywhere = pl.BlockSpec(memory_space=pl.ANY)
    smem = pl.BlockSpec(memory_space=pltpu.SMEM)
    plane = (EDGE, DEPTH)
    dma = pltpu.SemaphoreType.DMA
    return pl.pallas_call(
        move_kernel,
        name="sweep_solve_move",
        out_shape=(
            jax.ShapeDtypeStruct((N_SLAB, 32, 128), I32),
            jax.ShapeDtypeStruct((N_SLAB, 8, 128), I32),
            jax.ShapeDtypeStruct((P_DEV, 128), F32),
        ),
        in_specs=[anywhere] * 4 + [smem] * 3,
        out_specs=(anywhere,) * 3,
        scratch_shapes=[
            pltpu.VMEM((EDGE,) + plane, F32),
            pltpu.VMEM((SWEEPS + 1, 4, EDGE + 2) + plane, F32),
            pltpu.VMEM((SWEEPS, 2, 4) + plane, F32),
            pltpu.VMEM((SWEEPS, 2, 4) + plane, F32),
            pltpu.VMEM((EDGE + 2,) + plane, F32),
            pltpu.VMEM((2,) + plane, F32),
            pltpu.VMEM((2,) + plane, F32),
            pltpu.VMEM((EDGE + 1,) + plane, F32),
            pltpu.VMEM((EDGE,) + plane, F32),
            pltpu.VMEM((EDGE,) + plane, F32),
            pltpu.VMEM((EDGE,) + plane, F32),
            pltpu.VMEM((EDGE,) + plane, F32),
            pltpu.VMEM((EDGE,) + plane, F32),
            pltpu.VMEM((EDGE + 2,) + plane, F32),
            pltpu.VMEM((5, 2, EDGE) + plane, F32),
            pltpu.VMEM((4, EDGE + 1) + plane, F32),
            pltpu.VMEM((2, 2) + plane, I32),
            pltpu.VMEM((2, 9) + plane, F32),
            pltpu.VMEM((26, EDGE + 2) + plane, F32),
            pltpu.VMEM((EDGE + 1,) + plane, F32),
            pltpu.VMEM((4, 9, EDGE + 2) + plane, F32),
            pltpu.VMEM((N_SLAB, 40, 128), I32),
            pltpu.VMEM((N_SLAB, 40, 128), I32),
            pltpu.VMEM((N_SLAB, 32, 128), I32),
            pltpu.VMEM((N_SLAB, 16, 128), I32),
            pltpu.VMEM((N_SLAB, 16, 128), I32),
            pltpu.VMEM((N_SLAB, 8, 128), I32),
            pltpu.VMEM((ROWS, ROWS), BF16),
            pltpu.VMEM((ROWS, 1024), BF16),
            pltpu.VMEM((ROWS, 256), BF16),
            pltpu.VMEM((64, 128), I32),
            pltpu.VMEM((64, 128), I32),
            pltpu.VMEM((P_DEV, 128), F32),
            dma((4,)),
            dma((6, 2)),
            dma((6, 2)),
            dma((8, 2)),
            dma((8, 2)),
            dma(()),
            dma(()),
            dma(()),
            dma(()),
            dma(()),
            dma(()),
            dma(()),
            dma(()),
            dma(()),
            dma(()),
            dma(()),
        ],
        compiler_params=pltpu.CompilerParams(
            collective_id=0, has_side_effects=True, vmem_limit_bytes=56 * 1024 * 1024
        ),
    )(thermal, deform, modulus, plastic, flag, holder, position)


def decode_kernel(
    words_in, plastic_in, exponents_in, heat_out, moved_out, plastic_out, words, strain, exponents, heat, moved, straight, got, put
):
    pieces = N_SLAB // 4
    fetch = [
        pltpu.make_async_copy(words_in.at[pl.ds(pieces * k, pieces)], words.at[pl.ds(pieces * k, pieces)], got.at[k])
        for k in range(4)
    ]
    fetch.append(pltpu.make_async_copy(plastic_in, strain, got.at[5]))
    fetch.insert(0, pltpu.make_async_copy(exponents_in, exponents, got.at[4]))
    for copy in fetch:
        copy.start()
    fetch.pop(0).wait()
    scales = [
        jnp.broadcast_to(jnp.exp2(exponents[:, f : f + 1]) * (1.0 / (32767.0 * 32767.0)), (P_DEV, 128))
        for f in range(4)
    ]
    length = 128 * pieces
    writes = []
    for k in range(4):
        fetch[k].wait()
        for m in range(pieces * k, pieces * k + pieces):
            at = slice(128 * m, 128 * m + 128)
            for w in range(2):
                word = words[m, 16 * w : 16 * w + 16, :]
                for part in range(2):
                    code = lax.shift_right_logical(word, 16) if part == 0 else word & 65535
                    root = (code - 32768).astype(F32)
                    field = root * jnp.abs(root) * scales[2 * w + part]
                    if w == 0 and part == 0:
                        heat[:, at] = field
                    else:
                        moved[2 * w + part - 1, :, at] = field
        at = pl.ds(length * k, length)
        writes.append(pltpu.make_async_copy(heat.at[:, at], heat_out.at[0, 0, :, at], put.at[3 * k]))
        writes.append(pltpu.make_async_copy(moved.at[:, :, at], moved_out.at[0, 0, :, :, at], put.at[3 * k + 1]))
        for copy in writes[-2:]:
            copy.start()
        if k == 0:
            fetch[4].wait()
        for m in range(pieces * k, pieces * k + pieces):
            word = strain[m]
            for part in range(2):
                code = lax.shift_right_logical(word, 16) if part == 0 else word & 65535
                root = code.astype(F32) * (1.0 / PLASTIC_STEPS) + PLASTIC_LOW
                straight[8 * part : 8 * part + 8, 128 * m : 128 * m + 128] = root * root
        writes.append(pltpu.make_async_copy(straight.at[:, at], plastic_out.at[0, 0, :, at], put.at[3 * k + 2]))
        writes[-1].start()
    for copy in writes:
        copy.wait()


def decode(words, plastic, exponents):
    anywhere = pl.BlockSpec(memory_space=pl.ANY)
    length = EDGE**3
    heat, moved, strain = pl.pallas_call(
        decode_kernel,
        name="decode",
        out_shape=(
            jax.ShapeDtypeStruct((1, 1, P_DEV, length), F32),
            jax.ShapeDtypeStruct((1, 1, 3, P_DEV, length), F32),
            jax.ShapeDtypeStruct((1, 1, P_DEV, length), F32),
        ),
        in_specs=[anywhere] * 3,
        out_specs=(anywhere,) * 3,
        scratch_shapes=[
            pltpu.VMEM((N_SLAB, 32, 128), I32),
            pltpu.VMEM((N_SLAB, 8, 128), I32),
            pltpu.VMEM((P_DEV, 128), F32),
            pltpu.VMEM((P_DEV, length), F32),
            pltpu.VMEM((3, P_DEV, length), F32),
            pltpu.VMEM((P_DEV, length), F32),
            pltpu.SemaphoreType.DMA((6,)),
            pltpu.SemaphoreType.DMA((12,)),
        ],
        compiler_params=pltpu.CompilerParams(vmem_limit_bytes=56 * 1024 * 1024),
    )(words, plastic, exponents)
    return heat, moved.transpose(0, 1, 3, 2, 4), strain


def on_device(thermal, deform, modulus, plastic, flag, holder, position):
    return decode(*move(thermal, deform, modulus, plastic, flag, holder, position))


def solution(mesh):
    placed = (
        P("slab", "blk", None),
        P(None, "slab", "blk", None),
        P("slab", "blk", None),
        P("slab", "blk", None),
        P("slab", "blk", None),
        P("slab", "blk", None),
        P("slab", "blk", None),
    )
    return jax.shard_map(
        on_device,
        mesh=mesh,
        in_specs=placed,
        out_specs=(
            P("slab", "blk", None, None),
            P("slab", "blk", None, None, None),
            P("slab", "blk", None, None),
        ),
        check_vma=False,
    )
```
